256 devices in a mesh: tile: 64 (over y, z, core), sub: 4 (over x).
Axes of the slice: x: 4, y: 4, z: 8, core: 2. Of those that a mesh axis runs over, the one named last changes fastest.
Arguments:
- condition: bfloat16 [12, 16384, 1024], P(None, 'tile', 'sub'), may hold values from -6 to 6
- state: float32 [4, 16384, 1024], P(None, 'tile', 'sub'), may hold values from -12 to 12
- corner_rows: int32 [64, 4, 2], P('tile', 'sub'), may hold values from 0 to 256
- corner_cols: int32 [64, 4, 2], P('tile', 'sub'), may hold values from 0 to 256
- live_counts: int32 [64, 4], P('tile', 'sub'), may hold values from 1 to 2, as said below
- blend_weight: float32 [64, 4, 2, 128, 128], P('tile', 'sub'), may hold values from 0.2 to 5
- conv_in: bfloat16 [3, 3, 64, 16], replicated, may hold values from -0.5 to 0.5
- conv_mid: bfloat16 [3, 3, 64, 64], replicated, may hold values from -0.25 to 0.25
- proj_out: bfloat16 [4, 64], replicated, may hold values from -0.75 to 0.75
Outputs:
- denoised: float32 [4, 16384, 1024], P(None, 'tile', 'sub')
- next_state: float32 [4, 16384, 1024], P(None, 'tile', 'sub')
The draws below stay inside these ranges and needn't reach their ends.
Inputs may be any that keep to these rules, and one draw needn't show every extreme that they name: `live_counts`: each device has at least one and at most 2 live patches; some device has exactly 2.
All inputs are finite; a program needn't handle non-finite values.
Results may differ from the reference program's by a relative error of at most 0.00085.
Values may be sent and summed in bfloat16 or wider, within the bound.
No kernel may reach another device: no remote copies, remote signals or barrier semaphores. Data moves between devices by JAX's collectives and lax.ppermute only.
A program may use at most 128 MiB of HBM per device.

```python
import math
import jax
import jax.numpy as jnp
from jax import lax

CIN = 12
COUT = 4
HID = 64
PATCH = 128
BY = 256
BX = 256
PATCH_DEV = 2
NY = 16384
NX = 1024
N_TILE = 64
N_SUB = 4


def draw_live_counts(key, part):
    first = jax.random.fold_in(key, 11)
    second = jax.random.fold_in(key, 12)
    values = jax.random.randint(first, (N_TILE * N_SUB,), 1, PATCH_DEV + 1).astype(jnp.int32)
    place = jax.random.randint(second, (), 0, N_TILE * N_SUB)
    values = values.at[place].set(PATCH_DEV)
    return values.reshape(N_TILE, N_SUB)


def set_ends(entries, own_key, low, largest):
    spot = [jax.random.randint(jax.random.fold_in(own_key, axis), (), 0, length) for axis, length in enumerate(entries.shape)]
    widest = entries.shape.index(max(entries.shape))
    beside = spot[:widest] + [(spot[widest] + 1) % entries.shape[widest]] + spot[widest + 1:]
    return entries.at[tuple(spot)].set(low).at[tuple(beside)].set(largest)


def shard_levels(stream_key, dims, shards, least, top_value):
    factor_of = 1.0
    for axis_at, parts in shards:
        steps = jax.random.uniform(jax.random.fold_in(jax.random.fold_in(stream_key, 6), axis_at), (parts,), jnp.float32, least / len(shards), top_value / len(shards))
        factor_of = factor_of * jnp.repeat(jnp.exp(steps), dims[axis_at] // parts).reshape((-1,) + (1,) * (len(dims) - 1 - axis_at))
    return factor_of


def gaussian(own_key, dims, width, most, pieces=(), kind=jnp.bfloat16):
    result = jax.random.normal(own_key, dims, jnp.float32) * width
    if len(pieces) > 0:
        result = shard_levels(own_key, dims, pieces, -0.22, 0.18) * result
    return jnp.clip(result, min=-most, max=most).astype(kind)


def setup_inputs(seed: int = 0) -> dict:
    seeds = jax.random.split(jax.random.key(seed), 10)
    return {
        "condition": gaussian(seeds[0], (CIN, NY, NX), 1.0, 6.0, ((1, 64), (2, 4))),
        "state": gaussian(seeds[1], (COUT, NY, NX), 2.0, 12.0, ((1, 64), (2, 4)), jnp.float32),
        "corner_rows": set_ends(jax.random.randint(seeds[2], (N_TILE, N_SUB, PATCH_DEV), 0, BY + 1), jax.random.fold_in(seeds[2], 1), 0, BY).astype(jnp.int32),
        "corner_cols": set_ends(jax.random.randint(seeds[3], (N_TILE, N_SUB, PATCH_DEV), 0, BX + 1), jax.random.fold_in(seeds[3], 1), 0, BX).astype(jnp.int32),
        "live_counts": draw_live_counts(jax.random.fold_in(seeds[9], 71), 0),
        "blend_weight": jnp.clip(jnp.exp(math.log(5.0) - 3.218876 * jax.random.uniform(seeds[5], (N_TILE, N_SUB, PATCH_DEV, PATCH, PATCH), jnp.float32) ** shard_levels(seeds[5], (N_TILE, N_SUB, PATCH_DEV, PATCH, PATCH), ((0, 64), (1, 4)), -0.2, 0.2)), 0.2, 5.0),
        "conv_in": gaussian(seeds[6], (3, 3, HID, CIN + COUT), (9 * (CIN + COUT)) ** -0.5, 0.5),
        "conv_mid": gaussian(seeds[7], (3, 3, HID, HID), (9 * HID) ** -0.5, 0.25),
        "proj_out": gaussian(seeds[8], (COUT, HID), HID ** -0.5, 0.75),
    }


SIGMA = 2.0
SIGMA_NEXT = 1.6
C_IN = 1.0 / (SIGMA * SIGMA + 0.25) ** 0.5
C_SKIP = 0.25 / (SIGMA * SIGMA + 0.25)
C_OUT = 0.5 * SIGMA / (SIGMA * SIGMA + 0.25) ** 0.5


def convolve(values, kernel):
    side = values.shape[1]
    padded = jnp.pad(values, ((0, 0), (1, 1), (1, 1)))
    total = jnp.zeros((kernel.shape[2], side, side), jnp.float32)
    for first in range(3):
        for second in range(3):
            window = padded[:, first:first + side, second:second + side].astype(jnp.float32)
            total = total + jnp.einsum("oc,chw->ohw", kernel[first, second].astype(jnp.float32), window)
    return total


def network(patch, conv_in, conv_mid, proj_out):
    hidden_one = convolve(patch, conv_in)
    act_one = jax.nn.silu(hidden_one).astype(jnp.bfloat16)
    hidden_two = hidden_one + convolve(act_one, conv_mid)
    act_two = jax.nn.silu(hidden_two).astype(jnp.bfloat16)
    return jnp.einsum("oc,chw->ohw", proj_out.astype(jnp.float32), act_two.astype(jnp.float32))


def reference(condition, state, corner_rows, corner_cols, live_counts, blend_weight, conv_in, conv_mid, proj_out):
    half = PATCH // 2
    scaled = (state * C_IN).astype(jnp.bfloat16)
    inputs = jnp.concatenate([condition, scaled], axis=0)
    inputs = jnp.pad(inputs, ((0, 0), (half, half), (half, half)))
    total_slots = N_TILE * N_SUB * PATCH_DEV
    flat_rows = corner_rows.reshape(total_slots)
    flat_cols = corner_cols.reshape(total_slots)
    flat_weight = blend_weight.reshape(total_slots, PATCH, PATCH)
    numer0 = jnp.zeros((COUT, NY + PATCH, NX + PATCH), jnp.float32)
    weights0 = jnp.zeros((1, NY + PATCH, NX + PATCH), jnp.float32)

    def visit(carry, index):
        numer, weights = carry
        device = index // PATCH_DEV
        slot = index % PATCH_DEV
        tile_idx = device // N_SUB
        sub_idx = device % N_SUB
        live = slot < live_counts[tile_idx, sub_idx]
        row = (tile_idx * BY + flat_rows[index]).astype(jnp.int32)
        col = (sub_idx * BX + flat_cols[index]).astype(jnp.int32)
        zero = jnp.zeros((), jnp.int32)
        patch = lax.dynamic_slice(inputs, (zero, row, col), (CIN + COUT, PATCH, PATCH))
        net = lax.cond(live, lambda p: network(p, conv_in, conv_mid, proj_out),
                       lambda p: jnp.zeros((COUT, PATCH, PATCH), jnp.float32), patch)
        weight = flat_weight[index] * live.astype(jnp.float32)
        old_n = lax.dynamic_slice(numer, (zero, row, col), (COUT, PATCH, PATCH))
        numer = lax.dynamic_update_slice(numer, old_n + weight[None] * net, (zero, row, col))
        old_w = lax.dynamic_slice(weights, (zero, row, col), (1, PATCH, PATCH))
        weights = lax.dynamic_update_slice(weights, old_w + weight[None], (zero, row, col))
        return (numer, weights), None

    (numer, weights), _ = lax.scan(visit, (numer0, weights0), jnp.arange(total_slots, dtype=jnp.int32))
    numer = numer[:, half:half + NY, half:half + NX]
    weights = weights[:, half:half + NY, half:half + NX]
    denoised = (state * (1.0 + C_SKIP * weights) + C_OUT * numer) / (1.0 + weights)
    next_state = state + (SIGMA_NEXT - SIGMA) * (state - denoised) / SIGMA
    return denoised, next_state
```

```python
import jax
import jax.numpy as jnp
from jax import lax
from jax.experimental import pallas as pl
from jax.experimental.pallas import tpu as pltpu
from jax.sharding import PartitionSpec as P

SIGMA = 2.0
SIGMA_NEXT = 1.6
C_IN = 1.0 / (SIGMA * SIGMA + 0.25) ** 0.5
C_SKIP = 0.25 / (SIGMA * SIGMA + 0.25)
C_OUT = 0.5 * SIGMA / (SIGMA * SIGMA + 0.25) ** 0.5

BY = 256
BX = 256
SIDE = 128
HALF = 64
CC = 12
CH = 16
HID = 64
OUT = 4
SLOTS = 2
LANES = 128
WIDE = 2 * LANES
STEP = 8
X_ROWS = BY + 4
ACC_ROWS = BY + 2 * STEP + 8
W_ROWS = SIDE + 2 * STEP
PIECES = 9 * SLOTS
TILE_MSG = 2 * HALF + 4 * CH + 16
SUB_MSG = SIDE + 2 * HALF + 4 * CH + 64 + 16
F32 = jnp.float32
BF16 = jnp.bfloat16


def iota(shape, dim):
    return lax.broadcasted_iota(jnp.int32, shape, dim)


def scaled(state):
    return (state * C_IN).astype(BF16)


def own_meta(rows_ref, cols_ref, live_ref):
    sub = iota((16, LANES), 0)
    values = (rows_ref[0, 0, 0], rows_ref[0, 0, 1], cols_ref[0, 0, 0], cols_ref[0, 0, 1], live_ref[0, 0])
    tile = jnp.zeros((16, LANES), jnp.int32)
    for k, value in enumerate(values):
        tile = jnp.where(sub == k, value, tile)
    return tile


def pack_tile(rows_ref, cols_ref, live_ref, c_top, c_bot, s_top, s_bot, weight_ref, up_ref, down_ref, tmp):
    meta = own_meta(rows_ref, cols_ref, live_ref).astype(F32).astype(BF16)
    for out, cond, state, low, first_c, first_s in (
        (up_ref, c_top, s_top, 0, 0, 0),
        (down_ref, c_bot, s_bot, HALF, 14, 6),
    ):
        for p in range(SLOTS):
            out[p * HALF : (p + 1) * HALF, :] = weight_ref[0, 0, p, low : low + HALF, :].astype(BF16)
        for c in range(CH):
            if c < CC:
                tile = cond[c].astype(F32)[first_c : first_c + 2, :]
            else:
                tile = scaled(state[c - CC]).astype(F32)[first_s : first_s + 2, :]
            for t in range(2):
                for r in range(2):
                    at = t * 2 * CH + r * CH + c
                    tmp[at : at + 1, :] = tile[r : r + 1, t * LANES : (t + 1) * LANES]
        out[2 * HALF : 2 * HALF + 4 * CH, :] = tmp[...].astype(BF16)
        out[2 * HALF + 4 * CH :, :] = meta


def pack_sub(rows_ref, cols_ref, live_ref, cond_ref, state_ref, weight_ref, above_ref, below_ref, left_ref, right_ref):
    lane = iota((1, LANES), 1)
    meta0 = own_meta(rows_ref, cols_ref, live_ref).astype(F32)
    sub = iota((16, LANES), 0)
    first = 2 * HALF + 4 * CH
    meta_a = pltpu.roll(above_ref[first:, :].astype(F32), 5, 0)
    meta_b = pltpu.roll(below_ref[first:, :].astype(F32), 10, 0)
    meta = jnp.where(sub < 5, meta0, jnp.where(sub < 10, meta_a, meta_b)).astype(BF16)
    picks = iota((8, LANES), 0)
    spots = iota((8, LANES), 1)
    for out, side in ((left_ref, 0), (right_ref, 1)):
        def packed(one, two):
            if side == 0:
                return jnp.where(lane < HALF, one, pltpu.roll(two, HALF, 1)).astype(BF16)
            return jnp.where(lane < HALF, pltpu.roll(one, HALF, 1), two).astype(BF16)

        out[0:SIDE, :] = packed(weight_ref[0, 0, 0], weight_ref[0, 0, 1])
        at = SIDE
        for msg in (above_ref, below_ref):
            out[at : at + HALF, :] = packed(msg[0:HALF, :].astype(F32), msg[HALF : 2 * HALF, :].astype(F32))
            at += HALF
        for msg in (above_ref, below_ref):
            begin = 2 * HALF + side * 2 * CH
            out[at : at + 2 * CH, :] = msg[begin : begin + 2 * CH, :]
            at += 2 * CH
        lanes = slice(side * LANES, (side + 1) * LANES)
        pick = (spots == picks + (0 if side == 0 else LANES - 2)) & (picks < 2)
        pick = pick.astype(F32).astype(BF16)
        cond = cond_ref[:, :, lanes].reshape(CC * BY, LANES)
        state = scaled(state_ref[:, :, lanes]).reshape(OUT * BY, LANES)
        for q in range(4):
            part = cond[q * 4 * BY : (q + 1) * 4 * BY] if q < 3 else state
            edge = lax.dot_general(pick, part, (((1,), (1,)), ((), ())), preferred_element_type=F32)
            if q == 0:
                edges = edge
            else:
                edges = edges + pltpu.roll(edge, 2 * q, 0)
        for m in range(4):
            both = jnp.concatenate([edges[:, (2 * m) * LANES : (2 * m + 1) * LANES], edges[:, (2 * m + 1) * LANES : (2 * m + 2) * LANES]], axis=0)
            out[at : at + 16, :] = both.astype(BF16)
            at += 16
        out[at:, :] = meta


def main_kernel(
    rows_ref, cols_ref, live_ref, cond_ref, state_ref, weight_ref,
    above_ref, below_ref, left_ref, right_ref, w1_ref, w2_ref, w3_ref,
    den_ref, next_ref,
    x_ref, p_ref, a_ref, u_ref, acc_ref, wall_ref, meta_v, meta_s, sem,
):
    lane = iota((1, LANES), 1)
    first = 2 * HALF + 4 * CH
    meta_v[0:16, :] = own_meta(rows_ref, cols_ref, live_ref)
    meta_v[16:32, :] = above_ref[first:, :].astype(F32).astype(jnp.int32)
    meta_v[32:48, :] = below_ref[first:, :].astype(F32).astype(jnp.int32)
    meta_v[48:64, :] = left_ref[SUB_MSG - 16 :, :].astype(F32).astype(jnp.int32)
    meta_v[64:80, :] = right_ref[SUB_MSG - 16 :, :].astype(F32).astype(jnp.int32)
    copy = pltpu.make_async_copy(meta_v, meta_s, sem)
    copy.start()

    for c in range(CH):
        value = cond_ref[c].astype(F32) if c < CC else scaled(state_ref[c - CC]).astype(F32)
        for t in range(2):
            x_ref[t + 1, pl.ds(2 * CH + c, BY, stride=CH), :] = value[:, t * LANES : (t + 1) * LANES]
    corner = SIDE + 2 * HALF
    for msg, row, spot in ((above_ref, 0, 0), (below_ref, BY + 2, 2 * CH)):
        for t in range(2):
            x_ref[t + 1, row * CH : (row + 2) * CH, :] = msg[
                2 * HALF + t * 2 * CH : 2 * HALF + (t + 1) * 2 * CH, :
            ].astype(F32)
        from_left = left_ref[corner + spot : corner + spot + 2 * CH, :].astype(F32)
        from_right = right_ref[corner + spot : corner + spot + 2 * CH, :].astype(F32)
        x_ref[0, row * CH : (row + 2) * CH, :] = jnp.where(
            lane < 2, from_right, jnp.where(lane >= LANES - 2, from_left, 0.0)
        )
    edge_at = corner + 4 * CH
    picks = iota((8, LANES), 0)
    spots = iota((8, LANES), 1)
    for m in range(8):
        at = edge_at + 8 * m
        base = at - at % 16
        odd = (at % 16) // 8
        ours = []
        for msg in (left_ref, right_ref):
            ours.append(msg[base : base + 16, :].astype(F32)[8 * odd : 8 * odd + 8, :])
        both = jnp.concatenate(ours, axis=0)
        turned = both.T.astype(BF16)
        for q in range(4):
            to_left = (picks == 2 * q + spots - (LANES - 2)) & (spots >= LANES - 2)
            to_right = (picks == 2 * q + spots) & (spots < 2)
            place = jnp.concatenate([to_left.astype(F32), to_right.astype(F32)], axis=0).astype(BF16)
            value = jnp.dot(turned, place, preferred_element_type=F32)
            c = 4 * q + m // 2
            row = (m % 2) * LANES
            x_ref[0, pl.ds((2 + row) * CH + c, LANES, stride=CH), :] = value

    for p in range(SLOTS):
        wall_ref[p, 0:SIDE, :] = weight_ref[0, 0, p]
        wall_ref[2 + p, HALF:SIDE, :] = above_ref[p * HALF : (p + 1) * HALF, :].astype(F32)
        wall_ref[4 + p, 0:HALF, :] = below_ref[p * HALF : (p + 1) * HALF, :].astype(F32)
        for d, msg, turn in ((3, left_ref, p == 0), (6, right_ref, p == 1)):
            def side(lo, hi):
                part = msg[lo:hi, :].astype(F32)
                return pltpu.roll(part, HALF, 1) if turn else part

            wall_ref[2 * d + p, 0:SIDE, :] = side(0, SIDE)
            wall_ref[2 * d + 2 + p, HALF:SIDE, :] = side(SIDE, SIDE + HALF)
            wall_ref[2 * d + 4 + p, 0:HALF, :] = side(SIDE + HALF, SIDE + 2 * HALF)
    for k in range(PIECES):
        wall_ref[k, SIDE:W_ROWS, :] = jnp.zeros((W_ROWS - SIDE, LANES), F32)

    def clear(i, carry):
        for t in range(1, 3):
            acc_ref[t, pl.ds(pl.multiple_of(i * 64, 64), 64), :] = jnp.zeros((64, LANES), F32)
        return carry

    lax.fori_loop(0, BY * 8 // 64, clear, 0)
    copy.wait()

    one_row = (iota((8, 1), 0) == OUT).astype(F32)

    def piece(k, carry):
        d, p = k // 2, k % 2
        across, along = d // 3, d % 3
        base = jnp.where(across == 0, 16 * along, 32 + 16 * across + 5 * along)
        row0 = meta_s[base + p, 0] - HALF + jnp.where(along == 0, 0, jnp.where(along == 1, -BY, BY))
        col0 = meta_s[base + 2 + p, 0] - HALF + jnp.where(across == 0, 0, jnp.where(across == 1, -BX, BX))
        live = p < meta_s[base + 4, 0]
        begin = jnp.maximum(-row0, 0)
        end = jnp.minimum(SIDE, BY - row0)
        touches = (begin < end) & (col0 > -SIDE) & (col0 < BX) & live

        @pl.when(touches)
        def _():
            steps = (end - begin + 2 * STEP - 1) // (2 * STEP)
            high = steps * STEP
            q = (col0 + LANES) // LANES
            rem = (col0 + LANES) % LANES
            after_q = jnp.where(q == 2, 0, q + 1)
            turn = (LANES - rem) % LANES
            starts = (begin, begin + high)

            def stage(j):
                for h in range(2):
                    local = starts[h] - 2 + j
                    inside = ((local >= 0) & (local < SIDE)).astype(F32)
                    at = pl.multiple_of(jnp.clip(row0 + local + 2, 0, X_ROWS - 1) * CH, CH)
                    one = pltpu.roll(x_ref[q, pl.ds(at, CH), :], turn, 1)
                    two = pltpu.roll(x_ref[after_q, pl.ds(at, CH), :], turn, 1)
                    mid = jnp.where(lane < LANES - rem, one, two) * inside
                    before = jnp.where(lane == 0, 0.0, pltpu.roll(mid, 1, 1))
                    after = jnp.where(lane == LANES - 1, 0.0, pltpu.roll(mid, LANES - 1, 1))
                    full = jnp.concatenate([before, mid, after], axis=0).astype(BF16)
                    p_ref[pl.ds(pl.multiple_of(j * 3 * CH, 16), 3 * CH), h * LANES : (h + 1) * LANES] = full

            def stage_some(i, carry):
                for e in range(4):
                    stage(i * 4 + e)
                return carry

            lax.fori_loop(0, high // 4 + 1, stage_some, 0)

            def first_conv(a):
                rhs = p_ref[pl.ds(pl.multiple_of(a * 3 * CH, 16), 4 * 3 * CH), :]
                u = jnp.dot(w1_ref[...], rhs, preferred_element_type=F32)
                u_ref[pl.ds(pl.multiple_of(a * HID, HID), 2 * HID), :] = u
                act = u + u * jnp.tanh(u)
                for r in range(2):
                    for h in range(2):
                        mid = act[r * HID : (r + 1) * HID, h * LANES : (h + 1) * LANES]
                        before = jnp.where(lane == 0, 0.0, pltpu.roll(mid, 1, 1))
                        after = jnp.where(lane == LANES - 1, 0.0, pltpu.roll(mid, LANES - 1, 1))
                        for b, part in enumerate((before, mid, after)):
                            at = pl.multiple_of((a + r) * 3 * HID + b * HID, HID)
                            a_ref[pl.ds(at, HID), h * LANES : (h + 1) * LANES] = part.astype(BF16)

            first_conv(0)

            def first_some(i, carry):
                for e in range(STEP // 2):
                    first_conv(2 + i * STEP + 2 * e)
                return carry

            lax.fori_loop(0, steps, first_some, 0)

            for h in range(2):
                for spot in (-starts[h], SIDE + 1 - starts[h]):
                    @pl.when((spot >= 0) & (spot <= high + 1))
                    def _():
                        at = pl.multiple_of(spot * 3 * HID, HID)
                        a_ref[pl.ds(at, 3 * HID), h * LANES : (h + 1) * LANES] = jnp.zeros((3 * HID, LANES), BF16)

            def second_conv(r):
                rhs = a_ref[pl.ds(pl.multiple_of(r * 3 * HID, HID), 4 * 3 * HID), :]
                v = jnp.dot(w2_ref[...], rhs, preferred_element_type=F32)
                v = v + u_ref[pl.ds(pl.multiple_of((r + 1) * HID, HID), 2 * HID), :]
                return (v + v * jnp.tanh(v)).astype(BF16)

            def second_some(i, carry):
                for e in range(STEP // 4):
                    r = i * STEP + 4 * e
                    act = jnp.concatenate([second_conv(r), second_conv(r + 2)], axis=0)
                    net = jnp.dot(w3_ref[...], act, preferred_element_type=F32)
                    for f in range(4):
                        for h in range(2):
                            local = starts[h] + r + f
                            weight = wall_ref[k, pl.ds(local, 1), :]
                            y = (net[8 * f : 8 * f + 8, h * LANES : (h + 1) * LANES] + one_row) * weight
                            y = pltpu.roll(y, rem, 1)
                            at = pl.ds(pl.multiple_of((row0 + local) * 8, 8), 8)
                            acc_ref[q, at, :] += jnp.where(lane >= rem, y, 0.0)
                            acc_ref[after_q, at, :] += jnp.where(lane < rem, y, 0.0)
                return carry

            lax.fori_loop(0, steps, second_some, 0)

        return carry

    lax.fori_loop(0, PIECES, piece, 0)

    def finish(i, carry):
        row = pl.multiple_of(i * 8, 8)
        for t in range(2):
            lanes = slice(t * LANES, (t + 1) * LANES)
            total = acc_ref[t + 1, pl.ds(row * 8 + OUT, 8, stride=8), :]
            over = 1.0 / (1.0 + total)
            for o in range(OUT):
                state = state_ref[o, pl.ds(row, 8), lanes]
                numer = acc_ref[t + 1, pl.ds(row * 8 + o, 8, stride=8), :]
                den = (state * (1.0 + C_SKIP * total) + C_OUT * numer) * over
                den_ref[o, pl.ds(row, 8), lanes] = den
                next_ref[o, pl.ds(row, 8), lanes] = state + (SIGMA_NEXT - SIGMA) * (state - den) / SIGMA
        return carry

    lax.fori_loop(0, BY // 8, finish, 0)


def banded(kernel, times):
    outs, chans = kernel.shape[2], kernel.shape[3]
    flat = (0.5 * jnp.transpose(kernel, (2, 0, 1, 3))).astype(BF16).reshape(outs, 9 * chans)
    step = 3 * chans
    return jnp.concatenate([jnp.pad(flat, ((0, 0), (r * step, (times - 1 - r) * step))) for r in range(times)], axis=0)


def shifted(value, axis, steps):
    count = lax.axis_size(axis)
    first, last = max(0, -steps), min(count, count - steps)
    return lax.ppermute(value, axis, [(i, i + steps) for i in range(first, last)])


def per_device(condition, state, corner_rows, corner_cols, live_counts, blend_weight, conv_in, conv_mid, proj_out):
    smem = pl.BlockSpec(memory_space=pltpu.SMEM)
    vmem = pl.BlockSpec(memory_space=pltpu.VMEM)
    whole_w = pl.BlockSpec((1, 1, SLOTS, SIDE, SIDE), lambda i: (0, 0, 0, 0, 0))
    msg = jax.ShapeDtypeStruct((TILE_MSG, LANES), BF16)
    up, down = pl.pallas_call(
        pack_tile,
        grid=(1,),
        in_specs=[
            smem, smem, smem,
            pl.BlockSpec((CC, 16, BX), lambda i: (0, 0, 0)),
            pl.BlockSpec((CC, 16, BX), lambda i: (0, BY // 16 - 1, 0)),
            pl.BlockSpec((OUT, 8, BX), lambda i: (0, 0, 0)),
            pl.BlockSpec((OUT, 8, BX), lambda i: (0, BY // 8 - 1, 0)),
            whole_w,
        ],
        out_specs=[pl.BlockSpec((TILE_MSG, LANES), lambda i: (0, 0))] * 2,
        out_shape=[msg, msg],
        scratch_shapes=[pltpu.VMEM((4 * CH, LANES), F32)],
        name="pack_tile",
    )(corner_rows, corner_cols, live_counts, condition, condition, state, state, blend_weight)
    above = shifted(down, "tile", 1)
    below = shifted(up, "tile", -1)
    w1 = banded(conv_in, 2)
    w2 = banded(conv_mid, 2)
    rows8 = jnp.pad(proj_out, ((0, 8 - OUT), (0, 0)))
    w3 = jnp.concatenate([jnp.pad(rows8, ((0, 0), (r * HID, (3 - r) * HID))) for r in range(4)], axis=0)
    msg = jax.ShapeDtypeStruct((SUB_MSG, LANES), BF16)
    left, right = pl.pallas_call(
        pack_sub,
        in_specs=[smem] * 3 + [vmem] * 5,
        out_specs=[vmem] * 2,
        out_shape=[msg, msg],
        name="pack_sub",
        compiler_params=pltpu.CompilerParams(vmem_limit_bytes=32 << 20),
    )(corner_rows, corner_cols, live_counts, condition, state, blend_weight, above, below)
    from_left = shifted(right, "sub", 1)
    from_right = shifted(left, "sub", -1)
    out = jax.ShapeDtypeStruct((OUT, BY, BX), F32)
    return tuple(pl.pallas_call(
        main_kernel,
        in_specs=[smem] * 3 + [vmem] * 10,
        out_specs=[vmem] * 2,
        out_shape=[out, out],
        scratch_shapes=[
            pltpu.VMEM((3, X_ROWS * CH, LANES), F32),
            pltpu.VMEM(((HALF + 8) * 3 * CH, WIDE), BF16),
            pltpu.VMEM(((HALF + 4) * 3 * HID, WIDE), BF16),
            pltpu.VMEM(((HALF + 4) * HID, WIDE), F32),
            pltpu.VMEM((3, ACC_ROWS * 8, LANES), F32),
            pltpu.VMEM((PIECES, W_ROWS, LANES), F32),
            pltpu.VMEM((80, LANES), jnp.int32),
            pltpu.SMEM((80, LANES), jnp.int32),
            pltpu.SemaphoreType.DMA,
        ],
        name="patches",
        compiler_params=pltpu.CompilerParams(vmem_limit_bytes=56 << 20),
    )(corner_rows, corner_cols, live_counts, condition, state, blend_weight, above, below, from_left, from_right, w1, w2, w3))


def solution(mesh):
    placed = (
        P(None, "tile", "sub"),
        P(None, "tile", "sub"),
        P("tile", "sub", None),
        P("tile", "sub", None),
        P("tile", "sub"),
        P("tile", "sub", None, None, None),
        P(),
        P(),
        P(),
    )
    return jax.shard_map(
        per_device,
        mesh=mesh,
        in_specs=placed,
        out_specs=(P(None, "tile", "sub"), P(None, "tile", "sub")),
        check_vma=False,
    )
```

```python
import jax
import jax.numpy as jnp
from jax import lax
from jax.experimental import pallas as pl
from jax.experimental.pallas import tpu as pltpu
from jax.sharding import PartitionSpec as P

SIGMA = 2.0
SIGMA_NEXT = 1.6
C_IN = 1.0 / (SIGMA * SIGMA + 0.25) ** 0.5
C_SKIP = 0.25 / (SIGMA * SIGMA + 0.25)
C_OUT = 0.5 * SIGMA / (SIGMA * SIGMA + 0.25) ** 0.5

BY = 256
BX = 256
SIDE = 128
HALF = 64
CC = 12
CH = 16
HID = 64
OUT = 4
SLOTS = 2
LANES = 128
WIDE = 2 * LANES
STEP = 8
X_ROWS = BY + 4
ACC_ROWS = BY + 2 * STEP
LAG = 3
UNITS = 512
PIECES = 9 * SLOTS
TILE_MSG = 2 * HALF + 4 * CH + 16
SUB_MSG = SIDE + 2 * HALF + 4 * CH + 64 + 16
F32 = jnp.float32
BF16 = jnp.bfloat16


def iota(shape, dim):
    return lax.broadcasted_iota(jnp.int32, shape, dim)


def scaled(state):
    return (state * C_IN).astype(BF16)


def own_meta(rows_ref, cols_ref, live_ref):
    sub = iota((16, LANES), 0)
    values = (rows_ref[0, 0, 0], rows_ref[0, 0, 1], cols_ref[0, 0, 0], cols_ref[0, 0, 1], live_ref[0, 0])
    tile = jnp.zeros((16, LANES), jnp.int32)
    for k, value in enumerate(values):
        tile = jnp.where(sub == k, value, tile)
    return tile


def pack_tile(rows_ref, cols_ref, live_ref, c_top, c_bot, s_top, s_bot, weight_ref, up_ref, down_ref, tmp):
    meta = own_meta(rows_ref, cols_ref, live_ref).astype(F32).astype(BF16)
    for out, cond, state, low, first_c, first_s in (
        (up_ref, c_top, s_top, 0, 0, 0),
        (down_ref, c_bot, s_bot, HALF, 14, 6),
    ):
        for p in range(SLOTS):
            out[p * HALF : (p + 1) * HALF, :] = weight_ref[0, 0, p, low : low + HALF, :].astype(BF16)
        for c in range(CH):
            if c < CC:
                tile = cond[c].astype(F32)[first_c : first_c + 2, :]
            else:
                tile = scaled(state[c - CC]).astype(F32)[first_s : first_s + 2, :]
            for t in range(2):
                for r in range(2):
                    at = t * 2 * CH + r * CH + c
                    tmp[at : at + 1, :] = tile[r : r + 1, t * LANES : (t + 1) * LANES]
        out[2 * HALF : 2 * HALF + 4 * CH, :] = tmp[...].astype(BF16)
        out[2 * HALF + 4 * CH :, :] = meta


def prepare(cond_ref, state_ref, body_ref, edge_ref):
    to = iota((CH * CH, CH * CH), 0)
    of = iota((CH * CH, CH * CH), 1)
    turn = (of == (to % CH) * CH + to // CH).astype(F32).astype(BF16)
    picks = iota((16, LANES), 0)
    spots = iota((16, LANES), 1)
    first = ((picks == spots) & (picks < 2)).astype(F32).astype(BF16)
    last = ((picks == spots - (LANES - 4)) & (picks >= 2)).astype(F32).astype(BF16)

    def group(i, carry):
        rows = pl.ds(pl.multiple_of(i * CH, CH), CH)
        value = jnp.concatenate(
            [cond_ref[:, rows, :].reshape(CC * CH, BX), scaled(state_ref[:, rows, :]).reshape(OUT * CH, BX)], axis=0
        )
        value = jnp.dot(turn, value, preferred_element_type=F32).astype(BF16)
        at = pl.ds(pl.multiple_of(i * CH * CH, CH * CH), CH * CH)
        edge = jnp.zeros((16, CH * CH), F32)
        for t, pick in enumerate((first, last)):
            part = value[:, t * LANES : (t + 1) * LANES]
            body_ref[t, at, :] = part
            edge = edge + lax.dot_general(pick, part, (((1,), (1,)), ((), ())), preferred_element_type=F32)
        edge_ref[:, at] = edge.astype(BF16)
        return carry

    lax.fori_loop(0, BY // CH, group, 0)


def pack_sub(rows_ref, cols_ref, live_ref, weight_ref, edge_ref, above_ref, below_ref, left_ref, right_ref):
    lane = iota((1, LANES), 1)
    meta0 = own_meta(rows_ref, cols_ref, live_ref).astype(F32)
    sub = iota((16, LANES), 0)
    first = 2 * HALF + 4 * CH
    meta_a = pltpu.roll(above_ref[first:, :].astype(F32), 5, 0)
    meta_b = pltpu.roll(below_ref[first:, :].astype(F32), 10, 0)
    meta = jnp.where(sub < 5, meta0, jnp.where(sub < 10, meta_a, meta_b)).astype(BF16)
    for out, side in ((left_ref, 0), (right_ref, 1)):
        def packed(one, two):
            if side == 0:
                return jnp.where(lane < HALF, one, pltpu.roll(two, HALF, 1)).astype(BF16)
            return jnp.where(lane < HALF, pltpu.roll(one, HALF, 1), two).astype(BF16)

        out[0:SIDE, :] = packed(weight_ref[0, 0, 0], weight_ref[0, 0, 1])
        at = SIDE
        for msg in (above_ref, below_ref):
            out[at : at + HALF, :] = packed(msg[0:HALF, :].astype(F32), msg[HALF : 2 * HALF, :].astype(F32))
            at += HALF
        for msg in (above_ref, below_ref):
            begin = 2 * HALF + side * 2 * CH
            out[at : at + 2 * CH, :] = msg[begin : begin + 2 * CH, :]
            at += 2 * CH
        edge = edge_ref[...].astype(F32)
        for m in range(4):
            rows = []
            for e in range(8):
                spot = (8 * m + e) * LANES
                rows.append(edge[2 * side : 2 * side + 2, spot : spot + LANES])
            out[at : at + 16, :] = jnp.concatenate(rows, axis=0).astype(BF16)
            at += 16
        out[at:, :] = meta


def main_kernel(
    rows_ref, cols_ref, live_ref, body_ref, state_ref, weight_ref,
    above_ref, below_ref, left_ref, right_ref, w1_ref, w2_ref, w3_ref,
    den_ref, next_ref,
    xb_ref, p_ref, a_ref, u_ref, q_ref, acc_ref, wall_ref, meta_v, meta_s, unit_ref, place_ref, list_ref, sem, body_sem,
):
    lane = iota((1, LANES), 1)
    first = 2 * HALF + 4 * CH
    meta_v[0:16, :] = own_meta(rows_ref, cols_ref, live_ref)
    meta_v[16:32, :] = above_ref[first:, :].astype(F32).astype(jnp.int32)
    meta_v[32:48, :] = below_ref[first:, :].astype(F32).astype(jnp.int32)
    meta_v[48:64, :] = left_ref[SUB_MSG - 16 :, :].astype(F32).astype(jnp.int32)
    meta_v[64:80, :] = right_ref[SUB_MSG - 16 :, :].astype(F32).astype(jnp.int32)
    copy = pltpu.make_async_copy(meta_v, meta_s, sem)
    copy.start()

    body = pltpu.make_async_copy(body_ref, xb_ref.at[1:3, 2 * CH : (BY + 2) * CH, :], body_sem)
    body.start()
    corner = SIDE + 2 * HALF
    for msg, row, spot in ((above_ref, 0, 0), (below_ref, BY + 2, 2 * CH)):
        for t in range(2):
            xb_ref[t + 1, row * CH : (row + 2) * CH, :] = msg[2 * HALF + t * 2 * CH : 2 * HALF + (t + 1) * 2 * CH, :]
        from_left = left_ref[corner + spot : corner + spot + 2 * CH, :].astype(F32)
        from_right = right_ref[corner + spot : corner + spot + 2 * CH, :].astype(F32)
        xb_ref[0, row * CH : (row + 2) * CH, :] = jnp.where(
            lane < 2, from_right, jnp.where(lane >= LANES - 2, from_left, 0.0)
        ).astype(BF16)
    edge_at = corner + 4 * CH
    picks = iota((32, LANES), 0)
    spots = iota((32, LANES), 1)
    for m in range(4):
        rows = slice(edge_at + 16 * m, edge_at + 16 * m + 16)
        both = jnp.concatenate([left_ref[rows, :].astype(F32), right_ref[rows, :].astype(F32)], axis=0)
        turned = both.T.astype(BF16)
        for e in range(8):
            to_left = (picks - 2 * e == spots - (LANES - 2)) & (spots >= LANES - 2) & (picks < 16)
            to_right = (picks - 16 - 2 * e == spots) & (spots < 2) & (picks >= 16)
            place = (to_left | to_right).astype(F32).astype(BF16)
            at = 2 * CH + (8 * m + e) * LANES
            xb_ref[0, at : at + LANES, :] = jnp.dot(turned, place, preferred_element_type=F32).astype(BF16)
    p_ref[...] = jnp.zeros_like(p_ref)
    a_ref[...] = jnp.zeros_like(a_ref)

    for p in range(SLOTS):
        wall_ref[p, 0:SIDE, :] = weight_ref[0, 0, p]
        wall_ref[2 + p, HALF:SIDE, :] = above_ref[p * HALF : (p + 1) * HALF, :].astype(F32)
        wall_ref[4 + p, 0:HALF, :] = below_ref[p * HALF : (p + 1) * HALF, :].astype(F32)
        for d, msg, turn in ((3, left_ref, p == 0), (6, right_ref, p == 1)):
            def side(lo, hi):
                part = msg[lo:hi, :].astype(F32)
                return pltpu.roll(part, HALF, 1) if turn else part

            wall_ref[2 * d + p, 0:SIDE, :] = side(0, SIDE)
            wall_ref[2 * d + 2 + p, HALF:SIDE, :] = side(SIDE, SIDE + HALF)
            wall_ref[2 * d + 4 + p, 0:HALF, :] = side(SIDE + HALF, SIDE + 2 * HALF)

    def clear(i, carry):
        for t in range(1, 3):
            acc_ref[t, pl.ds(pl.multiple_of(i * 256 + STEP * 8, 64), 256), :] = jnp.zeros((256, LANES), F32)
        return carry

    lax.fori_loop(0, BY * 8 // 256, clear, 0)
    copy.wait()

    one_row = (iota((8, 1), 0) == OUT).astype(F32)

    def nothing(i):
        unit_ref[0, i] = 0
        unit_ref[1, i] = 0
        unit_ref[2, i] = BY

    for i in range(2 * LAG):
        nothing(i)

    total = jnp.int32(0)
    pos = jnp.int32(0)
    for k in range(PIECES):
        d, p = k // 2, k % 2
        across, along = d // 3, d % 3
        base = 16 * along if across == 0 else 32 + 16 * across + 5 * along
        row0 = meta_s[base + p, 0] + (0, -BY, BY)[along] - HALF
        col0 = meta_s[base + 2 + p, 0] + (0, -BX, BX)[across] - HALF
        low = jnp.maximum(-row0, 0) // STEP
        high = (jnp.minimum(SIDE, BY - row0) + STEP - 1) // STEP
        touches = (low < high) & (col0 > -SIDE) & (col0 < BX) & (p < meta_s[base + 4, 0])
        place_ref[0, k] = (col0 + LANES) // LANES
        place_ref[1, k] = (col0 + LANES) % LANES
        list_ref[0, pos] = k
        list_ref[1, pos] = low
        list_ref[2, pos] = high
        list_ref[3, pos] = row0
        pos = pos + touches.astype(jnp.int32)
        total = total + jnp.where(touches, high - low, 0)
    for i in range(4 * LAG + 4):
        list_ref[0, pos + i] = 0
        list_ref[1, pos + i] = 0
        list_ref[2, pos + i] = 1
        list_ref[3, pos + i] = BY
    count = total + 2 * LAG
    body.wait()

    def advance(unit, at, i):
        unit_ref[0, unit] = list_ref[0, at]
        unit_ref[1, unit] = i * STEP
        unit_ref[2, unit] = list_ref[3, at] + i * STEP
        done = i + 1 >= list_ref[2, at]
        at = at + done.astype(jnp.int32)
        return at, jnp.where(done, list_ref[1, at], i + 1)

    inner_lo = jnp.broadcast_to((lane > 0).astype(F32).astype(BF16), (CH, LANES))
    inner_hi = jnp.broadcast_to((lane < LANES - 1).astype(F32).astype(BF16), (CH, LANES))

    def keep(ref, z, row, h, part, mask):
        for m in range(part.shape[0] // CH):
            ref[z, row + m * CH : row + (m + 1) * CH, h * LANES : (h + 1) * LANES] = jnp.where(mask > 0, part[m * CH : (m + 1) * CH], jnp.zeros((), BF16))

    def blend(i):
        nets = [
            jnp.dot(w3_ref[...], q_ref[4 * e * HID : 4 * (e + 1) * HID, :], preferred_element_type=F32)
            for e in range(STEP // 4)
        ]
        for h in range(2):
            unit = 2 * i + h
            k, local, row = unit_ref[0, unit], unit_ref[1, unit], unit_ref[2, unit]
            q, rem = place_ref[0, k], place_ref[1, k]
            after_q = jnp.where(q == 2, 0, q + 1)
            parts = []
            for f in range(STEP):
                y = nets[f // 4][8 * (f % 4) : 8 * (f % 4) + 8, h * LANES : (h + 1) * LANES]
                parts.append((y + one_row) * wall_ref[k, pl.ds(local + f, 1), :])
            y = pltpu.roll(jnp.concatenate(parts, axis=0), rem, 1)
            at = pl.ds(pl.multiple_of((row + STEP) * 8, 8), 8 * STEP)
            acc_ref[q, at, :] += jnp.where(lane >= rem, y, 0.0)
            acc_ref[after_q, at, :] += jnp.where(lane < rem, y, 0.0)

    def second_conv(z):
        for e in range(STEP // 2):
            v = jnp.dot(w2_ref[...], a_ref[z, 2 * e * 3 * HID : (2 * e + 4) * 3 * HID, :], preferred_element_type=F32)
            v = v + u_ref[z, (2 * e + 1) * HID : (2 * e + 3) * HID, :]
            q_ref[2 * e * HID : (2 * e + 2) * HID, :] = (v + v * jnp.tanh(v)).astype(BF16)

    def first_conv(i, z):
        for e in range(STEP // 2 + 1):
            u = jnp.dot(w1_ref[...], p_ref[z, 2 * e * 3 * CH : (2 * e + 4) * 3 * CH, :], preferred_element_type=F32)
            u_ref[z, 2 * e * HID : (2 * e + 2) * HID, :] = u
            act = u + u * jnp.tanh(u)
            for h in range(2):
                local = unit_ref[1, 2 * i + h]
                for r in range(2):
                    mid = act[r * HID : (r + 1) * HID, h * LANES : (h + 1) * LANES]
                    row = 2 * e + r
                    if row == 0:
                        mid = mid * (local > 0).astype(F32)
                    if row == STEP + 1:
                        mid = mid * (local < SIDE - STEP).astype(F32)
                    mid = mid.astype(BF16)
                    at = row * 3 * HID
                    keep(a_ref, z, at, h, pltpu.roll(mid, 1, 1), inner_lo)
                    a_ref[z, at + HID : at + 2 * HID, h * LANES : (h + 1) * LANES] = mid
                    keep(a_ref, z, at + 2 * HID, h, pltpu.roll(mid, LANES - 1, 1), inner_hi)

    def stage(i, z):
        for h in range(2):
            unit = 2 * i + h
            k, local, row = unit_ref[0, unit], unit_ref[1, unit], unit_ref[2, unit]
            q, rem = place_ref[0, k], place_ref[1, k]
            after_q = jnp.where(q == 2, 0, q + 1)
            turn = (LANES - rem) % LANES
            inner = lane < LANES - rem
            for j in range(STEP + 4):
                at = pl.ds(pl.multiple_of(jnp.clip(row + j, 0, X_ROWS - 1) * CH, CH), CH)
                mid = jnp.where(inner, pltpu.roll(xb_ref[q, at, :], turn, 1), pltpu.roll(xb_ref[after_q, at, :], turn, 1))
                if j < 2:
                    mid = mid * (local > 0).astype(F32).astype(BF16)
                if j >= STEP + 2:
                    mid = mid * (local < SIDE - STEP).astype(F32).astype(BF16)
                keep(p_ref, z, j * 3 * CH, h, pltpu.roll(mid, 1, 1), inner_lo)
                p_ref[z, j * 3 * CH + CH : j * 3 * CH + 2 * CH, h * LANES : (h + 1) * LANES] = mid
                keep(p_ref, z, j * 3 * CH + 2 * CH, h, pltpu.roll(mid, LANES - 1, 1), inner_hi)

    def step(i, carry):
        at, row = carry
        for h in range(4):
            at, row = advance(4 * i + 2 * LAG + h, at, row)
        for z in range(2):
            blend(2 * i + z)
            first_conv(2 * i + z + 2, z)
            second_conv(1 - z)
            stage(2 * i + z + 3, 1 - z)
        return at, row

    lax.fori_loop(0, (count + 3) // 4, step, (jnp.int32(0), list_ref[1, 0]))

    def finish(i, carry):
        for t, part in ((t, part) for part in range(4) for t in range(2)):
            row = pl.multiple_of(i * 32 + part * 8, 8)
            lanes = slice(t * LANES, (t + 1) * LANES)
            total = acc_ref[t + 1, pl.ds((row + STEP) * 8 + OUT, 8, stride=8), :]
            over = 1.0 / (1.0 + total)
            for o in range(OUT):
                state = state_ref[o, pl.ds(row, 8), lanes]
                numer = acc_ref[t + 1, pl.ds((row + STEP) * 8 + o, 8, stride=8), :]
                den = (state * (1.0 + C_SKIP * total) + C_OUT * numer) * over
                den_ref[o, pl.ds(row, 8), lanes] = den
                next_ref[o, pl.ds(row, 8), lanes] = state + (SIGMA_NEXT - SIGMA) * (state - den) / SIGMA
        return carry

    lax.fori_loop(0, BY // 32, finish, 0)


def banded(kernel, times):
    outs, chans = kernel.shape[2], kernel.shape[3]
    flat = (0.5 * jnp.transpose(kernel, (2, 0, 1, 3))).astype(BF16).reshape(outs, 9 * chans)
    step = 3 * chans
    return jnp.concatenate([jnp.pad(flat, ((0, 0), (r * step, (times - 1 - r) * step))) for r in range(times)], axis=0)


def shifted(value, axis, steps):
    count = lax.axis_size(axis)
    first, last = max(0, -steps), min(count, count - steps)
    return lax.ppermute(value, axis, [(i, i + steps) for i in range(first, last)])


def per_device(condition, state, corner_rows, corner_cols, live_counts, blend_weight, conv_in, conv_mid, proj_out):
    smem = pl.BlockSpec(memory_space=pltpu.SMEM)
    vmem = pl.BlockSpec(memory_space=pltpu.VMEM)
    whole_w = pl.BlockSpec((1, 1, SLOTS, SIDE, SIDE), lambda i: (0, 0, 0, 0, 0))
    msg = jax.ShapeDtypeStruct((TILE_MSG, LANES), BF16)
    up, down = pl.pallas_call(
        pack_tile,
        grid=(1,),
        in_specs=[
            smem, smem, smem,
            pl.BlockSpec((CC, 16, BX), lambda i: (0, 0, 0)),
            pl.BlockSpec((CC, 16, BX), lambda i: (0, BY // 16 - 1, 0)),
            pl.BlockSpec((OUT, 8, BX), lambda i: (0, 0, 0)),
            pl.BlockSpec((OUT, 8, BX), lambda i: (0, BY // 8 - 1, 0)),
            whole_w,
        ],
        out_specs=[pl.BlockSpec((TILE_MSG, LANES), lambda i: (0, 0))] * 2,
        out_shape=[msg, msg],
        scratch_shapes=[pltpu.VMEM((4 * CH, LANES), F32)],
        name="pack_tile",
    )(corner_rows, corner_cols, live_counts, condition, condition, state, state, blend_weight)
    above = shifted(down, "tile", 1)
    below = shifted(up, "tile", -1)
    w1 = banded(conv_in, 2)
    w2 = banded(conv_mid, 2)
    rows8 = jnp.pad(proj_out, ((0, 8 - OUT), (0, 0)))
    w3 = jnp.concatenate([jnp.pad(rows8, ((0, 0), (r * HID, (3 - r) * HID))) for r in range(4)], axis=0)
    body, edge = pl.pallas_call(
        prepare,
        in_specs=[vmem] * 2,
        out_specs=[vmem] * 2,
        out_shape=[jax.ShapeDtypeStruct((2, BY * CH, LANES), BF16), jax.ShapeDtypeStruct((16, BY * CH), BF16)],
        name="prepare",
        compiler_params=pltpu.CompilerParams(vmem_limit_bytes=32 << 20),
        cost_estimate=pl.CostEstimate(flops=2 * 4096 * 256 * 256, bytes_accessed=5 << 20, transcendentals=0),
    )(condition, state)
    msg = jax.ShapeDtypeStruct((SUB_MSG, LANES), BF16)
    left, right = pl.pallas_call(
        pack_sub,
        in_specs=[smem] * 3 + [vmem] * 4,
        out_specs=[vmem] * 2,
        out_shape=[msg, msg],
        name="pack_sub",
        compiler_params=pltpu.CompilerParams(vmem_limit_bytes=32 << 20),
    )(corner_rows, corner_cols, live_counts, blend_weight, edge, above, below)
    from_left = shifted(right, "sub", 1)
    from_right = shifted(left, "sub", -1)
    out = jax.ShapeDtypeStruct((OUT, BY, BX), F32)
    return tuple(pl.pallas_call(
        main_kernel,
        in_specs=[smem] * 3 + [pl.BlockSpec(memory_space=pl.ANY)] + [vmem] * 9,
        out_specs=[vmem] * 2,
        out_shape=[out, out],
        scratch_shapes=[
            pltpu.VMEM((3, X_ROWS * CH, LANES), BF16),
            pltpu.VMEM((2, (STEP + 4) * 3 * CH, WIDE), BF16),
            pltpu.VMEM((2, (STEP + 2) * 3 * HID, WIDE), BF16),
            pltpu.VMEM((2, (STEP + 2) * HID, WIDE), F32),
            pltpu.VMEM((STEP * HID, WIDE), BF16),
            pltpu.VMEM((3, ACC_ROWS * 8, LANES), F32),
            pltpu.VMEM((PIECES, SIDE, LANES), F32),
            pltpu.VMEM((80, LANES), jnp.int32),
            pltpu.SMEM((80, LANES), jnp.int32),
            pltpu.SMEM((3, UNITS), jnp.int32),
            pltpu.SMEM((2, PIECES), jnp.int32),
            pltpu.SMEM((4, 2 * LANES), jnp.int32),
            pltpu.SemaphoreType.DMA,
            pltpu.SemaphoreType.DMA,
        ],
        name="patches",
        compiler_params=pltpu.CompilerParams(vmem_limit_bytes=56 << 20),
    )(corner_rows, corner_cols, live_counts, body, state, blend_weight, above, below, from_left, from_right, w1, w2, w3))


def solution(mesh):
    placed = (
        P(None, "tile", "sub"),
        P(None, "tile", "sub"),
        P("tile", "sub", None),
        P("tile", "sub", None),
        P("tile", "sub"),
        P("tile", "sub", None, None, None),
        P(),
        P(),
        P(),
    )
    return jax.shard_map(
        per_device,
        mesh=mesh,
        in_specs=placed,
        out_specs=(P(None, "tile", "sub"), P(None, "tile", "sub")),
        check_vma=False,
    )
```

```python
import jax
import jax.numpy as jnp
from jax import lax
from jax.experimental import pallas as pl
from jax.experimental.pallas import tpu as pltpu
from jax.sharding import PartitionSpec as P

SIGMA = 2.0
SIGMA_NEXT = 1.6
C_IN = 1.0 / (SIGMA * SIGMA + 0.25) ** 0.5
C_SKIP = 0.25 / (SIGMA * SIGMA + 0.25)
C_OUT = 0.5 * SIGMA / (SIGMA * SIGMA + 0.25) ** 0.5

BY = 256
BX = 256
SIDE = 128
HALF = 64
CC = 12
CH = 16
HID = 64
OUT = 4
SLOTS = 2
LANES = 128
WIDE = 2 * LANES
STEP = 8
X_ROWS = BY + 4
ACC_ROWS = BY + 2 * STEP
LAG = 3
UNITS = 512
PIECES = 9 * SLOTS
TILE_MSG = 2 * HALF + 4 * CH + 16
SUB_MSG = SIDE + 2 * HALF + 4 * CH + 64 + 16
F32 = jnp.float32
BF16 = jnp.bfloat16


def iota(shape, dim):
    return lax.broadcasted_iota(jnp.int32, shape, dim)


def scaled(state):
    return (state * C_IN).astype(BF16)


def own_meta(rows_ref, cols_ref, live_ref):
    sub = iota((16, LANES), 0)
    values = (rows_ref[0, 0, 0], rows_ref[0, 0, 1], cols_ref[0, 0, 0], cols_ref[0, 0, 1], live_ref[0, 0])
    tile = jnp.zeros((16, LANES), jnp.int32)
    for k, value in enumerate(values):
        tile = jnp.where(sub == k, value, tile)
    return tile


def pack_tile(rows_ref, cols_ref, live_ref, c_top, c_bot, s_top, s_bot, weight_ref, up_ref, down_ref, tmp):
    meta = own_meta(rows_ref, cols_ref, live_ref).astype(F32).astype(BF16)
    for out, cond, state, low, first_c, first_s in (
        (up_ref, c_top, s_top, 0, 0, 0),
        (down_ref, c_bot, s_bot, HALF, 14, 6),
    ):
        for p in range(SLOTS):
            out[p * HALF : (p + 1) * HALF, :] = weight_ref[0, 0, p, low : low + HALF, :].astype(BF16)
        for c in range(CH):
            if c < CC:
                tile = cond[c].astype(F32)[first_c : first_c + 2, :]
            else:
                tile = scaled(state[c - CC]).astype(F32)[first_s : first_s + 2, :]
            for t in range(2):
                for r in range(2):
                    at = t * 2 * CH + r * CH + c
                    tmp[at : at + 1, :] = tile[r : r + 1, t * LANES : (t + 1) * LANES]
        out[2 * HALF : 2 * HALF + 4 * CH, :] = tmp[...].astype(BF16)
        out[2 * HALF + 4 * CH :, :] = meta


def prepare(cond_ref, state_ref, body_ref, edge_ref, held_ref, sem):
    to = iota((CH * CH, CH * CH), 0)
    of = iota((CH * CH, CH * CH), 1)
    turn = (of == (to % CH) * CH + to // CH).astype(F32).astype(BF16)
    picks = iota((16, LANES), 0)
    spots = iota((16, LANES), 1)
    first = ((picks == spots) & (picks < 2)).astype(F32).astype(BF16)
    last = ((picks == spots - (LANES - 4)) & (picks >= 2)).astype(F32).astype(BF16)

    def group(i, carry):
        for e in range(4):
            start = pl.multiple_of((4 * i + e) * CH, CH)
            rows = pl.ds(start, CH)
            value = jnp.concatenate(
                [cond_ref[:, rows, :].reshape(CC * CH, BX), scaled(state_ref[:, rows, :]).reshape(OUT * CH, BX)], axis=0
            )
            value = jnp.dot(turn, value, preferred_element_type=F32).astype(BF16)
            at = pl.ds(start * CH, CH * CH)
            edge = jnp.zeros((16, CH * CH), F32)
            for t, pick in enumerate((first, last)):
                part = value[:, t * LANES : (t + 1) * LANES]
                held_ref[t, at, :] = part
                edge = edge + lax.dot_general(pick, part, (((1,), (1,)), ((), ())), preferred_element_type=F32)
            edge_ref[:, at] = edge.astype(BF16)
        return carry

    lax.fori_loop(0, BY // CH // 4, group, 0)
    copy = pltpu.make_async_copy(held_ref, body_ref, sem)
    copy.start()
    copy.wait()


def pack_sub(rows_ref, cols_ref, live_ref, weight_ref, edge_ref, above_ref, below_ref, left_ref, right_ref):
    lane = iota((1, LANES), 1)
    meta0 = own_meta(rows_ref, cols_ref, live_ref).astype(F32)
    sub = iota((16, LANES), 0)
    first = 2 * HALF + 4 * CH
    meta_a = pltpu.roll(above_ref[first:, :].astype(F32), 5, 0)
    meta_b = pltpu.roll(below_ref[first:, :].astype(F32), 10, 0)
    meta = jnp.where(sub < 5, meta0, jnp.where(sub < 10, meta_a, meta_b)).astype(BF16)
    for out, side in ((left_ref, 0), (right_ref, 1)):
        def packed(one, two):
            if side == 0:
                return jnp.where(lane < HALF, one, pltpu.roll(two, HALF, 1)).astype(BF16)
            return jnp.where(lane < HALF, pltpu.roll(one, HALF, 1), two).astype(BF16)

        out[0:SIDE, :] = packed(weight_ref[0, 0, 0], weight_ref[0, 0, 1])
        at = SIDE
        for msg in (above_ref, below_ref):
            out[at : at + HALF, :] = packed(msg[0:HALF, :].astype(F32), msg[HALF : 2 * HALF, :].astype(F32))
            at += HALF
        for msg in (above_ref, below_ref):
            begin = 2 * HALF + side * 2 * CH
            out[at : at + 2 * CH, :] = msg[begin : begin + 2 * CH, :]
            at += 2 * CH
        edge = edge_ref[...].astype(F32)
        for m in range(4):
            rows = []
            for e in range(8):
                spot = (8 * m + e) * LANES
                rows.append(edge[2 * side : 2 * side + 2, spot : spot + LANES])
            out[at : at + 16, :] = jnp.concatenate(rows, axis=0).astype(BF16)
            at += 16
        out[at:, :] = meta


def main_kernel(
    rows_ref, cols_ref, live_ref, body_ref, state_ref, weight_ref,
    above_ref, below_ref, left_ref, right_ref, w1_ref, w2_ref, w3_ref,
    den_ref, next_ref,
    xb_ref, p_ref, a_ref, u_ref, q_ref, acc_ref, wall_ref, meta_v, meta_s, unit_ref, place_ref, list_ref, sem, body_sem,
):
    lane = iota((1, LANES), 1)
    first = 2 * HALF + 4 * CH
    meta_v[0:16, :] = own_meta(rows_ref, cols_ref, live_ref)
    meta_v[16:32, :] = above_ref[first:, :].astype(F32).astype(jnp.int32)
    meta_v[32:48, :] = below_ref[first:, :].astype(F32).astype(jnp.int32)
    meta_v[48:64, :] = left_ref[SUB_MSG - 16 :, :].astype(F32).astype(jnp.int32)
    meta_v[64:80, :] = right_ref[SUB_MSG - 16 :, :].astype(F32).astype(jnp.int32)
    copy = pltpu.make_async_copy(meta_v, meta_s, sem)
    copy.start()

    body = pltpu.make_async_copy(body_ref, xb_ref.at[1:3, 2 * CH : (BY + 2) * CH, :], body_sem)
    body.start()
    corner = SIDE + 2 * HALF
    for msg, row, spot in ((above_ref, 0, 0), (below_ref, BY + 2, 2 * CH)):
        for t in range(2):
            xb_ref[t + 1, row * CH : (row + 2) * CH, :] = msg[2 * HALF + t * 2 * CH : 2 * HALF + (t + 1) * 2 * CH, :]
        from_left = left_ref[corner + spot : corner + spot + 2 * CH, :].astype(F32)
        from_right = right_ref[corner + spot : corner + spot + 2 * CH, :].astype(F32)
        xb_ref[0, row * CH : (row + 2) * CH, :] = jnp.where(
            lane < 2, from_right, jnp.where(lane >= LANES - 2, from_left, 0.0)
        ).astype(BF16)
    edge_at = corner + 4 * CH
    picks = iota((32, LANES), 0)
    spots = iota((32, LANES), 1)
    for m in range(4):
        rows = slice(edge_at + 16 * m, edge_at + 16 * m + 16)
        both = jnp.concatenate([left_ref[rows, :].astype(F32), right_ref[rows, :].astype(F32)], axis=0)
        turned = both.T.astype(BF16)
        for e in range(8):
            to_left = (picks - 2 * e == spots - (LANES - 2)) & (spots >= LANES - 2) & (picks < 16)
            to_right = (picks - 16 - 2 * e == spots) & (spots < 2) & (picks >= 16)
            place = (to_left | to_right).astype(F32).astype(BF16)
            at = 2 * CH + (8 * m + e) * LANES
            xb_ref[0, at : at + LANES, :] = jnp.dot(turned, place, preferred_element_type=F32).astype(BF16)
    p_ref[...] = jnp.zeros_like(p_ref)
    a_ref[...] = jnp.zeros_like(a_ref)

    for p in range(SLOTS):
        wall_ref[p, 0:SIDE, :] = weight_ref[0, 0, p]
        wall_ref[2 + p, HALF:SIDE, :] = above_ref[p * HALF : (p + 1) * HALF, :].astype(F32)
        wall_ref[4 + p, 0:HALF, :] = below_ref[p * HALF : (p + 1) * HALF, :].astype(F32)
        for d, msg, turn in ((3, left_ref, p == 0), (6, right_ref, p == 1)):
            def side(lo, hi):
                part = msg[lo:hi, :].astype(F32)
                return pltpu.roll(part, HALF, 1) if turn else part

            wall_ref[2 * d + p, 0:SIDE, :] = side(0, SIDE)
            wall_ref[2 * d + 2 + p, HALF:SIDE, :] = side(SIDE, SIDE + HALF)
            wall_ref[2 * d + 4 + p, 0:HALF, :] = side(SIDE + HALF, SIDE + 2 * HALF)

    def clear(i, carry):
        for t in range(1, 3):
            acc_ref[t, pl.ds(pl.multiple_of(i * 256 + STEP * 8, 64), 256), :] = jnp.zeros((256, LANES), F32)
        return carry

    lax.fori_loop(0, BY * 8 // 256, clear, 0)
    copy.wait()

    one_row = (iota((8, 1), 0) == OUT).astype(F32)

    def nothing(i):
        unit_ref[0, i] = 0
        unit_ref[1, i] = 0
        unit_ref[2, i] = BY

    for i in range(2 * LAG):
        nothing(i)

    total = jnp.int32(0)
    pos = jnp.int32(0)
    for k in range(PIECES):
        d, p = k // 2, k % 2
        across, along = d // 3, d % 3
        base = 16 * along if across == 0 else 32 + 16 * across + 5 * along
        row0 = meta_s[base + p, 0] + (0, -BY, BY)[along] - HALF
        col0 = meta_s[base + 2 + p, 0] + (0, -BX, BX)[across] - HALF
        low = jnp.maximum(-row0, 0) // STEP
        high = (jnp.minimum(SIDE, BY - row0) + STEP - 1) // STEP
        touches = (low < high) & (col0 > -SIDE) & (col0 < BX) & (p < meta_s[base + 4, 0])
        place_ref[0, k] = (col0 + LANES) // LANES
        place_ref[1, k] = (col0 + LANES) % LANES
        list_ref[0, pos] = k
        list_ref[1, pos] = low
        list_ref[2, pos] = high
        list_ref[3, pos] = row0
        pos = pos + touches.astype(jnp.int32)
        total = total + jnp.where(touches, high - low, 0)
    for i in range(4 * LAG + 4):
        list_ref[0, pos + i] = 0
        list_ref[1, pos + i] = 0
        list_ref[2, pos + i] = 1
        list_ref[3, pos + i] = BY
    count = total + 2 * LAG
    body.wait()

    def advance(unit, at, i):
        unit_ref[0, unit] = list_ref[0, at]
        unit_ref[1, unit] = i * STEP
        unit_ref[2, unit] = list_ref[3, at] + i * STEP
        done = i + 1 >= list_ref[2, at]
        at = at + done.astype(jnp.int32)
        return at, jnp.where(done, list_ref[1, at], i + 1)

    inner_lo = jnp.broadcast_to((lane > 0).astype(F32).astype(BF16), (CH, LANES))
    inner_hi = jnp.broadcast_to((lane < LANES - 1).astype(F32).astype(BF16), (CH, LANES))

    def keep(ref, z, row, h, part, mask):
        for m in range(part.shape[0] // CH):
            ref[z, row + m * CH : row + (m + 1) * CH, h * LANES : (h + 1) * LANES] = jnp.where(mask > 0, part[m * CH : (m + 1) * CH], jnp.zeros((), BF16))

    def blend(i):
        nets = [
            jnp.dot(w3_ref[...], q_ref[4 * e * HID : 4 * (e + 1) * HID, :], preferred_element_type=F32)
            for e in range(STEP // 4)
        ]
        for h in range(2):
            unit = 2 * i + h
            k, local, row = unit_ref[0, unit], unit_ref[1, unit], unit_ref[2, unit]
            q, rem = place_ref[0, k], place_ref[1, k]
            after_q = jnp.where(q == 2, 0, q + 1)
            parts = []
            for f in range(STEP):
                y = nets[f // 4][8 * (f % 4) : 8 * (f % 4) + 8, h * LANES : (h + 1) * LANES]
                parts.append((y + one_row) * wall_ref[k, pl.ds(local + f, 1), :])
            y = pltpu.roll(jnp.concatenate(parts, axis=0), rem, 1)
            at = pl.ds(pl.multiple_of((row + STEP) * 8, 8), 8 * STEP)
            acc_ref[q, at, :] += jnp.where(lane >= rem, y, 0.0)
            acc_ref[after_q, at, :] += jnp.where(lane < rem, y, 0.0)

    def second_conv(z):
        for e in range(STEP // 2):
            v = jnp.dot(w2_ref[...], a_ref[z, 2 * e * 3 * HID : (2 * e + 4) * 3 * HID, :], preferred_element_type=F32)
            v = v + u_ref[z, (2 * e + 1) * HID : (2 * e + 3) * HID, :]
            q_ref[2 * e * HID : (2 * e + 2) * HID, :] = (v + v * jnp.tanh(v)).astype(BF16)

    def first_conv(i, z):
        for e in range(STEP // 2 + 1):
            u = jnp.dot(w1_ref[...], p_ref[z, 2 * e * 3 * CH : (2 * e + 4) * 3 * CH, :], preferred_element_type=F32)
            u_ref[z, 2 * e * HID : (2 * e + 2) * HID, :] = u
            act = u + u * jnp.tanh(u)
            for h in range(2):
                local = unit_ref[1, 2 * i + h]
                for r in range(2):
                    mid = act[r * HID : (r + 1) * HID, h * LANES : (h + 1) * LANES]
                    row = 2 * e + r
                    if row == 0:
                        mid = mid * (local > 0).astype(F32)
                    if row == STEP + 1:
                        mid = mid * (local < SIDE - STEP).astype(F32)
                    mid = mid.astype(BF16)
                    at = row * 3 * HID
                    keep(a_ref, z, at, h, pltpu.roll(mid, 1, 1), inner_lo)
                    a_ref[z, at + HID : at + 2 * HID, h * LANES : (h + 1) * LANES] = mid
                    keep(a_ref, z, at + 2 * HID, h, pltpu.roll(mid, LANES - 1, 1), inner_hi)

    def stage(i, z):
        for h in range(2):
            unit = 2 * i + h
            k, local, row = unit_ref[0, unit], unit_ref[1, unit], unit_ref[2, unit]
            q, rem = place_ref[0, k], place_ref[1, k]
            after_q = jnp.where(q == 2, 0, q + 1)
            turn = (LANES - rem) % LANES
            inner = lane < LANES - rem
            for j in range(STEP + 4):
                at = pl.ds(pl.multiple_of(jnp.clip(row + j, 0, X_ROWS - 1) * CH, CH), CH)
                mid = jnp.where(inner, pltpu.roll(xb_ref[q, at, :], turn, 1), pltpu.roll(xb_ref[after_q, at, :], turn, 1))
                if j < 2:
                    mid = mid * (local > 0).astype(F32).astype(BF16)
                if j >= STEP + 2:
                    mid = mid * (local < SIDE - STEP).astype(F32).astype(BF16)
                keep(p_ref, z, j * 3 * CH, h, pltpu.roll(mid, 1, 1), inner_lo)
                p_ref[z, j * 3 * CH + CH : j * 3 * CH + 2 * CH, h * LANES : (h + 1) * LANES] = mid
                keep(p_ref, z, j * 3 * CH + 2 * CH, h, pltpu.roll(mid, LANES - 1, 1), inner_hi)

    def step(i, carry):
        at, row = carry
        for h in range(4):
            at, row = advance(4 * i + 2 * LAG + h, at, row)
        for z in range(2):
            blend(2 * i + z)
            first_conv(2 * i + z + 2, z)
            second_conv(1 - z)
            stage(2 * i + z + 3, 1 - z)
        return at, row

    lax.fori_loop(0, (count + 3) // 4, step, (jnp.int32(0), list_ref[1, 0]))

    def finish(i, carry):
        for t, part in ((t, part) for part in range(4) for t in range(2)):
            row = pl.multiple_of(i * 32 + part * 8, 8)
            lanes = slice(t * LANES, (t + 1) * LANES)
            total = acc_ref[t + 1, pl.ds((row + STEP) * 8 + OUT, 8, stride=8), :]
            over = 1.0 / (1.0 + total)
            for o in range(OUT):
                state = state_ref[o, pl.ds(row, 8), lanes]
                numer = acc_ref[t + 1, pl.ds((row + STEP) * 8 + o, 8, stride=8), :]
                den = (state * (1.0 + C_SKIP * total) + C_OUT * numer) * over
                den_ref[o, pl.ds(row, 8), lanes] = den
                next_ref[o, pl.ds(row, 8), lanes] = state + (SIGMA_NEXT - SIGMA) * (state - den) / SIGMA
        return carry

    lax.fori_loop(0, BY // 32, finish, 0)


def banded(kernel, times):
    outs, chans = kernel.shape[2], kernel.shape[3]
    flat = (0.5 * jnp.transpose(kernel, (2, 0, 1, 3))).astype(BF16).reshape(outs, 9 * chans)
    step = 3 * chans
    return jnp.concatenate([jnp.pad(flat, ((0, 0), (r * step, (times - 1 - r) * step))) for r in range(times)], axis=0)


def shifted(value, axis, steps):
    count = lax.axis_size(axis)
    first, last = max(0, -steps), min(count, count - steps)
    return lax.ppermute(value, axis, [(i, i + steps) for i in range(first, last)])


def per_device(condition, state, corner_rows, corner_cols, live_counts, blend_weight, conv_in, conv_mid, proj_out):
    smem = pl.BlockSpec(memory_space=pltpu.SMEM)
    vmem = pl.BlockSpec(memory_space=pltpu.VMEM)
    whole_w = pl.BlockSpec((1, 1, SLOTS, SIDE, SIDE), lambda i: (0, 0, 0, 0, 0))
    msg = jax.ShapeDtypeStruct((TILE_MSG, LANES), BF16)
    up, down = pl.pallas_call(
        pack_tile,
        grid=(1,),
        in_specs=[
            smem, smem, smem,
            pl.BlockSpec((CC, 16, BX), lambda i: (0, 0, 0)),
            pl.BlockSpec((CC, 16, BX), lambda i: (0, BY // 16 - 1, 0)),
            pl.BlockSpec((OUT, 8, BX), lambda i: (0, 0, 0)),
            pl.BlockSpec((OUT, 8, BX), lambda i: (0, BY // 8 - 1, 0)),
            whole_w,
        ],
        out_specs=[pl.BlockSpec((TILE_MSG, LANES), lambda i: (0, 0))] * 2,
        out_shape=[msg, msg],
        scratch_shapes=[pltpu.VMEM((4 * CH, LANES), F32)],
        name="pack_tile",
    )(corner_rows, corner_cols, live_counts, condition, condition, state, state, blend_weight)
    above = shifted(down, "tile", 1)
    below = shifted(up, "tile", -1)
    w1 = banded(conv_in, 2)
    w2 = banded(conv_mid, 2)
    rows8 = jnp.pad(proj_out, ((0, 8 - OUT), (0, 0)))
    w3 = jnp.concatenate([jnp.pad(rows8, ((0, 0), (r * HID, (3 - r) * HID))) for r in range(4)], axis=0)
    body, edge = pl.pallas_call(
        prepare,
        in_specs=[vmem] * 2,
        out_specs=[pl.BlockSpec(memory_space=pltpu.HBM), vmem],
        scratch_shapes=[pltpu.VMEM((2, BY * CH, LANES), BF16), pltpu.SemaphoreType.DMA],
        out_shape=[jax.ShapeDtypeStruct((2, BY * CH, LANES), BF16), jax.ShapeDtypeStruct((16, BY * CH), BF16)],
        name="prepare",
        compiler_params=pltpu.CompilerParams(vmem_limit_bytes=32 << 20),
        cost_estimate=pl.CostEstimate(flops=2 * 4096 * 256 * 256, bytes_accessed=5 << 20, transcendentals=0),
    )(condition, state)
    msg = jax.ShapeDtypeStruct((SUB_MSG, LANES), BF16)
    left, right = pl.pallas_call(
        pack_sub,
        in_specs=[smem] * 3 + [vmem] * 4,
        out_specs=[vmem] * 2,
        out_shape=[msg, msg],
        name="pack_sub",
        compiler_params=pltpu.CompilerParams(vmem_limit_bytes=32 << 20),
    )(corner_rows, corner_cols, live_counts, blend_weight, edge, above, below)
    from_left = shifted(right, "sub", 1)
    from_right = shifted(left, "sub", -1)
    out = jax.ShapeDtypeStruct((OUT, BY, BX), F32)
    return tuple(pl.pallas_call(
        main_kernel,
        in_specs=[smem] * 3 + [pl.BlockSpec(memory_space=pl.ANY)] + [vmem] * 9,
        out_specs=[vmem] * 2,
        out_shape=[out, out],
        scratch_shapes=[
            pltpu.VMEM((3, X_ROWS * CH, LANES), BF16),
            pltpu.VMEM((2, (STEP + 4) * 3 * CH, WIDE), BF16),
            pltpu.VMEM((2, (STEP + 2) * 3 * HID, WIDE), BF16),
            pltpu.VMEM((2, (STEP + 2) * HID, WIDE), F32),
            pltpu.VMEM((STEP * HID, WIDE), BF16),
            pltpu.VMEM((3, ACC_ROWS * 8, LANES), F32),
            pltpu.VMEM((PIECES, SIDE, LANES), F32),
            pltpu.VMEM((80, LANES), jnp.int32),
            pltpu.SMEM((80, LANES), jnp.int32),
            pltpu.SMEM((3, UNITS), jnp.int32),
            pltpu.SMEM((2, PIECES), jnp.int32),
            pltpu.SMEM((4, 2 * LANES), jnp.int32),
            pltpu.SemaphoreType.DMA,
            pltpu.SemaphoreType.DMA,
        ],
        name="patches",
        compiler_params=pltpu.CompilerParams(vmem_limit_bytes=56 << 20),
    )(corner_rows, corner_cols, live_counts, body, state, blend_weight, above, below, from_left, from_right, w1, w2, w3))


def solution(mesh):
    placed = (
        P(None, "tile", "sub"),
        P(None, "tile", "sub"),
        P("tile", "sub", None),
        P("tile", "sub", None),
        P("tile", "sub"),
        P("tile", "sub", None, None, None),
        P(),
        P(),
        P(),
    )
    return jax.shard_map(
        per_device,
        mesh=mesh,
        in_specs=placed,
        out_specs=(P(None, "tile", "sub"), P(None, "tile", "sub")),
        check_vma=False,
    )
```

```python
import jax
import jax.numpy as jnp
from jax import lax
from jax.experimental import pallas as pl
from jax.experimental.pallas import tpu as pltpu
from jax.sharding import PartitionSpec as P

SIGMA = 2.0
SIGMA_NEXT = 1.6
C_IN = 1.0 / (SIGMA * SIGMA + 0.25) ** 0.5
C_SKIP = 0.25 / (SIGMA * SIGMA + 0.25)
C_OUT = 0.5 * SIGMA / (SIGMA * SIGMA + 0.25) ** 0.5

BY = 256
BX = 256
SIDE = 128
HALF = 64
CC = 12
CH = 16
HID = 64
OUT = 4
SLOTS = 2
LANES = 128
WIDE = 2 * LANES
STEP = 8
X_ROWS = BY + 4
ACC_ROWS = BY + 2 * STEP
LAG = 3
UNITS = 512
PIECES = 9 * SLOTS
TILE_MSG = 2 * HALF + 4 * CH + 16
SUB_MSG = SIDE + 2 * HALF + 4 * CH + 64 + 16
F32 = jnp.float32
BF16 = jnp.bfloat16


def iota(shape, dim):
    return lax.broadcasted_iota(jnp.int32, shape, dim)


def scaled(state):
    return (state * C_IN).astype(BF16)


def own_meta(rows_ref, cols_ref, live_ref):
    sub = iota((16, LANES), 0)
    values = (rows_ref[0, 0, 0], rows_ref[0, 0, 1], cols_ref[0, 0, 0], cols_ref[0, 0, 1], live_ref[0, 0])
    tile = jnp.zeros((16, LANES), jnp.int32)
    for k, value in enumerate(values):
        tile = jnp.where(sub == k, value, tile)
    return tile


def pack_tile(rows_ref, cols_ref, live_ref, c_top, c_bot, s_top, s_bot, weight_ref, up_ref, down_ref, tmp):
    meta = own_meta(rows_ref, cols_ref, live_ref).astype(F32).astype(BF16)
    for out, cond, state, low, first_c, first_s in (
        (up_ref, c_top, s_top, 0, 0, 0),
        (down_ref, c_bot, s_bot, HALF, 14, 6),
    ):
        for p in range(SLOTS):
            out[p * HALF : (p + 1) * HALF, :] = weight_ref[0, 0, p, low : low + HALF, :].astype(BF16)
        for c in range(CH):
            if c < CC:
                tile = cond[c].astype(F32)[first_c : first_c + 2, :]
            else:
                tile = scaled(state[c - CC]).astype(F32)[first_s : first_s + 2, :]
            for t in range(2):
                for r in range(2):
                    at = t * 2 * CH + r * CH + c
                    tmp[at : at + 1, :] = tile[r : r + 1, t * LANES : (t + 1) * LANES]
        out[2 * HALF : 2 * HALF + 4 * CH, :] = tmp[...].astype(BF16)
        out[2 * HALF + 4 * CH :, :] = meta


def prepare(cond_ref, state_ref, body_ref, edge_ref):
    to = iota((CH * CH, CH * CH), 0)
    of = iota((CH * CH, CH * CH), 1)
    turn = (of == (to % CH) * CH + to // CH).astype(F32).astype(BF16)
    picks = iota((16, LANES), 0)
    spots = iota((16, LANES), 1)
    first = ((picks == spots) & (picks < 2)).astype(F32).astype(BF16)
    last = ((picks == spots - (LANES - 4)) & (picks >= 2)).astype(F32).astype(BF16)

    def group(i, carry):
        for e in range(4):
            start = pl.multiple_of((4 * i + e) * CH, CH)
            rows = pl.ds(start, CH)
            value = jnp.concatenate(
                [cond_ref[:, rows, :].reshape(CC * CH, BX), scaled(state_ref[:, rows, :]).reshape(OUT * CH, BX)], axis=0
            )
            value = jnp.dot(turn, value, preferred_element_type=F32).astype(BF16)
            at = pl.ds(start * CH, CH * CH)
            edge = jnp.zeros((16, CH * CH), F32)
            for t, pick in enumerate((first, last)):
                part = value[:, t * LANES : (t + 1) * LANES]
                body_ref[t, at, :] = part
                edge = edge + lax.dot_general(pick, part, (((1,), (1,)), ((), ())), preferred_element_type=F32)
            edge_ref[:, at] = edge.astype(BF16)
        return carry

    lax.fori_loop(0, BY // CH // 4, group, 0)


def pack_sub(rows_ref, cols_ref, live_ref, weight_ref, edge_ref, above_ref, below_ref, left_ref, right_ref):
    lane = iota((1, LANES), 1)
    meta0 = own_meta(rows_ref, cols_ref, live_ref).astype(F32)
    sub = iota((16, LANES), 0)
    first = 2 * HALF + 4 * CH
    meta_a = pltpu.roll(above_ref[first:, :].astype(F32), 5, 0)
    meta_b = pltpu.roll(below_ref[first:, :].astype(F32), 10, 0)
    meta = jnp.where(sub < 5, meta0, jnp.where(sub < 10, meta_a, meta_b)).astype(BF16)
    for out, side in ((left_ref, 0), (right_ref, 1)):
        def packed(one, two):
            if side == 0:
                return jnp.where(lane < HALF, one, pltpu.roll(two, HALF, 1)).astype(BF16)
            return jnp.where(lane < HALF, pltpu.roll(one, HALF, 1), two).astype(BF16)

        out[0:SIDE, :] = packed(weight_ref[0, 0, 0], weight_ref[0, 0, 1])
        at = SIDE
        for msg in (above_ref, below_ref):
            out[at : at + HALF, :] = packed(msg[0:HALF, :].astype(F32), msg[HALF : 2 * HALF, :].astype(F32))
            at += HALF
        for msg in (above_ref, below_ref):
            begin = 2 * HALF + side * 2 * CH
            out[at : at + 2 * CH, :] = msg[begin : begin + 2 * CH, :]
            at += 2 * CH
        edge = edge_ref[...].astype(F32)
        for m in range(4):
            rows = []
            for e in range(8):
                spot = (8 * m + e) * LANES
                rows.append(edge[2 * side : 2 * side + 2, spot : spot + LANES])
            out[at : at + 16, :] = jnp.concatenate(rows, axis=0).astype(BF16)
            at += 16
        out[at:, :] = meta


def main_kernel(
    rows_ref, cols_ref, live_ref, body_ref, state_ref, weight_ref,
    above_ref, below_ref, left_ref, right_ref, w1_ref, w2_ref, w3_ref,
    den_ref, next_ref,
    xb_ref, p_ref, a_ref, u_ref, q_ref, acc_ref, wall_ref, meta_v, meta_s, unit_ref, place_ref, list_ref, sem, body_sem,
):
    lane = iota((1, LANES), 1)
    first = 2 * HALF + 4 * CH
    meta_v[0:16, :] = own_meta(rows_ref, cols_ref, live_ref)
    meta_v[16:32, :] = above_ref[first:, :].astype(F32).astype(jnp.int32)
    meta_v[32:48, :] = below_ref[first:, :].astype(F32).astype(jnp.int32)
    meta_v[48:64, :] = left_ref[SUB_MSG - 16 :, :].astype(F32).astype(jnp.int32)
    meta_v[64:80, :] = right_ref[SUB_MSG - 16 :, :].astype(F32).astype(jnp.int32)
    copy = pltpu.make_async_copy(meta_v, meta_s, sem)
    copy.start()

    body = pltpu.make_async_copy(body_ref, xb_ref.at[1:3, 2 * CH : (BY + 2) * CH, :], body_sem)
    body.start()
    corner = SIDE + 2 * HALF
    for msg, row, spot in ((above_ref, 0, 0), (below_ref, BY + 2, 2 * CH)):
        for t in range(2):
            xb_ref[t + 1, row * CH : (row + 2) * CH, :] = msg[2 * HALF + t * 2 * CH : 2 * HALF + (t + 1) * 2 * CH, :]
        from_left = left_ref[corner + spot : corner + spot + 2 * CH, :].astype(F32)
        from_right = right_ref[corner + spot : corner + spot + 2 * CH, :].astype(F32)
        xb_ref[0, row * CH : (row + 2) * CH, :] = jnp.where(
            lane < 2, from_right, jnp.where(lane >= LANES - 2, from_left, 0.0)
        ).astype(BF16)
    edge_at = corner + 4 * CH
    picks = iota((32, LANES), 0)
    spots = iota((32, LANES), 1)
    for m in range(4):
        rows = slice(edge_at + 16 * m, edge_at + 16 * m + 16)
        both = jnp.concatenate([left_ref[rows, :].astype(F32), right_ref[rows, :].astype(F32)], axis=0)
        turned = both.T.astype(BF16)
        for e in range(8):
            to_left = (picks - 2 * e == spots - (LANES - 2)) & (spots >= LANES - 2) & (picks < 16)
            to_right = (picks - 16 - 2 * e == spots) & (spots < 2) & (picks >= 16)
            place = (to_left | to_right).astype(F32).astype(BF16)
            at = 2 * CH + (8 * m + e) * LANES
            xb_ref[0, at : at + LANES, :] = jnp.dot(turned, place, preferred_element_type=F32).astype(BF16)
    p_ref[...] = jnp.zeros_like(p_ref)
    a_ref[...] = jnp.zeros_like(a_ref)

    for p in range(SLOTS):
        wall_ref[p, 0:SIDE, :] = weight_ref[0, 0, p]
        wall_ref[2 + p, HALF:SIDE, :] = above_ref[p * HALF : (p + 1) * HALF, :].astype(F32)
        wall_ref[4 + p, 0:HALF, :] = below_ref[p * HALF : (p + 1) * HALF, :].astype(F32)
        for d, msg, turn in ((3, left_ref, p == 0), (6, right_ref, p == 1)):
            def side(lo, hi):
                part = msg[lo:hi, :].astype(F32)
                return pltpu.roll(part, HALF, 1) if turn else part

            wall_ref[2 * d + p, 0:SIDE, :] = side(0, SIDE)
            wall_ref[2 * d + 2 + p, HALF:SIDE, :] = side(SIDE, SIDE + HALF)
            wall_ref[2 * d + 4 + p, 0:HALF, :] = side(SIDE + HALF, SIDE + 2 * HALF)

    def clear(i, carry):
        for t in range(1, 3):
            acc_ref[t, pl.ds(pl.multiple_of(i * 256 + STEP * 8, 64), 256), :] = jnp.zeros((256, LANES), F32)
        return carry

    lax.fori_loop(0, BY * 8 // 256, clear, 0)
    copy.wait()

    one_row = (iota((8, 1), 0) == OUT).astype(F32)

    def nothing(i):
        unit_ref[0, i] = 0
        unit_ref[1, i] = 0
        unit_ref[2, i] = BY

    for i in range(2 * LAG):
        nothing(i)

    total = jnp.int32(0)
    pos = jnp.int32(0)
    for k in range(PIECES):
        d, p = k // 2, k % 2
        across, along = d // 3, d % 3
        base = 16 * along if across == 0 else 32 + 16 * across + 5 * along
        row0 = meta_s[base + p, 0] + (0, -BY, BY)[along] - HALF
        col0 = meta_s[base + 2 + p, 0] + (0, -BX, BX)[across] - HALF
        low = jnp.maximum(-row0, 0) // STEP
        high = (jnp.minimum(SIDE, BY - row0) + STEP - 1) // STEP
        touches = (low < high) & (col0 > -SIDE) & (col0 < BX) & (p < meta_s[base + 4, 0])
        place_ref[0, k] = (col0 + LANES) // LANES
        place_ref[1, k] = (col0 + LANES) % LANES
        list_ref[0, pos] = k
        list_ref[1, pos] = low
        list_ref[2, pos] = high
        list_ref[3, pos] = row0
        pos = pos + touches.astype(jnp.int32)
        total = total + jnp.where(touches, high - low, 0)
    for i in range(4 * LAG + 4):
        list_ref[0, pos + i] = 0
        list_ref[1, pos + i] = 0
        list_ref[2, pos + i] = 1
        list_ref[3, pos + i] = BY
    count = total + 2 * LAG
    body.wait()

    def advance(unit, at, i):
        unit_ref[0, unit] = list_ref[0, at]
        unit_ref[1, unit] = i * STEP
        unit_ref[2, unit] = list_ref[3, at] + i * STEP
        done = i + 1 >= list_ref[2, at]
        at = at + done.astype(jnp.int32)
        return at, jnp.where(done, list_ref[1, at], i + 1)

    inner_lo = jnp.broadcast_to((lane > 0).astype(F32).astype(BF16), (CH, LANES))
    inner_hi = jnp.broadcast_to((lane < LANES - 1).astype(F32).astype(BF16), (CH, LANES))

    def keep(ref, z, row, h, part, mask):
        for m in range(part.shape[0] // CH):
            ref[z, row + m * CH : row + (m + 1) * CH, h * LANES : (h + 1) * LANES] = jnp.where(mask > 0, part[m * CH : (m + 1) * CH], jnp.zeros((), BF16))

    def blend(i):
        nets = [
            jnp.dot(w3_ref[...], q_ref[4 * e * HID : 4 * (e + 1) * HID, :], preferred_element_type=F32)
            for e in range(STEP // 4)
        ]
        for h in range(2):
            unit = 2 * i + h
            k, local, row = unit_ref[0, unit], unit_ref[1, unit], unit_ref[2, unit]
            q, rem = place_ref[0, k], place_ref[1, k]
            after_q = jnp.where(q == 2, 0, q + 1)
            parts = []
            for f in range(STEP):
                y = nets[f // 4][8 * (f % 4) : 8 * (f % 4) + 8, h * LANES : (h + 1) * LANES]
                parts.append((y + one_row) * wall_ref[k, pl.ds(local + f, 1), :])
            y = pltpu.roll(jnp.concatenate(parts, axis=0), rem, 1)
            at = pl.ds(pl.multiple_of((row + STEP) * 8, 8), 8 * STEP)
            acc_ref[q, at, :] += jnp.where(lane >= rem, y, 0.0)
            acc_ref[after_q, at, :] += jnp.where(lane < rem, y, 0.0)

    def second_conv(z):
        for e in range(STEP // 2):
            v = jnp.dot(w2_ref[...], a_ref[z, 2 * e * 3 * HID : (2 * e + 4) * 3 * HID, :], preferred_element_type=F32)
            v = v + u_ref[z, (2 * e + 1) * HID : (2 * e + 3) * HID, :]
            q_ref[2 * e * HID : (2 * e + 2) * HID, :] = (v + v * jnp.tanh(v)).astype(BF16)

    def first_conv(i, z):
        for e in range(STEP // 2 + 1):
            u = jnp.dot(w1_ref[...], p_ref[z, 2 * e * 3 * CH : (2 * e + 4) * 3 * CH, :], preferred_element_type=F32)
            u_ref[z, 2 * e * HID : (2 * e + 2) * HID, :] = u
            act = u + u * jnp.tanh(u)
            for h in range(2):
                local = unit_ref[1, 2 * i + h]
                for r in range(2):
                    mid = act[r * HID : (r + 1) * HID, h * LANES : (h + 1) * LANES]
                    row = 2 * e + r
                    if row == 0:
                        mid = mid * (local > 0).astype(F32)
                    if row == STEP + 1:
                        mid = mid * (local < SIDE - STEP).astype(F32)
                    mid = mid.astype(BF16)
                    at = row * 3 * HID
                    keep(a_ref, z, at, h, pltpu.roll(mid, 1, 1), inner_lo)
                    a_ref[z, at + HID : at + 2 * HID, h * LANES : (h + 1) * LANES] = mid
                    keep(a_ref, z, at + 2 * HID, h, pltpu.roll(mid, LANES - 1, 1), inner_hi)

    def stage(i, z):
        for h in range(2):
            unit = 2 * i + h
            k, local, row = unit_ref[0, unit], unit_ref[1, unit], unit_ref[2, unit]
            q, rem = place_ref[0, k], place_ref[1, k]
            after_q = jnp.where(q == 2, 0, q + 1)
            turn = (LANES - rem) % LANES
            inner = lane < LANES - rem
            for j in range(STEP + 4):
                at = pl.ds(pl.multiple_of(jnp.clip(row + j, 0, X_ROWS - 1) * CH, CH), CH)
                mid = jnp.where(inner, pltpu.roll(xb_ref[q, at, :], turn, 1), pltpu.roll(xb_ref[after_q, at, :], turn, 1))
                if j < 2:
                    mid = mid * (local > 0).astype(F32).astype(BF16)
                if j >= STEP + 2:
                    mid = mid * (local < SIDE - STEP).astype(F32).astype(BF16)
                keep(p_ref, z, j * 3 * CH, h, pltpu.roll(mid, 1, 1), inner_lo)
                p_ref[z, j * 3 * CH + CH : j * 3 * CH + 2 * CH, h * LANES : (h + 1) * LANES] = mid
                keep(p_ref, z, j * 3 * CH + 2 * CH, h, pltpu.roll(mid, LANES - 1, 1), inner_hi)

    def step(i, carry):
        at, row = carry
        for h in range(4):
            at, row = advance(4 * i + 2 * LAG + h, at, row)
        for z in range(2):
            blend(2 * i + z)
            first_conv(2 * i + z + 2, z)
            second_conv(1 - z)
            stage(2 * i + z + 3, 1 - z)
        return at, row

    lax.fori_loop(0, (count + 3) // 4, step, (jnp.int32(0), list_ref[1, 0]))

    def finish(i, carry):
        for t, part in ((t, part) for part in range(4) for t in range(2)):
            row = pl.multiple_of(i * 32 + part * 8, 8)
            lanes = slice(t * LANES, (t + 1) * LANES)
            total = acc_ref[t + 1, pl.ds((row + STEP) * 8 + OUT, 8, stride=8), :]
            over = 1.0 / (1.0 + total)
            for o in range(OUT):
                state = state_ref[o, pl.ds(row, 8), lanes]
                numer = acc_ref[t + 1, pl.ds((row + STEP) * 8 + o, 8, stride=8), :]
                den = (state * (1.0 + C_SKIP * total) + C_OUT * numer) * over
                den_ref[o, pl.ds(row, 8), lanes] = den
                next_ref[o, pl.ds(row, 8), lanes] = state + (SIGMA_NEXT - SIGMA) * (state - den) / SIGMA
        return carry

    lax.fori_loop(0, BY // 32, finish, 0)


def banded(kernel, times):
    outs, chans = kernel.shape[2], kernel.shape[3]
    flat = (0.5 * jnp.transpose(kernel, (2, 0, 1, 3))).astype(BF16).reshape(outs, 9 * chans)
    step = 3 * chans
    return jnp.concatenate([jnp.pad(flat, ((0, 0), (r * step, (times - 1 - r) * step))) for r in range(times)], axis=0)


def shifted(value, axis, steps):
    count = lax.axis_size(axis)
    first, last = max(0, -steps), min(count, count - steps)
    return lax.ppermute(value, axis, [(i, i + steps) for i in range(first, last)])


def per_device(condition, state, corner_rows, corner_cols, live_counts, blend_weight, conv_in, conv_mid, proj_out):
    smem = pl.BlockSpec(memory_space=pltpu.SMEM)
    vmem = pl.BlockSpec(memory_space=pltpu.VMEM)
    whole_w = pl.BlockSpec((1, 1, SLOTS, SIDE, SIDE), lambda i: (0, 0, 0, 0, 0))
    msg = jax.ShapeDtypeStruct((TILE_MSG, LANES), BF16)
    up, down = pl.pallas_call(
        pack_tile,
        grid=(1,),
        in_specs=[
            smem, smem, smem,
            pl.BlockSpec((CC, 16, BX), lambda i: (0, 0, 0)),
            pl.BlockSpec((CC, 16, BX), lambda i: (0, BY // 16 - 1, 0)),
            pl.BlockSpec((OUT, 8, BX), lambda i: (0, 0, 0)),
            pl.BlockSpec((OUT, 8, BX), lambda i: (0, BY // 8 - 1, 0)),
            whole_w,
        ],
        out_specs=[pl.BlockSpec((TILE_MSG, LANES), lambda i: (0, 0))] * 2,
        out_shape=[msg, msg],
        scratch_shapes=[pltpu.VMEM((4 * CH, LANES), F32)],
        name="pack_tile",
    )(corner_rows, corner_cols, live_counts, condition, condition, state, state, blend_weight)
    above = shifted(down, "tile", 1)
    below = shifted(up, "tile", -1)
    w1 = banded(conv_in, 2)
    w2 = banded(conv_mid, 2)
    rows8 = jnp.pad(proj_out, ((0, 8 - OUT), (0, 0)))
    w3 = jnp.concatenate([jnp.pad(rows8, ((0, 0), (r * HID, (3 - r) * HID))) for r in range(4)], axis=0)
    body, edge = pl.pallas_call(
        prepare,
        in_specs=[vmem] * 2,
        out_specs=[vmem] * 2,
        out_shape=[jax.ShapeDtypeStruct((2, BY * CH, LANES), BF16), jax.ShapeDtypeStruct((16, BY * CH), BF16)],
        name="prepare",
        compiler_params=pltpu.CompilerParams(vmem_limit_bytes=16 << 20),
        cost_estimate=pl.CostEstimate(flops=2 * 4096 * 256 * 256, bytes_accessed=5 << 20, transcendentals=0),
    )(condition, state)
    msg = jax.ShapeDtypeStruct((SUB_MSG, LANES), BF16)
    left, right = pl.pallas_call(
        pack_sub,
        in_specs=[smem] * 3 + [vmem] * 4,
        out_specs=[vmem] * 2,
        out_shape=[msg, msg],
        name="pack_sub",
        compiler_params=pltpu.CompilerParams(vmem_limit_bytes=16 << 20),
    )(corner_rows, corner_cols, live_counts, blend_weight, edge, above, below)
    from_left = shifted(right, "sub", 1)
    from_right = shifted(left, "sub", -1)
    out = jax.ShapeDtypeStruct((OUT, BY, BX), F32)
    return tuple(pl.pallas_call(
        main_kernel,
        in_specs=[smem] * 3 + [vmem] * 10,
        out_specs=[vmem] * 2,
        out_shape=[out, out],
        scratch_shapes=[
            pltpu.VMEM((3, X_ROWS * CH, LANES), BF16),
            pltpu.VMEM((2, (STEP + 4) * 3 * CH, WIDE), BF16),
            pltpu.VMEM((2, (STEP + 2) * 3 * HID, WIDE), BF16),
            pltpu.VMEM((2, (STEP + 2) * HID, WIDE), F32),
            pltpu.VMEM((STEP * HID, WIDE), BF16),
            pltpu.VMEM((3, ACC_ROWS * 8, LANES), F32),
            pltpu.VMEM((PIECES, SIDE, LANES), F32),
            pltpu.VMEM((80, LANES), jnp.int32),
            pltpu.SMEM((80, LANES), jnp.int32),
            pltpu.SMEM((3, UNITS), jnp.int32),
            pltpu.SMEM((2, PIECES), jnp.int32),
            pltpu.SMEM((4, 2 * LANES), jnp.int32),
            pltpu.SemaphoreType.DMA,
            pltpu.SemaphoreType.DMA,
        ],
        name="patches",
        compiler_params=pltpu.CompilerParams(vmem_limit_bytes=26 << 20),
    )(corner_rows, corner_cols, live_counts, body, state, blend_weight, above, below, from_left, from_right, w1, w2, w3))


def solution(mesh):
    placed = (
        P(None, "tile", "sub"),
        P(None, "tile", "sub"),
        P("tile", "sub", None),
        P("tile", "sub", None),
        P("tile", "sub"),
        P("tile", "sub", None, None, None),
        P(),
        P(),
        P(),
    )
    return jax.shard_map(
        per_device,
        mesh=mesh,
        in_specs=placed,
        out_specs=(P(None, "tile", "sub"), P(None, "tile", "sub")),
        check_vma=False,
    )
```

```python
import jax
import jax.numpy as jnp
from jax import lax
from jax.experimental import pallas as pl
from jax.experimental.pallas import tpu as pltpu
from jax.sharding import PartitionSpec as P

SIGMA = 2.0
SIGMA_NEXT = 1.6
C_IN = 1.0 / (SIGMA * SIGMA + 0.25) ** 0.5
C_SKIP = 0.25 / (SIGMA * SIGMA + 0.25)
C_OUT = 0.5 * SIGMA / (SIGMA * SIGMA + 0.25) ** 0.5

BY = 256
BX = 256
SIDE = 128
HALF = 64
CC = 12
CH = 16
HID = 64
OUT = 4
SLOTS = 2
LANES = 128
WIDE = 2 * LANES
STEP = 8
X_TOP = 10
X_ROWS = BY + 24
ACC_ROWS = BY + 2 * STEP
LAG = 3
UNITS = 768
PIECES = 9 * SLOTS
TILE_MSG = 2 * HALF + 4 * CH + 16
SUB_MSG = SIDE + 2 * HALF + 4 * CH + 64 + 16
F32 = jnp.float32
BF16 = jnp.bfloat16


def iota(shape, dim):
    return lax.broadcasted_iota(jnp.int32, shape, dim)


def scaled(state):
    return (state * C_IN).astype(BF16)


def own_meta(rows_ref, cols_ref, live_ref):
    sub = iota((16, LANES), 0)
    values = (rows_ref[0, 0, 0], rows_ref[0, 0, 1], cols_ref[0, 0, 0], cols_ref[0, 0, 1], live_ref[0, 0])
    tile = jnp.zeros((16, LANES), jnp.int32)
    for k, value in enumerate(values):
        tile = jnp.where(sub == k, value, tile)
    return tile


def pack_tile(rows_ref, cols_ref, live_ref, c_top, c_bot, s_top, s_bot, weight_ref, up_ref, down_ref, tmp):
    meta = own_meta(rows_ref, cols_ref, live_ref).astype(F32).astype(BF16)
    for out, cond, state, low, first_c, first_s in (
        (up_ref, c_top, s_top, 0, 0, 0),
        (down_ref, c_bot, s_bot, HALF, 14, 6),
    ):
        for p in range(SLOTS):
            out[p * HALF : (p + 1) * HALF, :] = weight_ref[0, 0, p, low : low + HALF, :].astype(BF16)
        for c in range(CH):
            if c < CC:
                tile = cond[c].astype(F32)[first_c : first_c + 2, :]
            else:
                tile = scaled(state[c - CC]).astype(F32)[first_s : first_s + 2, :]
            for t in range(2):
                for r in range(2):
                    at = t * 2 * CH + r * CH + c
                    tmp[at : at + 1, :] = tile[r : r + 1, t * LANES : (t + 1) * LANES]
        out[2 * HALF : 2 * HALF + 4 * CH, :] = tmp[...].astype(BF16)
        out[2 * HALF + 4 * CH :, :] = meta


def prepare(cond_ref, state_ref, body_ref, edge_ref):
    to = iota((CH * CH, CH * CH), 0)
    of = iota((CH * CH, CH * CH), 1)
    turn = (of == (to % CH) * CH + to // CH).astype(F32).astype(BF16)
    picks = iota((16, LANES), 0)
    spots = iota((16, LANES), 1)
    first = ((picks == spots) & (picks < 2)).astype(F32).astype(BF16)
    last = ((picks == spots - (LANES - 4)) & (picks >= 2)).astype(F32).astype(BF16)

    def group(i, carry):
        for e in range(4):
            start = pl.multiple_of((4 * i + e) * CH, CH)
            rows = pl.ds(start, CH)
            value = jnp.concatenate(
                [cond_ref[:, rows, :].reshape(CC * CH, BX), scaled(state_ref[:, rows, :]).reshape(OUT * CH, BX)], axis=0
            )
            value = jnp.dot(turn, value, preferred_element_type=F32).astype(BF16)
            at = pl.ds(start * CH, CH * CH)
            edge = jnp.zeros((16, CH * CH), F32)
            for t, pick in enumerate((first, last)):
                part = value[:, t * LANES : (t + 1) * LANES]
                body_ref[t, at, :] = part
                edge = edge + lax.dot_general(pick, part, (((1,), (1,)), ((), ())), preferred_element_type=F32)
            edge_ref[:, at] = edge.astype(BF16)
        return carry

    lax.fori_loop(0, BY // CH // 4, group, 0)


def pack_sub(rows_ref, cols_ref, live_ref, weight_ref, edge_ref, above_ref, below_ref, left_ref, right_ref):
    lane = iota((1, LANES), 1)
    meta0 = own_meta(rows_ref, cols_ref, live_ref).astype(F32)
    sub = iota((16, LANES), 0)
    first = 2 * HALF + 4 * CH
    meta_a = pltpu.roll(above_ref[first:, :].astype(F32), 5, 0)
    meta_b = pltpu.roll(below_ref[first:, :].astype(F32), 10, 0)
    meta = jnp.where(sub < 5, meta0, jnp.where(sub < 10, meta_a, meta_b)).astype(BF16)
    for out, side in ((left_ref, 0), (right_ref, 1)):
        def packed(one, two):
            if side == 0:
                return jnp.where(lane < HALF, one, pltpu.roll(two, HALF, 1)).astype(BF16)
            return jnp.where(lane < HALF, pltpu.roll(one, HALF, 1), two).astype(BF16)

        out[0:SIDE, :] = packed(weight_ref[0, 0, 0], weight_ref[0, 0, 1])
        at = SIDE
        for msg in (above_ref, below_ref):
            out[at : at + HALF, :] = packed(msg[0:HALF, :].astype(F32), msg[HALF : 2 * HALF, :].astype(F32))
            at += HALF
        for msg in (above_ref, below_ref):
            begin = 2 * HALF + side * 2 * CH
            out[at : at + 2 * CH, :] = msg[begin : begin + 2 * CH, :]
            at += 2 * CH
        edge = edge_ref[...].astype(F32)
        for m in range(4):
            rows = []
            for e in range(8):
                spot = (8 * m + e) * LANES
                rows.append(edge[2 * side : 2 * side + 2, spot : spot + LANES])
            out[at : at + 16, :] = jnp.concatenate(rows, axis=0).astype(BF16)
            at += 16
        out[at:, :] = meta


def main_kernel(
    rows_ref, cols_ref, live_ref, body_ref, state_ref, weight_ref,
    above_ref, below_ref, left_ref, right_ref, w1_ref, w2_ref, w3_ref,
    den_ref, next_ref,
    xb_ref, p_ref, a_ref, u_ref, q_ref, acc_ref, wall_ref, meta_v, meta_s, unit_ref, place_ref, list_ref, sem, body_sem,
):
    lane = iota((1, LANES), 1)
    first = 2 * HALF + 4 * CH
    meta_v[0:16, :] = own_meta(rows_ref, cols_ref, live_ref)
    meta_v[16:32, :] = above_ref[first:, :].astype(F32).astype(jnp.int32)
    meta_v[32:48, :] = below_ref[first:, :].astype(F32).astype(jnp.int32)
    meta_v[48:64, :] = left_ref[SUB_MSG - 16 :, :].astype(F32).astype(jnp.int32)
    meta_v[64:80, :] = right_ref[SUB_MSG - 16 :, :].astype(F32).astype(jnp.int32)
    copy = pltpu.make_async_copy(meta_v, meta_s, sem)
    copy.start()

    body = pltpu.make_async_copy(body_ref, xb_ref.at[1:3, X_TOP * CH : (BY + X_TOP) * CH, :], body_sem)
    body.start()
    corner = SIDE + 2 * HALF
    for msg, row, spot in ((above_ref, X_TOP - 2, 0), (below_ref, BY + X_TOP, 2 * CH)):
        for t in range(2):
            xb_ref[t + 1, row * CH : (row + 2) * CH, :] = msg[2 * HALF + t * 2 * CH : 2 * HALF + (t + 1) * 2 * CH, :]
        from_left = left_ref[corner + spot : corner + spot + 2 * CH, :].astype(F32)
        from_right = right_ref[corner + spot : corner + spot + 2 * CH, :].astype(F32)
        xb_ref[0, row * CH : (row + 2) * CH, :] = jnp.where(
            lane < 2, from_right, jnp.where(lane >= LANES - 2, from_left, 0.0)
        ).astype(BF16)
    edge_at = corner + 4 * CH
    picks = iota((32, LANES), 0)
    spots = iota((32, LANES), 1)
    for m in range(4):
        rows = slice(edge_at + 16 * m, edge_at + 16 * m + 16)
        both = jnp.concatenate([left_ref[rows, :].astype(F32), right_ref[rows, :].astype(F32)], axis=0)
        turned = both.T.astype(BF16)
        for e in range(8):
            to_left = (picks - 2 * e == spots - (LANES - 2)) & (spots >= LANES - 2) & (picks < 16)
            to_right = (picks - 16 - 2 * e == spots) & (spots < 2) & (picks >= 16)
            place = (to_left | to_right).astype(F32).astype(BF16)
            at = X_TOP * CH + (8 * m + e) * LANES
            xb_ref[0, at : at + LANES, :] = jnp.dot(turned, place, preferred_element_type=F32).astype(BF16)
    for t in range(3):
        xb_ref[t, 0 : (X_TOP - 2) * CH, :] = jnp.zeros(((X_TOP - 2) * CH, LANES), BF16)
        low = (BY + X_TOP + 2) * CH
        xb_ref[t, low:, :] = jnp.zeros((X_ROWS * CH - low, LANES), BF16)
    p_ref[...] = jnp.zeros_like(p_ref)
    a_ref[...] = jnp.zeros_like(a_ref)

    for p in range(SLOTS):
        wall_ref[p, 0:SIDE, :] = weight_ref[0, 0, p]
        wall_ref[2 + p, HALF:SIDE, :] = above_ref[p * HALF : (p + 1) * HALF, :].astype(F32)
        wall_ref[4 + p, 0:HALF, :] = below_ref[p * HALF : (p + 1) * HALF, :].astype(F32)
        for d, msg in ((3, left_ref), (6, right_ref)):
            def side(lo, hi):
                part = msg[lo:hi, :].astype(F32)
                return jnp.where((lane < HALF) == (p == 0), part, pltpu.roll(part, HALF, 1))

            wall_ref[2 * d + p, 0:SIDE, :] = side(0, SIDE)
            wall_ref[2 * d + 2 + p, HALF:SIDE, :] = side(SIDE, SIDE + HALF)
            wall_ref[2 * d + 4 + p, 0:HALF, :] = side(SIDE + HALF, SIDE + 2 * HALF)

    def clear(i, carry):
        for t in range(1, 3):
            acc_ref[t, pl.ds(pl.multiple_of(i * 256 + STEP * 8, 64), 256), :] = jnp.zeros((256, LANES), F32)
        return carry

    lax.fori_loop(0, BY * 8 // 256, clear, 0)
    copy.wait()

    one_row = (iota((8, 1), 0) == OUT).astype(F32)

    def nothing(i):
        unit_ref[0, i] = 0
        unit_ref[1, i] = 0
        unit_ref[2, i] = BY
        unit_ref[3, i] = 0

    for i in range(4 * LAG):
        nothing(i)

    pos = jnp.int32(0)
    totals = []
    pieces = []
    for k in range(PIECES):
        d, p = k // 2, k % 2
        across, along = d // 3, d % 3
        base = 16 * along if across == 0 else 32 + 16 * across + 5 * along
        row0 = meta_s[base + p, 0] + (0, -BY, BY)[along] - HALF
        col0 = meta_s[base + 2 + p, 0] + (0, -BX, BX)[across] - HALF
        low = jnp.maximum(-row0, 0) // STEP
        high = (jnp.minimum(SIDE, BY - row0) + STEP - 1) // STEP
        touches = (low < high) & (col0 > -SIDE) & (col0 < BX) & (p < meta_s[base + 4, 0])
        spot = col0 + LANES
        q, rem = spot // LANES, spot % LANES
        after_q = jnp.where(q == 2, 0, q + 1)
        whole = ((q, rem, q, rem, LANES), (after_q, rem, after_q, 0, rem))
        bound = LANES - rem
        if across == 0:
            narrow = jnp.bool_(False)
        else:
            if across == 1:
                narrow = spot <= HALF - 2
                ours = [(3, (spot + HALF * (1 - g)) % LANES, 1, 0, spot) for g in range(2)]
            else:
                narrow = col0 >= BX - (HALF - 2)
                ours = [(4, (spot + HALF * g) % LANES, 2, col0 - LANES, LANES) for g in range(2)]
            whole = [[jnp.where(narrow, x, y) for x, y in zip(mine, all_)] for mine, all_ in zip(ours, whole)]
            bound = jnp.where(narrow, HALF, bound)
        for g in range(2):
            for f in range(5):
                place_ref[5 * g + f, k] = whole[g][f]
        place_ref[10, k] = bound
        pieces.append((k, low, high, row0, touches, narrow))
    for half in range(2):
        total = jnp.int32(0)
        for k, low, high, row0, touches, narrow in pieces:
            if half == 1 and k < 6:
                continue
            ours = touches & (narrow if half == 1 else jnp.logical_not(narrow))
            list_ref[0, pos] = k
            list_ref[1, pos] = low
            list_ref[2, pos] = high
            list_ref[3, pos] = row0
            list_ref[4, pos] = half
            pos = pos + ours.astype(jnp.int32)
            total = total + jnp.where(ours, high - low, 0)
        totals.append(total)
    for i in range(8 * LAG + 16):
        list_ref[0, pos + i] = 0
        list_ref[1, pos + i] = 0
        list_ref[2, pos + i] = 1
        list_ref[3, pos + i] = BY
        list_ref[4, pos + i] = 1
    count = totals[0] + (totals[1] + 1) // 2 + 2 * LAG
    body.wait()

    def edges(i, carry):
        at = pl.ds(pl.multiple_of(i * (X_ROWS * CH // 5), CH), X_ROWS * CH // 5)
        outer = xb_ref[0, at, :]
        xb_ref[3, at, :] = jnp.where(lane < HALF, xb_ref[1, at, :], outer)
        xb_ref[4, at, :] = jnp.where(lane < HALF, outer, xb_ref[2, at, :])
        return carry

    lax.fori_loop(0, 5, edges, 0)

    def advance(unit, g, at, i):
        half = list_ref[4, at]
        unit_ref[0, unit] = list_ref[0, at]
        unit_ref[1, unit] = i * STEP
        unit_ref[2, unit] = list_ref[3, at] + i * STEP
        unit_ref[3, unit] = half
        ahead = i + (half if g == 0 else 1)
        done = ahead >= list_ref[2, at]
        at = at + done.astype(jnp.int32)
        return at, jnp.where(done, list_ref[1, at], ahead)

    first_half = lane < HALF

    def by_half(values):
        return jnp.where(first_half, values[0].astype(F32), values[1].astype(F32))

    def borders(split):
        lo = jnp.where((lane == 0) | ((lane == HALF) & (split > 0)), 0.0, 1.0)
        hi = jnp.where((lane == LANES - 1) | ((lane == HALF - 1) & (split > 0)), 0.0, 1.0)
        return [jnp.broadcast_to(part, (CH, LANES)).astype(BF16) for part in (lo, hi)]

    def keep(ref, z, row, h, part, mask):
        for m in range(part.shape[0] // CH):
            ref[z, row + m * CH : row + (m + 1) * CH, h * LANES : (h + 1) * LANES] = jnp.where(mask > 0, part[m * CH : (m + 1) * CH], jnp.zeros((), BF16))

    def blend(i):
        nets = [
            jnp.dot(w3_ref[...], q_ref[4 * e * HID : 4 * (e + 1) * HID, :], preferred_element_type=F32)
            for e in range(STEP // 4)
        ]
        for h in range(2):
            units = [4 * i + 2 * h + g for g in range(2)]
            ks = [unit_ref[0, unit] for unit in units]
            locals_ = [unit_ref[1, unit] for unit in units]
            parts = []
            for f in range(STEP):
                y = nets[f // 4][8 * (f % 4) : 8 * (f % 4) + 8, h * LANES : (h + 1) * LANES]
                one, two = [wall_ref[k, pl.ds(local + f, 1), :] for k, local in zip(ks, locals_)]
                parts.append((y + one_row) * jnp.where(first_half, one, two))
            value = jnp.concatenate(parts, axis=0)
            for g in range(2):
                turn, tile, lo, hi = [place_ref[5 * g + f, ks[g]] for f in range(1, 5)]
                y = pltpu.roll(value, turn, 1)
                at = pl.ds(pl.multiple_of((unit_ref[2, units[g]] + STEP) * 8, 8), 8 * STEP)
                acc_ref[tile, at, :] += jnp.where((lane >= lo) & (lane < hi), y, 0.0)

    def second_conv(z):
        for e in range(STEP // 2):
            v = jnp.dot(w2_ref[...], a_ref[z, 2 * e * 3 * HID : (2 * e + 4) * 3 * HID, :], preferred_element_type=F32)
            v = v + u_ref[z, (2 * e + 1) * HID : (2 * e + 3) * HID, :]
            q_ref[2 * e * HID : (2 * e + 2) * HID, :] = (v + v * jnp.tanh(v)).astype(BF16)

    def first_conv(i, z):
        for e in range(STEP // 2 + 1):
            u = jnp.dot(w1_ref[...], p_ref[z, 2 * e * 3 * CH : (2 * e + 4) * 3 * CH, :], preferred_element_type=F32)
            u_ref[z, 2 * e * HID : (2 * e + 2) * HID, :] = u
            act = u + u * jnp.tanh(u)
            for h in range(2):
                units = [4 * i + 2 * h + g for g in range(2)]
                locals_ = [unit_ref[1, unit] for unit in units]
                inner_lo, inner_hi = borders(unit_ref[3, units[0]])
                for r in range(2):
                    mid = act[r * HID : (r + 1) * HID, h * LANES : (h + 1) * LANES]
                    row = 2 * e + r
                    if row == 0:
                        mid = mid * by_half([local > 0 for local in locals_])
                    if row == STEP + 1:
                        mid = mid * by_half([local < SIDE - STEP for local in locals_])
                    mid = mid.astype(BF16)
                    at = row * 3 * HID
                    keep(a_ref, z, at, h, pltpu.roll(mid, 1, 1), inner_lo)
                    a_ref[z, at + HID : at + 2 * HID, h * LANES : (h + 1) * LANES] = mid
                    keep(a_ref, z, at + 2 * HID, h, pltpu.roll(mid, LANES - 1, 1), inner_hi)

    def stage(i, z):
        for h in range(2):
            units = [4 * i + 2 * h + g for g in range(2)]
            locals_ = [unit_ref[1, unit] for unit in units]
            inner_lo, inner_hi = borders(unit_ref[3, units[0]])
            ks = [unit_ref[0, unit] for unit in units]
            tiles = [place_ref[5 * g, ks[g]] for g in range(2)]
            turns = [(LANES - place_ref[5 * g + 1, ks[g]]) % LANES for g in range(2)]
            rows = [unit_ref[2, unit] for unit in units]
            low_part = lane < place_ref[10, ks[0]]
            both = []
            for tile, turn, row in zip(tiles, turns, rows):
                at = pl.ds(pl.multiple_of((row + X_TOP - 2) * CH, CH), (STEP + 4) * CH)
                both.append(pltpu.roll(xb_ref[tile, at, :], turn, 1))
            value = jnp.where(low_part, both[0], both[1])
            for j in range(STEP + 4):
                mid = value[j * CH : (j + 1) * CH]
                if j < 2:
                    mid = mid * by_half([local > 0 for local in locals_]).astype(BF16)
                if j >= STEP + 2:
                    mid = mid * by_half([local < SIDE - STEP for local in locals_]).astype(BF16)
                keep(p_ref, z, j * 3 * CH, h, pltpu.roll(mid, 1, 1), inner_lo)
                p_ref[z, j * 3 * CH + CH : j * 3 * CH + 2 * CH, h * LANES : (h + 1) * LANES] = mid
                keep(p_ref, z, j * 3 * CH + 2 * CH, h, pltpu.roll(mid, LANES - 1, 1), inner_hi)

    def step(i, carry):
        at, row = carry
        for z in range(2):
            blend(2 * i + z)
            first_conv(2 * i + z + 2, z)
            second_conv(1 - z)
            stage(2 * i + z + 3, 1 - z)
        return more(i + 1, at, row)

    def more(i, at, row):
        for h in range(8):
            at, row = advance(8 * i + 4 * LAG + h, h % 2, at, row)
        return at, row

    lax.fori_loop(0, (count + 3) // 4, step, more(0, jnp.int32(0), list_ref[1, 0]))

    def finish(i, carry):
        for t, part in ((t, part) for part in range(4) for t in range(2)):
            row = pl.multiple_of(i * 32 + part * 8, 8)
            lanes = slice(t * LANES, (t + 1) * LANES)
            total = acc_ref[t + 1, pl.ds((row + STEP) * 8 + OUT, 8, stride=8), :]
            over = 1.0 / (1.0 + total)
            for o in range(OUT):
                state = state_ref[o, pl.ds(row, 8), lanes]
                numer = acc_ref[t + 1, pl.ds((row + STEP) * 8 + o, 8, stride=8), :]
                den = (state * (1.0 + C_SKIP * total) + C_OUT * numer) * over
                den_ref[o, pl.ds(row, 8), lanes] = den
                next_ref[o, pl.ds(row, 8), lanes] = state + (SIGMA_NEXT - SIGMA) * (state - den) / SIGMA
        return carry

    lax.fori_loop(0, BY // 32, finish, 0)


def banded(kernel, times):
    outs, chans = kernel.shape[2], kernel.shape[3]
    flat = (0.5 * jnp.transpose(kernel, (2, 0, 1, 3))).astype(BF16).reshape(outs, 9 * chans)
    step = 3 * chans
    return jnp.concatenate([jnp.pad(flat, ((0, 0), (r * step, (times - 1 - r) * step))) for r in range(times)], axis=0)


def shifted(value, axis, steps):
    count = lax.axis_size(axis)
    first, last = max(0, -steps), min(count, count - steps)
    return lax.ppermute(value, axis, [(i, i + steps) for i in range(first, last)])


def per_device(condition, state, corner_rows, corner_cols, live_counts, blend_weight, conv_in, conv_mid, proj_out):
    smem = pl.BlockSpec(memory_space=pltpu.SMEM)
    vmem = pl.BlockSpec(memory_space=pltpu.VMEM)
    whole_w = pl.BlockSpec((1, 1, SLOTS, SIDE, SIDE), lambda i: (0, 0, 0, 0, 0))
    msg = jax.ShapeDtypeStruct((TILE_MSG, LANES), BF16)
    up, down = pl.pallas_call(
        pack_tile,
        grid=(1,),
        in_specs=[
            smem, smem, smem,
            pl.BlockSpec((CC, 16, BX), lambda i: (0, 0, 0)),
            pl.BlockSpec((CC, 16, BX), lambda i: (0, BY // 16 - 1, 0)),
            pl.BlockSpec((OUT, 8, BX), lambda i: (0, 0, 0)),
            pl.BlockSpec((OUT, 8, BX), lambda i: (0, BY // 8 - 1, 0)),
            whole_w,
        ],
        out_specs=[pl.BlockSpec((TILE_MSG, LANES), lambda i: (0, 0))] * 2,
        out_shape=[msg, msg],
        scratch_shapes=[pltpu.VMEM((4 * CH, LANES), F32)],
        name="pack_tile",
    )(corner_rows, corner_cols, live_counts, condition, condition, state, state, blend_weight)
    above = shifted(down, "tile", 1)
    below = shifted(up, "tile", -1)
    w1 = banded(conv_in, 2)
    w2 = banded(conv_mid, 2)
    rows8 = jnp.pad(proj_out, ((0, 8 - OUT), (0, 0)))
    w3 = jnp.concatenate([jnp.pad(rows8, ((0, 0), (r * HID, (3 - r) * HID))) for r in range(4)], axis=0)
    body, edge = pl.pallas_call(
        prepare,
        in_specs=[vmem] * 2,
        out_specs=[vmem] * 2,
        out_shape=[jax.ShapeDtypeStruct((2, BY * CH, LANES), BF16), jax.ShapeDtypeStruct((16, BY * CH), BF16)],
        name="prepare",
        compiler_params=pltpu.CompilerParams(vmem_limit_bytes=16 << 20),
        cost_estimate=pl.CostEstimate(flops=2 * 4096 * 256 * 256, bytes_accessed=5 << 20, transcendentals=0),
    )(condition, state)
    msg = jax.ShapeDtypeStruct((SUB_MSG, LANES), BF16)
    left, right = pl.pallas_call(
        pack_sub,
        in_specs=[smem] * 3 + [vmem] * 4,
        out_specs=[vmem] * 2,
        out_shape=[msg, msg],
        name="pack_sub",
        compiler_params=pltpu.CompilerParams(vmem_limit_bytes=16 << 20),
    )(corner_rows, corner_cols, live_counts, blend_weight, edge, above, below)
    from_left = shifted(right, "sub", 1)
    from_right = shifted(left, "sub", -1)
    out = jax.ShapeDtypeStruct((OUT, BY, BX), F32)
    return tuple(pl.pallas_call(
        main_kernel,
        in_specs=[smem] * 3 + [vmem] * 10,
        out_specs=[vmem] * 2,
        out_shape=[out, out],
        scratch_shapes=[
            pltpu.VMEM((5, X_ROWS * CH, LANES), BF16),
            pltpu.VMEM((2, (STEP + 4) * 3 * CH, WIDE), BF16),
            pltpu.VMEM((2, (STEP + 2) * 3 * HID, WIDE), BF16),
            pltpu.VMEM((2, (STEP + 2) * HID, WIDE), F32),
            pltpu.VMEM((STEP * HID, WIDE), BF16),
            pltpu.VMEM((3, ACC_ROWS * 8, LANES), F32),
            pltpu.VMEM((PIECES, SIDE, LANES), F32),
            pltpu.VMEM((80, LANES), jnp.int32),
            pltpu.SMEM((80, LANES), jnp.int32),
            pltpu.SMEM((4, UNITS), jnp.int32),
            pltpu.SMEM((11, PIECES), jnp.int32),
            pltpu.SMEM((5, LANES), jnp.int32),
            pltpu.SemaphoreType.DMA,
            pltpu.SemaphoreType.DMA,
        ],
        name="patches",
        compiler_params=pltpu.CompilerParams(vmem_limit_bytes=26 << 20),
    )(corner_rows, corner_cols, live_counts, body, state, blend_weight, above, below, from_left, from_right, w1, w2, w3))


def solution(mesh):
    placed = (
        P(None, "tile", "sub"),
        P(None, "tile", "sub"),
        P("tile", "sub", None),
        P("tile", "sub", None),
        P("tile", "sub"),
        P("tile", "sub", None, None, None),
        P(),
        P(),
        P(),
    )
    return jax.shard_map(
        per_device,
        mesh=mesh,
        in_specs=placed,
        out_specs=(P(None, "tile", "sub"), P(None, "tile", "sub")),
        check_vma=False,
    )
```

```python
import jax
import jax.numpy as jnp
from jax import lax
from jax.experimental import pallas as pl
from jax.experimental.pallas import tpu as pltpu
from jax.sharding import PartitionSpec as P

SIGMA = 2.0
SIGMA_NEXT = 1.6
C_IN = 1.0 / (SIGMA * SIGMA + 0.25) ** 0.5
C_SKIP = 0.25 / (SIGMA * SIGMA + 0.25)
C_OUT = 0.5 * SIGMA / (SIGMA * SIGMA + 0.25) ** 0.5

BY = 256
BX = 256
SIDE = 128
HALF = 64
CC = 12
CH = 16
HID = 64
OUT = 4
SLOTS = 2
LANES = 128
WIDE = 2 * LANES
STEP = 8
X_TOP = 10
X_ROWS = BY + 24
ACC_ROWS = BY + 2 * STEP
LAG = 3
UNITS = 768
PIECES = 9 * SLOTS
TILE_MSG = 2 * HALF + 4 * CH + 16
SUB_MSG = SIDE + 2 * HALF + 4 * CH + 64 + 16
F32 = jnp.float32
BF16 = jnp.bfloat16


def iota(shape, dim):
    return lax.broadcasted_iota(jnp.int32, shape, dim)


def scaled(state):
    return (state * C_IN).astype(BF16)


def own_meta(rows_ref, cols_ref, live_ref):
    sub = iota((16, LANES), 0)
    values = (rows_ref[0, 0, 0], rows_ref[0, 0, 1], cols_ref[0, 0, 0], cols_ref[0, 0, 1], live_ref[0, 0])
    tile = jnp.zeros((16, LANES), jnp.int32)
    for k, value in enumerate(values):
        tile = jnp.where(sub == k, value, tile)
    return tile


def pack_tile(rows_ref, cols_ref, live_ref, c_top, c_bot, s_top, s_bot, weight_ref, up_ref, down_ref):
    meta = own_meta(rows_ref, cols_ref, live_ref).astype(F32).astype(BF16)
    to = iota((2 * CH, CH * CH), 0)
    of = iota((2 * CH, CH * CH), 1)
    for out, cond, state, low, first in ((up_ref, c_top, s_top, 0, 0), (down_ref, c_bot, s_bot, HALF, CH - 2)):
        for p in range(SLOTS):
            out[p * HALF : (p + 1) * HALF, :] = weight_ref[0, 0, p, low : low + HALF, :].astype(BF16)
        pick = (of == (to % CH) * CH + to // CH + first).astype(F32).astype(BF16)
        value = jnp.concatenate([cond[...].reshape(CC * CH, BX), scaled(state[...]).reshape(OUT * CH, BX)], axis=0)
        value = jnp.dot(pick, value, preferred_element_type=F32).astype(BF16)
        for t in range(2):
            at = 2 * HALF + t * 2 * CH
            out[at : at + 2 * CH, :] = value[:, t * LANES : (t + 1) * LANES]
        out[2 * HALF + 4 * CH :, :] = meta


def prepare(cond_ref, state_ref, body_ref, edge_ref):
    to = iota((CH * CH, CH * CH), 0)
    of = iota((CH * CH, CH * CH), 1)
    turn = (of == (to % CH) * CH + to // CH).astype(F32).astype(BF16)
    picks = iota((16, LANES), 0)
    spots = iota((16, LANES), 1)
    first = ((picks == spots) & (picks < 2)).astype(F32).astype(BF16)
    last = ((picks == spots - (LANES - 4)) & (picks >= 2)).astype(F32).astype(BF16)

    def group(i, carry):
        for e in range(4):
            start = pl.multiple_of((4 * i + e) * CH, CH)
            rows = pl.ds(start, CH)
            value = jnp.concatenate(
                [cond_ref[:, rows, :].reshape(CC * CH, BX), scaled(state_ref[:, rows, :]).reshape(OUT * CH, BX)], axis=0
            )
            value = jnp.dot(turn, value, preferred_element_type=F32).astype(BF16)
            at = pl.ds(start * CH, CH * CH)
            edge = jnp.zeros((16, CH * CH), F32)
            for t, pick in enumerate((first, last)):
                part = value[:, t * LANES : (t + 1) * LANES]
                body_ref[t, at, :] = part
                edge = edge + lax.dot_general(pick, part, (((1,), (1,)), ((), ())), preferred_element_type=F32)
            edge_ref[:, at] = edge.astype(BF16)
        return carry

    lax.fori_loop(0, BY // CH // 4, group, 0)


def pack_sub(rows_ref, cols_ref, live_ref, weight_ref, edge_ref, above_ref, below_ref, left_ref, right_ref):
    lane = iota((1, LANES), 1)
    meta0 = own_meta(rows_ref, cols_ref, live_ref).astype(F32)
    sub = iota((16, LANES), 0)
    first = 2 * HALF + 4 * CH
    meta_a = pltpu.roll(above_ref[first:, :].astype(F32), 5, 0)
    meta_b = pltpu.roll(below_ref[first:, :].astype(F32), 10, 0)
    meta = jnp.where(sub < 5, meta0, jnp.where(sub < 10, meta_a, meta_b)).astype(BF16)
    for out, side in ((left_ref, 0), (right_ref, 1)):
        def packed(one, two):
            if side == 0:
                return jnp.where(lane < HALF, one, pltpu.roll(two, HALF, 1)).astype(BF16)
            return jnp.where(lane < HALF, pltpu.roll(one, HALF, 1), two).astype(BF16)

        out[0:SIDE, :] = packed(weight_ref[0, 0, 0], weight_ref[0, 0, 1])
        at = SIDE
        for msg in (above_ref, below_ref):
            out[at : at + HALF, :] = packed(msg[0:HALF, :].astype(F32), msg[HALF : 2 * HALF, :].astype(F32))
            at += HALF
        for msg in (above_ref, below_ref):
            begin = 2 * HALF + side * 2 * CH
            out[at : at + 2 * CH, :] = msg[begin : begin + 2 * CH, :]
            at += 2 * CH
        edge = edge_ref[...].astype(F32)
        for m in range(4):
            rows = []
            for e in range(8):
                spot = (8 * m + e) * LANES
                rows.append(edge[2 * side : 2 * side + 2, spot : spot + LANES])
            out[at : at + 16, :] = jnp.concatenate(rows, axis=0).astype(BF16)
            at += 16
        out[at:, :] = meta


def main_kernel(
    rows_ref, cols_ref, live_ref, body_ref, state_ref, weight_ref,
    above_ref, below_ref, left_ref, right_ref, w1_ref, w2_ref, w3_ref,
    den_out, next_out,
    xb_ref, p_ref, a_ref, u_ref, q_ref, acc_ref, wall_ref, meta_v, meta_s, unit_ref, place_ref, list_ref, den_ref, next_ref, sem, body_sem, out_sems,
):
    lane = iota((1, LANES), 1)
    first = 2 * HALF + 4 * CH
    meta_v[0:16, :] = own_meta(rows_ref, cols_ref, live_ref)
    meta_v[16:32, :] = above_ref[first:, :].astype(F32).astype(jnp.int32)
    meta_v[32:48, :] = below_ref[first:, :].astype(F32).astype(jnp.int32)
    meta_v[48:64, :] = left_ref[SUB_MSG - 16 :, :].astype(F32).astype(jnp.int32)
    meta_v[64:80, :] = right_ref[SUB_MSG - 16 :, :].astype(F32).astype(jnp.int32)
    copy = pltpu.make_async_copy(meta_v, meta_s, sem)
    copy.start()

    body = pltpu.make_async_copy(body_ref, xb_ref.at[1:3, X_TOP * CH : (BY + X_TOP) * CH, :], body_sem)
    body.start()
    corner = SIDE + 2 * HALF
    for msg, row, spot in ((above_ref, X_TOP - 2, 0), (below_ref, BY + X_TOP, 2 * CH)):
        for t in range(2):
            xb_ref[t + 1, row * CH : (row + 2) * CH, :] = msg[2 * HALF + t * 2 * CH : 2 * HALF + (t + 1) * 2 * CH, :]
        from_left = left_ref[corner + spot : corner + spot + 2 * CH, :].astype(F32)
        from_right = right_ref[corner + spot : corner + spot + 2 * CH, :].astype(F32)
        xb_ref[0, row * CH : (row + 2) * CH, :] = jnp.where(
            lane < 2, from_right, jnp.where(lane >= LANES - 2, from_left, 0.0)
        ).astype(BF16)
    edge_at = corner + 4 * CH
    picks = iota((32, LANES), 0)
    spots = iota((32, LANES), 1)
    for m in range(4):
        rows = slice(edge_at + 16 * m, edge_at + 16 * m + 16)
        both = jnp.concatenate([left_ref[rows, :].astype(F32), right_ref[rows, :].astype(F32)], axis=0)
        turned = both.T.astype(BF16)
        for e in range(8):
            to_left = (picks - 2 * e == spots - (LANES - 2)) & (spots >= LANES - 2) & (picks < 16)
            to_right = (picks - 16 - 2 * e == spots) & (spots < 2) & (picks >= 16)
            place = (to_left | to_right).astype(F32).astype(BF16)
            at = X_TOP * CH + (8 * m + e) * LANES
            xb_ref[0, at : at + LANES, :] = jnp.dot(turned, place, preferred_element_type=F32).astype(BF16)
    for t in range(3):
        xb_ref[t, 0 : (X_TOP - 2) * CH, :] = jnp.zeros(((X_TOP - 2) * CH, LANES), BF16)
        low = (BY + X_TOP + 2) * CH
        xb_ref[t, low:, :] = jnp.zeros((X_ROWS * CH - low, LANES), BF16)
    p_ref[...] = jnp.zeros_like(p_ref)
    a_ref[...] = jnp.zeros_like(a_ref)

    for p in range(SLOTS):
        wall_ref[p, 0:SIDE, :] = weight_ref[0, 0, p]
        wall_ref[2 + p, HALF:SIDE, :] = above_ref[p * HALF : (p + 1) * HALF, :].astype(F32)
        wall_ref[4 + p, 0:HALF, :] = below_ref[p * HALF : (p + 1) * HALF, :].astype(F32)
        for d, msg in ((3, left_ref), (6, right_ref)):
            def side(lo, hi):
                part = msg[lo:hi, :].astype(F32)
                return jnp.where((lane < HALF) == (p == 0), part, pltpu.roll(part, HALF, 1))

            wall_ref[2 * d + p, 0:SIDE, :] = side(0, SIDE)
            wall_ref[2 * d + 2 + p, HALF:SIDE, :] = side(SIDE, SIDE + HALF)
            wall_ref[2 * d + 4 + p, 0:HALF, :] = side(SIDE + HALF, SIDE + 2 * HALF)

    def clear(i, carry):
        for t in range(1, 3):
            acc_ref[t, pl.ds(pl.multiple_of(i * 256 + STEP * 8, 64), 256), :] = jnp.zeros((256, LANES), F32)
        return carry

    lax.fori_loop(0, BY * 8 // 256, clear, 0)
    copy.wait()

    one_row = (iota((8, 1), 0) == OUT).astype(F32)

    def nothing(i):
        unit_ref[0, i] = 0
        unit_ref[1, i] = 0
        unit_ref[2, i] = BY
        unit_ref[3, i] = 0

    for i in range(4 * LAG):
        nothing(i)

    pos = jnp.int32(0)
    totals = []
    pieces = []
    for k in range(PIECES):
        d, p = k // 2, k % 2
        across, along = d // 3, d % 3
        base = 16 * along if across == 0 else 32 + 16 * across + 5 * along
        row0 = meta_s[base + p, 0] + (0, -BY, BY)[along] - HALF
        col0 = meta_s[base + 2 + p, 0] + (0, -BX, BX)[across] - HALF
        low = jnp.maximum(-row0, 0) // STEP
        high = (jnp.minimum(SIDE, BY - row0) + STEP - 1) // STEP
        touches = (low < high) & (col0 > -SIDE) & (col0 < BX) & (p < meta_s[base + 4, 0])
        spot = col0 + LANES
        q, rem = spot // LANES, spot % LANES
        after_q = jnp.where(q == 2, 0, q + 1)
        whole = ((q, rem, q, rem, LANES), (after_q, rem, after_q, 0, rem))
        bound = LANES - rem
        if across == 0:
            narrow = jnp.bool_(False)
        else:
            if across == 1:
                narrow = spot <= HALF - 2
                ours = [(3, (spot + HALF * (1 - g)) % LANES, 1, 0, spot) for g in range(2)]
            else:
                narrow = col0 >= BX - (HALF - 2)
                ours = [(4, (spot + HALF * g) % LANES, 2, col0 - LANES, LANES) for g in range(2)]
            whole = [[jnp.where(narrow, x, y) for x, y in zip(mine, all_)] for mine, all_ in zip(ours, whole)]
            bound = jnp.where(narrow, HALF, bound)
        for g in range(2):
            for f in range(5):
                place_ref[5 * g + f, k] = whole[g][f]
        place_ref[10, k] = bound
        pieces.append((k, low, high, row0, touches, narrow))
    for half in range(2):
        total = jnp.int32(0)
        for k, low, high, row0, touches, narrow in pieces:
            if half == 1 and k < 6:
                continue
            ours = touches & (narrow if half == 1 else jnp.logical_not(narrow))
            list_ref[0, pos] = k
            list_ref[1, pos] = low
            list_ref[2, pos] = high
            list_ref[3, pos] = row0
            list_ref[4, pos] = half
            pos = pos + ours.astype(jnp.int32)
            total = total + jnp.where(ours, high - low, 0)
        totals.append(total)
    for i in range(8 * LAG + 16):
        list_ref[0, pos + i] = 0
        list_ref[1, pos + i] = 0
        list_ref[2, pos + i] = 1
        list_ref[3, pos + i] = BY
        list_ref[4, pos + i] = 1
    count = totals[0] + (totals[1] + 1) // 2 + 2 * LAG
    body.wait()

    def edges(i, carry):
        at = pl.ds(pl.multiple_of(i * (X_ROWS * CH // 5), CH), X_ROWS * CH // 5)
        outer = xb_ref[0, at, :]
        xb_ref[3, at, :] = jnp.where(lane < HALF, xb_ref[1, at, :], outer)
        xb_ref[4, at, :] = jnp.where(lane < HALF, outer, xb_ref[2, at, :])
        return carry

    lax.fori_loop(0, 5, edges, 0)

    def advance(unit, g, at, i):
        half = list_ref[4, at]
        unit_ref[0, unit] = list_ref[0, at]
        unit_ref[1, unit] = i * STEP
        unit_ref[2, unit] = list_ref[3, at] + i * STEP
        unit_ref[3, unit] = half
        ahead = i + (half if g == 0 else 1)
        done = ahead >= list_ref[2, at]
        at = at + done.astype(jnp.int32)
        return at, jnp.where(done, list_ref[1, at], ahead)

    first_half = lane < HALF

    def by_half(values):
        return jnp.where(first_half, values[0].astype(F32), values[1].astype(F32))

    def borders(split):
        lo = jnp.where((lane == 0) | ((lane == HALF) & (split > 0)), 0.0, 1.0)
        hi = jnp.where((lane == LANES - 1) | ((lane == HALF - 1) & (split > 0)), 0.0, 1.0)
        return [jnp.broadcast_to(part, (CH, LANES)).astype(BF16) for part in (lo, hi)]

    def keep(ref, z, row, h, part, mask):
        for m in range(part.shape[0] // CH):
            ref[z, row + m * CH : row + (m + 1) * CH, h * LANES : (h + 1) * LANES] = jnp.where(mask > 0, part[m * CH : (m + 1) * CH], jnp.zeros((), BF16))

    def blend(i):
        nets = [
            jnp.dot(w3_ref[...], q_ref[4 * e * HID : 4 * (e + 1) * HID, :], preferred_element_type=F32)
            for e in range(STEP // 4)
        ]
        for h in range(2):
            units = [4 * i + 2 * h + g for g in range(2)]
            ks = [unit_ref[0, unit] for unit in units]
            locals_ = [unit_ref[1, unit] for unit in units]
            parts = []
            for f in range(STEP):
                y = nets[f // 4][8 * (f % 4) : 8 * (f % 4) + 8, h * LANES : (h + 1) * LANES]
                one, two = [wall_ref[k, pl.ds(local + f, 1), :] for k, local in zip(ks, locals_)]
                parts.append((y + one_row) * jnp.where(first_half, one, two))
            value = jnp.concatenate(parts, axis=0)
            for g in range(2):
                turn, tile, lo, hi = [place_ref[5 * g + f, ks[g]] for f in range(1, 5)]
                y = pltpu.roll(value, turn, 1)
                at = pl.ds(pl.multiple_of((unit_ref[2, units[g]] + STEP) * 8, 8), 8 * STEP)
                acc_ref[tile, at, :] += jnp.where((lane >= lo) & (lane < hi), y, 0.0)

    def second_conv(z):
        for e in range(STEP // 2):
            v = jnp.dot(w2_ref[...], a_ref[z, 2 * e * 3 * HID : (2 * e + 4) * 3 * HID, :], preferred_element_type=F32)
            v = v + u_ref[z, (2 * e + 1) * HID : (2 * e + 3) * HID, :]
            q_ref[2 * e * HID : (2 * e + 2) * HID, :] = (v + v * jnp.tanh(v)).astype(BF16)

    def first_conv(i, z):
        for e in range(STEP // 2 + 1):
            u = jnp.dot(w1_ref[...], p_ref[z, 2 * e * 3 * CH : (2 * e + 4) * 3 * CH, :], preferred_element_type=F32)
            u_ref[z, 2 * e * HID : (2 * e + 2) * HID, :] = u
            act = u + u * jnp.tanh(u)
            for h in range(2):
                units = [4 * i + 2 * h + g for g in range(2)]
                locals_ = [unit_ref[1, unit] for unit in units]
                inner_lo, inner_hi = borders(unit_ref[3, units[0]])
                for r in range(2):
                    mid = act[r * HID : (r + 1) * HID, h * LANES : (h + 1) * LANES]
                    row = 2 * e + r
                    if row == 0:
                        mid = mid * by_half([local > 0 for local in locals_])
                    if row == STEP + 1:
                        mid = mid * by_half([local < SIDE - STEP for local in locals_])
                    mid = mid.astype(BF16)
                    at = row * 3 * HID
                    keep(a_ref, z, at, h, pltpu.roll(mid, 1, 1), inner_lo)
                    a_ref[z, at + HID : at + 2 * HID, h * LANES : (h + 1) * LANES] = mid
                    keep(a_ref, z, at + 2 * HID, h, pltpu.roll(mid, LANES - 1, 1), inner_hi)

    def stage(i, z):
        for h in range(2):
            units = [4 * i + 2 * h + g for g in range(2)]
            locals_ = [unit_ref[1, unit] for unit in units]
            inner_lo, inner_hi = borders(unit_ref[3, units[0]])
            ks = [unit_ref[0, unit] for unit in units]
            tiles = [place_ref[5 * g, ks[g]] for g in range(2)]
            turns = [(LANES - place_ref[5 * g + 1, ks[g]]) % LANES for g in range(2)]
            rows = [unit_ref[2, unit] for unit in units]
            low_part = lane < place_ref[10, ks[0]]
            both = []
            for tile, turn, row in zip(tiles, turns, rows):
                at = pl.ds(pl.multiple_of((row + X_TOP - 2) * CH, CH), (STEP + 4) * CH)
                both.append(pltpu.roll(xb_ref[tile, at, :], turn, 1))
            value = jnp.where(low_part, both[0], both[1])
            for j in range(STEP + 4):
                mid = value[j * CH : (j + 1) * CH]
                if j < 2:
                    mid = mid * by_half([local > 0 for local in locals_]).astype(BF16)
                if j >= STEP + 2:
                    mid = mid * by_half([local < SIDE - STEP for local in locals_]).astype(BF16)
                keep(p_ref, z, j * 3 * CH, h, pltpu.roll(mid, 1, 1), inner_lo)
                p_ref[z, j * 3 * CH + CH : j * 3 * CH + 2 * CH, h * LANES : (h + 1) * LANES] = mid
                keep(p_ref, z, j * 3 * CH + 2 * CH, h, pltpu.roll(mid, LANES - 1, 1), inner_hi)

    def step(i, carry):
        at, row = carry
        for z in range(2):
            first_conv(2 * i + z + 2, z)
            blend(2 * i + z)
            second_conv(1 - z)
            stage(2 * i + z + 3, 1 - z)
        return more(i + 1, at, row)

    def more(i, at, row):
        for h in range(8):
            at, row = advance(8 * i + 4 * LAG + h, h % 2, at, row)
        return at, row

    lax.fori_loop(0, (count + 3) // 4, step, more(0, jnp.int32(0), list_ref[1, 0]))

    def finish(i, carry):
        for t, part in ((t, part) for part in range(4) for t in range(2)):
            row = pl.multiple_of(i * 32 + part * 8, 8)
            lanes = slice(t * LANES, (t + 1) * LANES)
            total = acc_ref[t + 1, pl.ds((row + STEP) * 8 + OUT, 8, stride=8), :]
            over = 1.0 / (1.0 + total)
            for o in range(OUT):
                state = state_ref[o, pl.ds(row, 8), lanes]
                numer = acc_ref[t + 1, pl.ds((row + STEP) * 8 + o, 8, stride=8), :]
                den = (state * (1.0 + C_SKIP * total) + C_OUT * numer) * over
                den_ref[o, pl.ds(row, 8), lanes] = den
                next_ref[o, pl.ds(row, 8), lanes] = state + (SIGMA_NEXT - SIGMA) * (state - den) / SIGMA
        rows = pl.ds(pl.multiple_of(i * 32, 32), 32)
        for held, out, at in ((den_ref, den_out, 0), (next_ref, next_out, 1)):
            pltpu.make_async_copy(held.at[:, rows, :], out.at[:, rows, :], out_sems.at[at]).start()
        return carry

    lax.fori_loop(0, BY // 32, finish, 0)
    for held, out, at in ((den_ref, den_out, 0), (next_ref, next_out, 1)):
        pltpu.make_async_copy(held, out, out_sems.at[at]).wait()


def banded(kernel, times):
    outs, chans = kernel.shape[2], kernel.shape[3]
    flat = (0.5 * jnp.transpose(kernel, (2, 0, 1, 3))).astype(BF16).reshape(outs, 9 * chans)
    step = 3 * chans
    return jnp.concatenate([jnp.pad(flat, ((0, 0), (r * step, (times - 1 - r) * step))) for r in range(times)], axis=0)


def shifted(value, axis, steps):
    count = lax.axis_size(axis)
    first, last = max(0, -steps), min(count, count - steps)
    return lax.ppermute(value, axis, [(i, i + steps) for i in range(first, last)])


def per_device(condition, state, corner_rows, corner_cols, live_counts, blend_weight, conv_in, conv_mid, proj_out):
    smem = pl.BlockSpec(memory_space=pltpu.SMEM)
    vmem = pl.BlockSpec(memory_space=pltpu.VMEM)
    whole_w = pl.BlockSpec((1, 1, SLOTS, SIDE, SIDE), lambda i: (0, 0, 0, 0, 0))
    msg = jax.ShapeDtypeStruct((TILE_MSG, LANES), BF16)
    up, down = pl.pallas_call(
        pack_tile,
        grid=(1,),
        in_specs=[
            smem, smem, smem,
            pl.BlockSpec((CC, 16, BX), lambda i: (0, 0, 0)),
            pl.BlockSpec((CC, 16, BX), lambda i: (0, BY // 16 - 1, 0)),
            pl.BlockSpec((OUT, 16, BX), lambda i: (0, 0, 0)),
            pl.BlockSpec((OUT, 16, BX), lambda i: (0, BY // 16 - 1, 0)),
            whole_w,
        ],
        out_specs=[pl.BlockSpec((TILE_MSG, LANES), lambda i: (0, 0))] * 2,
        out_shape=[msg, msg],
        name="pack_tile",
    )(corner_rows, corner_cols, live_counts, condition, condition, state, state, blend_weight)
    above = shifted(down, "tile", 1)
    below = shifted(up, "tile", -1)
    w1 = banded(conv_in, 2)
    w2 = banded(conv_mid, 2)
    rows8 = jnp.pad(proj_out, ((0, 8 - OUT), (0, 0)))
    w3 = jnp.concatenate([jnp.pad(rows8, ((0, 0), (r * HID, (3 - r) * HID))) for r in range(4)], axis=0)
    body, edge = pl.pallas_call(
        prepare,
        in_specs=[vmem] * 2,
        out_specs=[vmem] * 2,
        out_shape=[jax.ShapeDtypeStruct((2, BY * CH, LANES), BF16), jax.ShapeDtypeStruct((16, BY * CH), BF16)],
        name="prepare",
        compiler_params=pltpu.CompilerParams(vmem_limit_bytes=16 << 20),
        cost_estimate=pl.CostEstimate(flops=2 * 4096 * 256 * 256, bytes_accessed=5 << 20, transcendentals=0),
    )(condition, state)
    msg = jax.ShapeDtypeStruct((SUB_MSG, LANES), BF16)
    left, right = pl.pallas_call(
        pack_sub,
        in_specs=[smem] * 3 + [vmem] * 4,
        out_specs=[vmem] * 2,
        out_shape=[msg, msg],
        name="pack_sub",
        compiler_params=pltpu.CompilerParams(vmem_limit_bytes=16 << 20),
    )(corner_rows, corner_cols, live_counts, blend_weight, edge, above, below)
    from_left = shifted(right, "sub", 1)
    from_right = shifted(left, "sub", -1)
    out = jax.ShapeDtypeStruct((OUT, BY, BX), F32)
    return tuple(pl.pallas_call(
        main_kernel,
        in_specs=[smem] * 3 + [vmem] * 10,
        out_specs=[pl.BlockSpec(memory_space=pl.ANY)] * 2,
        out_shape=[out, out],
        scratch_shapes=[
            pltpu.VMEM((5, X_ROWS * CH, LANES), BF16),
            pltpu.VMEM((2, (STEP + 4) * 3 * CH, WIDE), BF16),
            pltpu.VMEM((2, (STEP + 2) * 3 * HID, WIDE), BF16),
            pltpu.VMEM((2, (STEP + 2) * HID, WIDE), F32),
            pltpu.VMEM((STEP * HID, WIDE), BF16),
            pltpu.VMEM((3, ACC_ROWS * 8, LANES), F32),
            pltpu.VMEM((PIECES, SIDE, LANES), F32),
            pltpu.VMEM((80, LANES), jnp.int32),
            pltpu.SMEM((80, LANES), jnp.int32),
            pltpu.SMEM((4, UNITS), jnp.int32),
            pltpu.SMEM((11, PIECES), jnp.int32),
            pltpu.SMEM((5, LANES), jnp.int32),
            pltpu.VMEM((OUT, BY, BX), F32),
            pltpu.VMEM((OUT, BY, BX), F32),
            pltpu.SemaphoreType.DMA,
            pltpu.SemaphoreType.DMA,
            pltpu.SemaphoreType.DMA((2,)),
        ],
        name="patches",
        compiler_params=pltpu.CompilerParams(vmem_limit_bytes=26 << 20),
    )(corner_rows, corner_cols, live_counts, body, state, blend_weight, above, below, from_left, from_right, w1, w2, w3))


def solution(mesh):
    placed = (
        P(None, "tile", "sub"),
        P(None, "tile", "sub"),
        P("tile", "sub", None),
        P("tile", "sub", None),
        P("tile", "sub"),
        P("tile", "sub", None, None, None),
        P(),
        P(),
        P(),
    )
    return jax.shard_map(
        per_device,
        mesh=mesh,
        in_specs=placed,
        out_specs=(P(None, "tile", "sub"), P(None, "tile", "sub")),
        check_vma=False,
    )
```

```python
import jax
import jax.numpy as jnp
from jax import lax
from jax.experimental import pallas as pl
from jax.experimental.pallas import tpu as pltpu
from jax.sharding import PartitionSpec as P

SIGMA = 2.0
SIGMA_NEXT = 1.6
C_IN = 1.0 / (SIGMA * SIGMA + 0.25) ** 0.5
C_SKIP = 0.25 / (SIGMA * SIGMA + 0.25)
C_OUT = 0.5 * SIGMA / (SIGMA * SIGMA + 0.25) ** 0.5

BY = 256
BX = 256
SIDE = 128
HALF = 64
CC = 12
CH = 16
HID = 64
OUT = 4
SLOTS = 2
LANES = 128
WIDE = 2 * LANES
STEP = 8
X_TOP = 10
X_ROWS = BY + 24
ACC_ROWS = BY + 2 * STEP
LAG = 3
UNITS = 768
PIECES = 9 * SLOTS
TILE_MSG = 2 * HALF + 4 * CH + 16
SUB_MSG = SIDE + 2 * HALF + 4 * CH + 64 + 16
F32 = jnp.float32
BF16 = jnp.bfloat16


def iota(shape, dim):
    return lax.broadcasted_iota(jnp.int32, shape, dim)


def scaled(state):
    return (state * C_IN).astype(BF16)


def own_meta(rows_ref, cols_ref, live_ref):
    sub = iota((16, LANES), 0)
    values = (rows_ref[0, 0, 0], rows_ref[0, 0, 1], cols_ref[0, 0, 0], cols_ref[0, 0, 1], live_ref[0, 0])
    tile = jnp.zeros((16, LANES), jnp.int32)
    for k, value in enumerate(values):
        tile = jnp.where(sub == k, value, tile)
    return tile


def pack_tile(rows_ref, cols_ref, live_ref, c_top, c_bot, s_top, s_bot, weight_ref, up_ref, down_ref):
    meta = own_meta(rows_ref, cols_ref, live_ref).astype(F32).astype(BF16)
    to = iota((2 * CH, CH * CH), 0)
    of = iota((2 * CH, CH * CH), 1)
    for out, cond, state, low, first in ((up_ref, c_top, s_top, 0, 0), (down_ref, c_bot, s_bot, HALF, CH - 2)):
        for p in range(SLOTS):
            out[p * HALF : (p + 1) * HALF, :] = weight_ref[0, 0, p, low : low + HALF, :].astype(BF16)
        pick = (of == (to % CH) * CH + to // CH + first).astype(F32).astype(BF16)
        value = jnp.concatenate([cond[...].reshape(CC * CH, BX), scaled(state[...]).reshape(OUT * CH, BX)], axis=0)
        value = jnp.dot(pick, value, preferred_element_type=F32).astype(BF16)
        for t in range(2):
            at = 2 * HALF + t * 2 * CH
            out[at : at + 2 * CH, :] = value[:, t * LANES : (t + 1) * LANES]
        out[2 * HALF + 4 * CH :, :] = meta


def prepare(cond_ref, state_ref, body_ref, edge_ref):
    to = iota((CH * CH, CH * CH), 0)
    of = iota((CH * CH, CH * CH), 1)
    turn = (of == (to % CH) * CH + to // CH).astype(F32).astype(BF16)
    picks = iota((16, LANES), 0)
    spots = iota((16, LANES), 1)
    first = ((picks == spots) & (picks < 2)).astype(F32).astype(BF16)
    last = ((picks == spots - (LANES - 4)) & (picks >= 2)).astype(F32).astype(BF16)

    def group(i, carry):
        for e in range(4):
            start = pl.multiple_of((4 * i + e) * CH, CH)
            rows = pl.ds(start, CH)
            value = jnp.concatenate(
                [cond_ref[:, rows, :].reshape(CC * CH, BX), scaled(state_ref[:, rows, :]).reshape(OUT * CH, BX)], axis=0
            )
            value = jnp.dot(turn, value, preferred_element_type=F32).astype(BF16)
            at = pl.ds(start * CH, CH * CH)
            edge = jnp.zeros((16, CH * CH), F32)
            for t, pick in enumerate((first, last)):
                part = value[:, t * LANES : (t + 1) * LANES]
                body_ref[t, at, :] = part
                edge = edge + lax.dot_general(pick, part, (((1,), (1,)), ((), ())), preferred_element_type=F32)
            edge_ref[:, at] = edge.astype(BF16)
        return carry

    lax.fori_loop(0, BY // CH // 4, group, 0)


def pack_sub(rows_ref, cols_ref, live_ref, weight_ref, edge_ref, above_ref, below_ref, left_ref, right_ref):
    lane = iota((1, LANES), 1)
    meta0 = own_meta(rows_ref, cols_ref, live_ref).astype(F32)
    sub = iota((16, LANES), 0)
    first = 2 * HALF + 4 * CH
    meta_a = pltpu.roll(above_ref[first:, :].astype(F32), 5, 0)
    meta_b = pltpu.roll(below_ref[first:, :].astype(F32), 10, 0)
    meta = jnp.where(sub < 5, meta0, jnp.where(sub < 10, meta_a, meta_b)).astype(BF16)
    for out, side in ((left_ref, 0), (right_ref, 1)):
        def packed(one, two):
            if side == 0:
                return jnp.where(lane < HALF, one, pltpu.roll(two, HALF, 1)).astype(BF16)
            return jnp.where(lane < HALF, pltpu.roll(one, HALF, 1), two).astype(BF16)

        out[0:SIDE, :] = packed(weight_ref[0, 0, 0], weight_ref[0, 0, 1])
        at = SIDE
        for msg in (above_ref, below_ref):
            out[at : at + HALF, :] = packed(msg[0:HALF, :].astype(F32), msg[HALF : 2 * HALF, :].astype(F32))
            at += HALF
        for msg in (above_ref, below_ref):
            begin = 2 * HALF + side * 2 * CH
            out[at : at + 2 * CH, :] = msg[begin : begin + 2 * CH, :]
            at += 2 * CH
        edge = edge_ref[...].astype(F32)
        for m in range(4):
            rows = []
            for e in range(8):
                spot = (8 * m + e) * LANES
                rows.append(edge[2 * side : 2 * side + 2, spot : spot + LANES])
            out[at : at + 16, :] = jnp.concatenate(rows, axis=0).astype(BF16)
            at += 16
        out[at:, :] = meta


def main_kernel(
    rows_ref, cols_ref, live_ref, body_ref, state_ref, weight_ref,
    above_ref, below_ref, left_ref, right_ref, w1_ref, w2_ref, w3_ref,
    den_out, next_out,
    xb_ref, p_ref, a_ref, u_ref, q_ref, acc_ref, wall_ref, meta_v, meta_s, unit_ref, place_ref, list_ref, den_ref, next_ref, sem, body_sem, out_sems,
):
    lane = iota((1, LANES), 1)
    first = 2 * HALF + 4 * CH
    meta_v[0:16, :] = own_meta(rows_ref, cols_ref, live_ref)
    meta_v[16:32, :] = above_ref[first:, :].astype(F32).astype(jnp.int32)
    meta_v[32:48, :] = below_ref[first:, :].astype(F32).astype(jnp.int32)
    meta_v[48:64, :] = left_ref[SUB_MSG - 16 :, :].astype(F32).astype(jnp.int32)
    meta_v[64:80, :] = right_ref[SUB_MSG - 16 :, :].astype(F32).astype(jnp.int32)
    copy = pltpu.make_async_copy(meta_v, meta_s, sem)
    copy.start()

    body = pltpu.make_async_copy(body_ref, xb_ref.at[1:3, X_TOP * CH : (BY + X_TOP) * CH, :], body_sem)
    body.start()
    corner = SIDE + 2 * HALF
    for msg, row, spot in ((above_ref, X_TOP - 2, 0), (below_ref, BY + X_TOP, 2 * CH)):
        for t in range(2):
            xb_ref[t + 1, row * CH : (row + 2) * CH, :] = msg[2 * HALF + t * 2 * CH : 2 * HALF + (t + 1) * 2 * CH, :]
        from_left = left_ref[corner + spot : corner + spot + 2 * CH, :].astype(F32)
        from_right = right_ref[corner + spot : corner + spot + 2 * CH, :].astype(F32)
        xb_ref[0, row * CH : (row + 2) * CH, :] = jnp.where(
            lane < 2, from_right, jnp.where(lane >= LANES - 2, from_left, 0.0)
        ).astype(BF16)
    edge_at = corner + 4 * CH
    picks = iota((32, LANES), 0)
    spots = iota((32, LANES), 1)
    for m in range(4):
        rows = slice(edge_at + 16 * m, edge_at + 16 * m + 16)
        both = jnp.concatenate([left_ref[rows, :].astype(F32), right_ref[rows, :].astype(F32)], axis=0)
        turned = both.T.astype(BF16)
        for e in range(8):
            to_left = (picks - 2 * e == spots - (LANES - 2)) & (spots >= LANES - 2) & (picks < 16)
            to_right = (picks - 16 - 2 * e == spots) & (spots < 2) & (picks >= 16)
            place = (to_left | to_right).astype(F32).astype(BF16)
            at = X_TOP * CH + (8 * m + e) * LANES
            xb_ref[0, at : at + LANES, :] = jnp.dot(turned, place, preferred_element_type=F32).astype(BF16)
    for t in range(3):
        xb_ref[t, 0 : (X_TOP - 2) * CH, :] = jnp.zeros(((X_TOP - 2) * CH, LANES), BF16)
        low = (BY + X_TOP + 2) * CH
        xb_ref[t, low:, :] = jnp.zeros((X_ROWS * CH - low, LANES), BF16)
    p_ref[...] = jnp.zeros_like(p_ref)
    a_ref[...] = jnp.zeros_like(a_ref)

    for p in range(SLOTS):
        wall_ref[p, 0:SIDE, :] = weight_ref[0, 0, p]
        wall_ref[2 + p, HALF:SIDE, :] = above_ref[p * HALF : (p + 1) * HALF, :].astype(F32)
        wall_ref[4 + p, 0:HALF, :] = below_ref[p * HALF : (p + 1) * HALF, :].astype(F32)
        for d, msg in ((3, left_ref), (6, right_ref)):
            def side(lo, hi):
                part = msg[lo:hi, :].astype(F32)
                return jnp.where((lane < HALF) == (p == 0), part, pltpu.roll(part, HALF, 1))

            wall_ref[2 * d + p, 0:SIDE, :] = side(0, SIDE)
            wall_ref[2 * d + 2 + p, HALF:SIDE, :] = side(SIDE, SIDE + HALF)
            wall_ref[2 * d + 4 + p, 0:HALF, :] = side(SIDE + HALF, SIDE + 2 * HALF)

    def clear(i, carry):
        for t in range(1, 3):
            acc_ref[t, pl.ds(pl.multiple_of(i * 256 + STEP * 8, 64), 256), :] = jnp.zeros((256, LANES), F32)
        return carry

    lax.fori_loop(0, BY * 8 // 256, clear, 0)
    copy.wait()

    one_row = (iota((8, 1), 0) == OUT).astype(F32)

    def nothing(i):
        unit_ref[0, i] = 0
        unit_ref[1, i] = 0
        unit_ref[2, i] = BY
        unit_ref[3, i] = 0

    for i in range(4 * LAG):
        nothing(i)

    pos = jnp.int32(0)
    totals = []
    pieces = []
    for k in range(PIECES):
        d, p = k // 2, k % 2
        across, along = d // 3, d % 3
        base = 16 * along if across == 0 else 32 + 16 * across + 5 * along
        row0 = meta_s[base + p, 0] + (0, -BY, BY)[along] - HALF
        col0 = meta_s[base + 2 + p, 0] + (0, -BX, BX)[across] - HALF
        low = jnp.maximum(-row0, 0) // STEP
        high = (jnp.minimum(SIDE, BY - row0) + STEP - 1) // STEP
        touches = (low < high) & (col0 > -SIDE) & (col0 < BX) & (p < meta_s[base + 4, 0])
        spot = col0 + LANES
        q, rem = spot // LANES, spot % LANES
        after_q = jnp.where(q == 2, 0, q + 1)
        whole = ((q, rem, q, rem, LANES), (after_q, rem, after_q, 0, rem))
        bound = LANES - rem
        if across == 0:
            narrow = jnp.bool_(False)
        else:
            if across == 1:
                narrow = spot <= HALF - 2
                ours = [(3, (spot + HALF * (1 - g)) % LANES, 1, 0, spot) for g in range(2)]
            else:
                narrow = col0 >= BX - (HALF - 2)
                ours = [(4, (spot + HALF * g) % LANES, 2, col0 - LANES, LANES) for g in range(2)]
            whole = [[jnp.where(narrow, x, y) for x, y in zip(mine, all_)] for mine, all_ in zip(ours, whole)]
            bound = jnp.where(narrow, HALF, bound)
        for g in range(2):
            for f in range(5):
                place_ref[5 * g + f, k] = whole[g][f]
        place_ref[10, k] = bound
        pieces.append((k, low, high, row0, touches, narrow))
    for half in range(2):
        total = jnp.int32(0)
        for k, low, high, row0, touches, narrow in pieces:
            if half == 1 and k < 6:
                continue
            ours = touches & (narrow if half == 1 else jnp.logical_not(narrow))
            list_ref[0, pos] = k
            list_ref[1, pos] = low
            list_ref[2, pos] = high
            list_ref[3, pos] = row0
            list_ref[4, pos] = half
            pos = pos + ours.astype(jnp.int32)
            total = total + jnp.where(ours, high - low, 0)
        totals.append(total)
    for i in range(8 * LAG + 16):
        list_ref[0, pos + i] = 0
        list_ref[1, pos + i] = 0
        list_ref[2, pos + i] = 1
        list_ref[3, pos + i] = BY
        list_ref[4, pos + i] = 1
    count = totals[0] + (totals[1] + 1) // 2 + 2 * LAG
    body.wait()

    def edges(i, carry):
        at = pl.ds(pl.multiple_of(i * (X_ROWS * CH // 5), CH), X_ROWS * CH // 5)
        outer = xb_ref[0, at, :]
        xb_ref[3, at, :] = jnp.where(lane < HALF, xb_ref[1, at, :], outer)
        xb_ref[4, at, :] = jnp.where(lane < HALF, outer, xb_ref[2, at, :])
        return carry

    lax.fori_loop(0, 5, edges, 0)

    def advance(unit, g, at, i):
        half = list_ref[4, at]
        unit_ref[0, unit] = list_ref[0, at]
        unit_ref[1, unit] = i * STEP
        unit_ref[2, unit] = list_ref[3, at] + i * STEP
        unit_ref[3, unit] = half
        ahead = i + (half if g == 0 else 1)
        done = ahead >= list_ref[2, at]
        at = at + done.astype(jnp.int32)
        return at, jnp.where(done, list_ref[1, at], ahead)

    first_half = lane < HALF

    def by_half(values):
        return jnp.where(first_half, values[0].astype(F32), values[1].astype(F32))

    def borders(split):
        lo = jnp.where((lane == 0) | ((lane == HALF) & (split > 0)), 0.0, 1.0)
        hi = jnp.where((lane == LANES - 1) | ((lane == HALF - 1) & (split > 0)), 0.0, 1.0)
        return [jnp.broadcast_to(part, (CH, LANES)).astype(BF16) for part in (lo, hi)]

    def keep(ref, z, row, h, part, mask):
        for m in range(part.shape[0] // CH):
            ref[z, row + m * CH : row + (m + 1) * CH, h * LANES : (h + 1) * LANES] = jnp.where(mask > 0, part[m * CH : (m + 1) * CH], jnp.zeros((), BF16))

    def blend(i, z):
        nets = [
            jnp.dot(w3_ref[...], q_ref[z, 4 * e * HID : 4 * (e + 1) * HID, :], preferred_element_type=F32)
            for e in range(STEP // 4)
        ]
        for h in range(2):
            units = [4 * i + 2 * h + g for g in range(2)]
            ks = [unit_ref[0, unit] for unit in units]
            locals_ = [unit_ref[1, unit] for unit in units]
            parts = []
            for f in range(STEP):
                y = nets[f // 4][8 * (f % 4) : 8 * (f % 4) + 8, h * LANES : (h + 1) * LANES]
                one, two = [wall_ref[k, pl.ds(local + f, 1), :] for k, local in zip(ks, locals_)]
                parts.append((y + one_row) * jnp.where(first_half, one, two))
            value = jnp.concatenate(parts, axis=0)
            for g in range(2):
                turn, tile, lo, hi = [place_ref[5 * g + f, ks[g]] for f in range(1, 5)]
                y = pltpu.roll(value, turn, 1)
                at = pl.ds(pl.multiple_of((unit_ref[2, units[g]] + STEP) * 8, 8), 8 * STEP)
                acc_ref[tile, at, :] += jnp.where((lane >= lo) & (lane < hi), y, 0.0)

    def second_conv(z, y):
        for e in range(STEP // 2):
            v = jnp.dot(w2_ref[...], a_ref[z, 2 * e * 3 * HID : (2 * e + 4) * 3 * HID, :], preferred_element_type=F32)
            v = v + u_ref[z, (2 * e + 1) * HID : (2 * e + 3) * HID, :]
            q_ref[y, 2 * e * HID : (2 * e + 2) * HID, :] = (v + v * jnp.tanh(v)).astype(BF16)

    def first_conv(i, z):
        for e in range(STEP // 2 + 1):
            u = jnp.dot(w1_ref[...], p_ref[z, 2 * e * 3 * CH : (2 * e + 4) * 3 * CH, :], preferred_element_type=F32)
            u_ref[z, 2 * e * HID : (2 * e + 2) * HID, :] = u
            act = u + u * jnp.tanh(u)
            for h in range(2):
                units = [4 * i + 2 * h + g for g in range(2)]
                locals_ = [unit_ref[1, unit] for unit in units]
                inner_lo, inner_hi = borders(unit_ref[3, units[0]])
                for r in range(2):
                    mid = act[r * HID : (r + 1) * HID, h * LANES : (h + 1) * LANES]
                    row = 2 * e + r
                    if row == 0:
                        mid = mid * by_half([local > 0 for local in locals_])
                    if row == STEP + 1:
                        mid = mid * by_half([local < SIDE - STEP for local in locals_])
                    mid = mid.astype(BF16)
                    at = row * 3 * HID
                    keep(a_ref, z, at, h, pltpu.roll(mid, 1, 1), inner_lo)
                    a_ref[z, at + HID : at + 2 * HID, h * LANES : (h + 1) * LANES] = mid
                    keep(a_ref, z, at + 2 * HID, h, pltpu.roll(mid, LANES - 1, 1), inner_hi)

    def stage(i, z):
        for h in range(2):
            units = [4 * i + 2 * h + g for g in range(2)]
            locals_ = [unit_ref[1, unit] for unit in units]
            inner_lo, inner_hi = borders(unit_ref[3, units[0]])
            ks = [unit_ref[0, unit] for unit in units]
            tiles = [place_ref[5 * g, ks[g]] for g in range(2)]
            turns = [(LANES - place_ref[5 * g + 1, ks[g]]) % LANES for g in range(2)]
            rows = [unit_ref[2, unit] for unit in units]
            low_part = lane < place_ref[10, ks[0]]
            both = []
            for tile, turn, row in zip(tiles, turns, rows):
                at = pl.ds(pl.multiple_of((row + X_TOP - 2) * CH, CH), (STEP + 4) * CH)
                both.append(pltpu.roll(xb_ref[tile, at, :], turn, 1))
            value = jnp.where(low_part, both[0], both[1])
            for j in range(STEP + 4):
                mid = value[j * CH : (j + 1) * CH]
                if j < 2:
                    mid = mid * by_half([local > 0 for local in locals_]).astype(BF16)
                if j >= STEP + 2:
                    mid = mid * by_half([local < SIDE - STEP for local in locals_]).astype(BF16)
                keep(p_ref, z, j * 3 * CH, h, pltpu.roll(mid, 1, 1), inner_lo)
                p_ref[z, j * 3 * CH + CH : j * 3 * CH + 2 * CH, h * LANES : (h + 1) * LANES] = mid
                keep(p_ref, z, j * 3 * CH + 2 * CH, h, pltpu.roll(mid, LANES - 1, 1), inner_hi)

    def step(i, carry):
        at, row = carry
        for z in range(2):
            first_conv(2 * i + z + 2, z)
            blend(2 * i + z, 1 - z)
            second_conv(1 - z, z)
            stage(2 * i + z + 3, 1 - z)
        return more(i + 1, at, row)

    def more(i, at, row):
        for h in range(8):
            at, row = advance(8 * i + 4 * LAG + h, h % 2, at, row)
        return at, row

    lax.fori_loop(0, (count + 3) // 4, step, more(0, jnp.int32(0), list_ref[1, 0]))

    def finish(i, carry):
        for t, part in ((t, part) for part in range(4) for t in range(2)):
            row = pl.multiple_of(i * 32 + part * 8, 8)
            lanes = slice(t * LANES, (t + 1) * LANES)
            total = acc_ref[t + 1, pl.ds((row + STEP) * 8 + OUT, 8, stride=8), :]
            over = 1.0 / (1.0 + total)
            for o in range(OUT):
                state = state_ref[o, pl.ds(row, 8), lanes]
                numer = acc_ref[t + 1, pl.ds((row + STEP) * 8 + o, 8, stride=8), :]
                den = (state * (1.0 + C_SKIP * total) + C_OUT * numer) * over
                den_ref[o, pl.ds(row, 8), lanes] = den
                next_ref[o, pl.ds(row, 8), lanes] = state + (SIGMA_NEXT - SIGMA) * (state - den) / SIGMA
        rows = pl.ds(pl.multiple_of(i * 32, 32), 32)
        for held, out, at in ((den_ref, den_out, 0), (next_ref, next_out, 1)):
            pltpu.make_async_copy(held.at[:, rows, :], out.at[:, rows, :], out_sems.at[at]).start()
        return carry

    lax.fori_loop(0, BY // 32, finish, 0)
    for held, out, at in ((den_ref, den_out, 0), (next_ref, next_out, 1)):
        pltpu.make_async_copy(held, out, out_sems.at[at]).wait()


def banded(kernel, times):
    outs, chans = kernel.shape[2], kernel.shape[3]
    flat = (0.5 * jnp.transpose(kernel, (2, 0, 1, 3))).astype(BF16).reshape(outs, 9 * chans)
    step = 3 * chans
    return jnp.concatenate([jnp.pad(flat, ((0, 0), (r * step, (times - 1 - r) * step))) for r in range(times)], axis=0)


def shifted(value, axis, steps):
    count = lax.axis_size(axis)
    first, last = max(0, -steps), min(count, count - steps)
    return lax.ppermute(value, axis, [(i, i + steps) for i in range(first, last)])


def per_device(condition, state, corner_rows, corner_cols, live_counts, blend_weight, conv_in, conv_mid, proj_out):
    smem = pl.BlockSpec(memory_space=pltpu.SMEM)
    vmem = pl.BlockSpec(memory_space=pltpu.VMEM)
    whole_w = pl.BlockSpec((1, 1, SLOTS, SIDE, SIDE), lambda i: (0, 0, 0, 0, 0))
    msg = jax.ShapeDtypeStruct((TILE_MSG, LANES), BF16)
    up, down = pl.pallas_call(
        pack_tile,
        grid=(1,),
        in_specs=[
            smem, smem, smem,
            pl.BlockSpec((CC, 16, BX), lambda i: (0, 0, 0)),
            pl.BlockSpec((CC, 16, BX), lambda i: (0, BY // 16 - 1, 0)),
            pl.BlockSpec((OUT, 16, BX), lambda i: (0, 0, 0)),
            pl.BlockSpec((OUT, 16, BX), lambda i: (0, BY // 16 - 1, 0)),
            whole_w,
        ],
        out_specs=[pl.BlockSpec((TILE_MSG, LANES), lambda i: (0, 0))] * 2,
        out_shape=[msg, msg],
        name="pack_tile",
    )(corner_rows, corner_cols, live_counts, condition, condition, state, state, blend_weight)
    above = shifted(down, "tile", 1)
    below = shifted(up, "tile", -1)
    w1 = banded(conv_in, 2)
    w2 = banded(conv_mid, 2)
    rows8 = jnp.pad(proj_out, ((0, 8 - OUT), (0, 0)))
    w3 = jnp.concatenate([jnp.pad(rows8, ((0, 0), (r * HID, (3 - r) * HID))) for r in range(4)], axis=0)
    body, edge = pl.pallas_call(
        prepare,
        in_specs=[vmem] * 2,
        out_specs=[vmem] * 2,
        out_shape=[jax.ShapeDtypeStruct((2, BY * CH, LANES), BF16), jax.ShapeDtypeStruct((16, BY * CH), BF16)],
        name="prepare",
        compiler_params=pltpu.CompilerParams(vmem_limit_bytes=16 << 20),
        cost_estimate=pl.CostEstimate(flops=2 * 4096 * 256 * 256, bytes_accessed=5 << 20, transcendentals=0),
    )(condition, state)
    msg = jax.ShapeDtypeStruct((SUB_MSG, LANES), BF16)
    left, right = pl.pallas_call(
        pack_sub,
        in_specs=[smem] * 3 + [vmem] * 4,
        out_specs=[vmem] * 2,
        out_shape=[msg, msg],
        name="pack_sub",
        compiler_params=pltpu.CompilerParams(vmem_limit_bytes=16 << 20),
    )(corner_rows, corner_cols, live_counts, blend_weight, edge, above, below)
    from_left = shifted(right, "sub", 1)
    from_right = shifted(left, "sub", -1)
    out = jax.ShapeDtypeStruct((OUT, BY, BX), F32)
    return tuple(pl.pallas_call(
        main_kernel,
        in_specs=[smem] * 3 + [vmem] * 10,
        out_specs=[pl.BlockSpec(memory_space=pl.ANY)] * 2,
        out_shape=[out, out],
        scratch_shapes=[
            pltpu.VMEM((5, X_ROWS * CH, LANES), BF16),
            pltpu.VMEM((2, (STEP + 4) * 3 * CH, WIDE), BF16),
            pltpu.VMEM((2, (STEP + 2) * 3 * HID, WIDE), BF16),
            pltpu.VMEM((2, (STEP + 2) * HID, WIDE), F32),
            pltpu.VMEM((2, STEP * HID, WIDE), BF16),
            pltpu.VMEM((3, ACC_ROWS * 8, LANES), F32),
            pltpu.VMEM((PIECES, SIDE, LANES), F32),
            pltpu.VMEM((80, LANES), jnp.int32),
            pltpu.SMEM((80, LANES), jnp.int32),
            pltpu.SMEM((4, UNITS), jnp.int32),
            pltpu.SMEM((11, PIECES), jnp.int32),
            pltpu.SMEM((5, LANES), jnp.int32),
            pltpu.VMEM((OUT, BY, BX), F32),
            pltpu.VMEM((OUT, BY, BX), F32),
            pltpu.SemaphoreType.DMA,
            pltpu.SemaphoreType.DMA,
            pltpu.SemaphoreType.DMA((2,)),
        ],
        name="patches",
        compiler_params=pltpu.CompilerParams(vmem_limit_bytes=26 << 20),
    )(corner_rows, corner_cols, live_counts, body, state, blend_weight, above, below, from_left, from_right, w1, w2, w3))


def solution(mesh):
    placed = (
        P(None, "tile", "sub"),
        P(None, "tile", "sub"),
        P("tile", "sub", None),
        P("tile", "sub", None),
        P("tile", "sub"),
        P("tile", "sub", None, None, None),
        P(),
        P(),
        P(),
    )
    return jax.shard_map(
        per_device,
        mesh=mesh,
        in_specs=placed,
        out_specs=(P(None, "tile", "sub"), P(None, "tile", "sub")),
        check_vma=False,
    )
```

```python
import jax
import jax.numpy as jnp
from jax import lax
from jax.experimental import pallas as pl
from jax.experimental.pallas import tpu as pltpu
from jax.sharding import PartitionSpec as P

SIGMA = 2.0
SIGMA_NEXT = 1.6
C_IN = 1.0 / (SIGMA * SIGMA + 0.25) ** 0.5
C_SKIP = 0.25 / (SIGMA * SIGMA + 0.25)
C_OUT = 0.5 * SIGMA / (SIGMA * SIGMA + 0.25) ** 0.5

BY = 256
BX = 256
SIDE = 128
HALF = 64
CC = 12
CH = 16
HID = 64
OUT = 4
SLOTS = 2
LANES = 128
WIDE = 2 * LANES
STEP = 8
X_TOP = 10
X_ROWS = BY + 24
ACC_ROWS = BY + 2 * STEP
LAG = 3
UNITS = 768
PIECES = 9 * SLOTS
TILE_MSG = 2 * HALF + 4 * CH + 16
SUB_MSG = SIDE + 2 * HALF + 4 * CH + 64 + 16
F32 = jnp.float32
BF16 = jnp.bfloat16


def iota(shape, dim):
    return lax.broadcasted_iota(jnp.int32, shape, dim)


def scaled(state):
    return (state * C_IN).astype(BF16)


def own_meta(rows_ref, cols_ref, live_ref):
    sub = iota((16, LANES), 0)
    values = (rows_ref[0, 0, 0], rows_ref[0, 0, 1], cols_ref[0, 0, 0], cols_ref[0, 0, 1], live_ref[0, 0])
    tile = jnp.zeros((16, LANES), jnp.int32)
    for k, value in enumerate(values):
        tile = jnp.where(sub == k, value, tile)
    return tile


def pack_tile(rows_ref, cols_ref, live_ref, c_top, c_bot, s_top, s_bot, weight_ref, up_ref, down_ref, tmp):
    meta = own_meta(rows_ref, cols_ref, live_ref).astype(F32).astype(BF16)
    for out, cond, state, low, first_c, first_s in (
        (up_ref, c_top, s_top, 0, 0, 0),
        (down_ref, c_bot, s_bot, HALF, 14, 6),
    ):
        for p in range(SLOTS):
            out[p * HALF : (p + 1) * HALF, :] = weight_ref[0, 0, p, low : low + HALF, :].astype(BF16)
        for c in range(CH):
            if c < CC:
                tile = cond[c].astype(F32)[first_c : first_c + 2, :]
            else:
                tile = scaled(state[c - CC]).astype(F32)[first_s : first_s + 2, :]
            for t in range(2):
                for r in range(2):
                    at = t * 2 * CH + r * CH + c
                    tmp[at : at + 1, :] = tile[r : r + 1, t * LANES : (t + 1) * LANES]
        out[2 * HALF : 2 * HALF + 4 * CH, :] = tmp[...].astype(BF16)
        out[2 * HALF + 4 * CH :, :] = meta


def prepare(cond_ref, state_ref, body_ref, edge_ref):
    to = iota((CH * CH, CH * CH), 0)
    of = iota((CH * CH, CH * CH), 1)
    turn = (of == (to % CH) * CH + to // CH).astype(F32).astype(BF16)
    picks = iota((16, LANES), 0)
    spots = iota((16, LANES), 1)
    first = ((picks == spots) & (picks < 2)).astype(F32).astype(BF16)
    last = ((picks == spots - (LANES - 4)) & (picks >= 2)).astype(F32).astype(BF16)

    def group(i, carry):
        for e in range(4):
            start = pl.multiple_of((4 * i + e) * CH, CH)
            rows = pl.ds(start, CH)
            value = jnp.concatenate(
                [cond_ref[:, rows, :].reshape(CC * CH, BX), scaled(state_ref[:, rows, :]).reshape(OUT * CH, BX)], axis=0
            )
            value = jnp.dot(turn, value, preferred_element_type=F32).astype(BF16)
            at = pl.ds(start * CH, CH * CH)
            edge = jnp.zeros((16, CH * CH), F32)
            for t, pick in enumerate((first, last)):
                part = value[:, t * LANES : (t + 1) * LANES]
                body_ref[t, at, :] = part
                edge = edge + lax.dot_general(pick, part, (((1,), (1,)), ((), ())), preferred_element_type=F32)
            edge_ref[:, at] = edge.astype(BF16)
        return carry

    lax.fori_loop(0, BY // CH // 4, group, 0)


def pack_sub(rows_ref, cols_ref, live_ref, weight_ref, edge_ref, above_ref, below_ref, left_ref, right_ref):
    lane = iota((1, LANES), 1)
    meta0 = own_meta(rows_ref, cols_ref, live_ref).astype(F32)
    sub = iota((16, LANES), 0)
    first = 2 * HALF + 4 * CH
    meta_a = pltpu.roll(above_ref[first:, :].astype(F32), 5, 0)
    meta_b = pltpu.roll(below_ref[first:, :].astype(F32), 10, 0)
    meta = jnp.where(sub < 5, meta0, jnp.where(sub < 10, meta_a, meta_b)).astype(BF16)
    for out, side in ((left_ref, 0), (right_ref, 1)):
        def packed(one, two):
            if side == 0:
                return jnp.where(lane < HALF, one, pltpu.roll(two, HALF, 1)).astype(BF16)
            return jnp.where(lane < HALF, pltpu.roll(one, HALF, 1), two).astype(BF16)

        out[0:SIDE, :] = packed(weight_ref[0, 0, 0], weight_ref[0, 0, 1])
        at = SIDE
        for msg in (above_ref, below_ref):
            out[at : at + HALF, :] = packed(msg[0:HALF, :].astype(F32), msg[HALF : 2 * HALF, :].astype(F32))
            at += HALF
        for msg in (above_ref, below_ref):
            begin = 2 * HALF + side * 2 * CH
            out[at : at + 2 * CH, :] = msg[begin : begin + 2 * CH, :]
            at += 2 * CH
        edge = edge_ref[...].astype(F32)
        for m in range(4):
            rows = []
            for e in range(8):
                spot = (8 * m + e) * LANES
                rows.append(edge[2 * side : 2 * side + 2, spot : spot + LANES])
            out[at : at + 16, :] = jnp.concatenate(rows, axis=0).astype(BF16)
            at += 16
        out[at:, :] = meta


def main_kernel(
    rows_ref, cols_ref, live_ref, body_ref, state_ref, weight_ref,
    above_ref, below_ref, left_ref, right_ref, w1_ref, w2_ref, w3_ref,
    den_out, next_out,
    xb_ref, p_ref, a_ref, u_ref, q_ref, acc_ref, wall_ref, meta_v, meta_s, unit_ref, place_ref, list_ref, den_ref, next_ref, sem, body_sem, out_sems,
):
    lane = iota((1, LANES), 1)
    first = 2 * HALF + 4 * CH
    meta_v[0:16, :] = own_meta(rows_ref, cols_ref, live_ref)
    meta_v[16:32, :] = above_ref[first:, :].astype(F32).astype(jnp.int32)
    meta_v[32:48, :] = below_ref[first:, :].astype(F32).astype(jnp.int32)
    meta_v[48:64, :] = left_ref[SUB_MSG - 16 :, :].astype(F32).astype(jnp.int32)
    meta_v[64:80, :] = right_ref[SUB_MSG - 16 :, :].astype(F32).astype(jnp.int32)
    copy = pltpu.make_async_copy(meta_v, meta_s, sem)
    copy.start()

    body = pltpu.make_async_copy(body_ref, xb_ref.at[1:3, X_TOP * CH : (BY + X_TOP) * CH, :], body_sem)
    body.start()
    corner = SIDE + 2 * HALF
    for msg, row, spot in ((above_ref, X_TOP - 2, 0), (below_ref, BY + X_TOP, 2 * CH)):
        for t in range(2):
            xb_ref[t + 1, row * CH : (row + 2) * CH, :] = msg[2 * HALF + t * 2 * CH : 2 * HALF + (t + 1) * 2 * CH, :]
        from_left = left_ref[corner + spot : corner + spot + 2 * CH, :].astype(F32)
        from_right = right_ref[corner + spot : corner + spot + 2 * CH, :].astype(F32)
        xb_ref[0, row * CH : (row + 2) * CH, :] = jnp.where(
            lane < 2, from_right, jnp.where(lane >= LANES - 2, from_left, 0.0)
        ).astype(BF16)
    edge_at = corner + 4 * CH
    picks = iota((32, LANES), 0)
    spots = iota((32, LANES), 1)
    for m in range(4):
        rows = slice(edge_at + 16 * m, edge_at + 16 * m + 16)
        both = jnp.concatenate([left_ref[rows, :].astype(F32), right_ref[rows, :].astype(F32)], axis=0)
        turned = both.T.astype(BF16)
        for e in range(8):
            to_left = (picks - 2 * e == spots - (LANES - 2)) & (spots >= LANES - 2) & (picks < 16)
            to_right = (picks - 16 - 2 * e == spots) & (spots < 2) & (picks >= 16)
            place = (to_left | to_right).astype(F32).astype(BF16)
            at = X_TOP * CH + (8 * m + e) * LANES
            xb_ref[0, at : at + LANES, :] = jnp.dot(turned, place, preferred_element_type=F32).astype(BF16)
    for t in range(3):
        xb_ref[t, 0 : (X_TOP - 2) * CH, :] = jnp.zeros(((X_TOP - 2) * CH, LANES), BF16)
        low = (BY + X_TOP + 2) * CH
        xb_ref[t, low:, :] = jnp.zeros((X_ROWS * CH - low, LANES), BF16)
    p_ref[...] = jnp.zeros_like(p_ref)
    a_ref[...] = jnp.zeros_like(a_ref)

    for p in range(SLOTS):
        wall_ref[p, 0:SIDE, :] = weight_ref[0, 0, p]
        wall_ref[2 + p, HALF:SIDE, :] = above_ref[p * HALF : (p + 1) * HALF, :].astype(F32)
        wall_ref[4 + p, 0:HALF, :] = below_ref[p * HALF : (p + 1) * HALF, :].astype(F32)
        for d, msg in ((3, left_ref), (6, right_ref)):
            def side(lo, hi):
                part = msg[lo:hi, :].astype(F32)
                return jnp.where((lane < HALF) == (p == 0), part, pltpu.roll(part, HALF, 1))

            wall_ref[2 * d + p, 0:SIDE, :] = side(0, SIDE)
            wall_ref[2 * d + 2 + p, HALF:SIDE, :] = side(SIDE, SIDE + HALF)
            wall_ref[2 * d + 4 + p, 0:HALF, :] = side(SIDE + HALF, SIDE + 2 * HALF)

    def clear(i, carry):
        for t in range(1, 3):
            acc_ref[t, pl.ds(pl.multiple_of(i * 256 + STEP * 8, 64), 256), :] = jnp.zeros((256, LANES), F32)
        return carry

    lax.fori_loop(0, BY * 8 // 256, clear, 0)
    copy.wait()

    one_row = (iota((8, 1), 0) == OUT).astype(F32)

    def nothing(i):
        unit_ref[0, i] = 0
        unit_ref[1, i] = 0
        unit_ref[2, i] = BY
        unit_ref[3, i] = 0

    for i in range(4 * LAG):
        nothing(i)

    pos = jnp.int32(0)
    totals = []
    pieces = []
    for k in range(PIECES):
        d, p = k // 2, k % 2
        across, along = d // 3, d % 3
        base = 16 * along if across == 0 else 32 + 16 * across + 5 * along
        row0 = meta_s[base + p, 0] + (0, -BY, BY)[along] - HALF
        col0 = meta_s[base + 2 + p, 0] + (0, -BX, BX)[across] - HALF
        low = jnp.maximum(-row0, 0) // STEP
        high = (jnp.minimum(SIDE, BY - row0) + STEP - 1) // STEP
        touches = (low < high) & (col0 > -SIDE) & (col0 < BX) & (p < meta_s[base + 4, 0])
        spot = col0 + LANES
        q, rem = spot // LANES, spot % LANES
        after_q = jnp.where(q == 2, 0, q + 1)
        whole = ((q, rem, q, rem, LANES), (after_q, rem, after_q, 0, rem))
        bound = LANES - rem
        if across == 0:
            narrow = jnp.bool_(False)
        else:
            if across == 1:
                narrow = spot <= HALF - 2
                ours = [(3, (spot + HALF * (1 - g)) % LANES, 1, 0, spot) for g in range(2)]
            else:
                narrow = col0 >= BX - (HALF - 2)
                ours = [(4, (spot + HALF * g) % LANES, 2, col0 - LANES, LANES) for g in range(2)]
            whole = [[jnp.where(narrow, x, y) for x, y in zip(mine, all_)] for mine, all_ in zip(ours, whole)]
            bound = jnp.where(narrow, HALF, bound)
        for g in range(2):
            for f in range(5):
                place_ref[5 * g + f, k] = whole[g][f]
        place_ref[10, k] = bound
        pieces.append((k, low, high, row0, touches, narrow))
    for half in range(2):
        total = jnp.int32(0)
        for k, low, high, row0, touches, narrow in pieces:
            if half == 1 and k < 6:
                continue
            ours = touches & (narrow if half == 1 else jnp.logical_not(narrow))
            list_ref[0, pos] = k
            list_ref[1, pos] = low
            list_ref[2, pos] = high
            list_ref[3, pos] = row0
            list_ref[4, pos] = half
            pos = pos + ours.astype(jnp.int32)
            total = total + jnp.where(ours, high - low, 0)
        totals.append(total)
    for i in range(8 * LAG + 16):
        list_ref[0, pos + i] = 0
        list_ref[1, pos + i] = 0
        list_ref[2, pos + i] = 1
        list_ref[3, pos + i] = BY
        list_ref[4, pos + i] = 1
    count = totals[0] + (totals[1] + 1) // 2 + 2 * LAG
    body.wait()

    def edges(i, carry):
        at = pl.ds(pl.multiple_of(i * (X_ROWS * CH // 5), CH), X_ROWS * CH // 5)
        outer = xb_ref[0, at, :]
        xb_ref[3, at, :] = jnp.where(lane < HALF, xb_ref[1, at, :], outer)
        xb_ref[4, at, :] = jnp.where(lane < HALF, outer, xb_ref[2, at, :])
        return carry

    lax.fori_loop(0, 5, edges, 0)

    def advance(unit, g, at, i):
        half = list_ref[4, at]
        unit_ref[0, unit] = list_ref[0, at]
        unit_ref[1, unit] = i * STEP
        unit_ref[2, unit] = list_ref[3, at] + i * STEP
        unit_ref[3, unit] = half
        ahead = i + (half if g == 0 else 1)
        done = ahead >= list_ref[2, at]
        at = at + done.astype(jnp.int32)
        return at, jnp.where(done, list_ref[1, at], ahead)

    first_half = lane < HALF

    def by_half(values):
        return jnp.where(first_half, values[0].astype(F32), values[1].astype(F32))

    def borders(split):
        lo = jnp.where((lane == 0) | ((lane == HALF) & (split > 0)), 0.0, 1.0)
        hi = jnp.where((lane == LANES - 1) | ((lane == HALF - 1) & (split > 0)), 0.0, 1.0)
        return [jnp.broadcast_to(part, (CH, LANES)).astype(BF16) for part in (lo, hi)]

    def keep(ref, z, row, h, part, mask):
        for m in range(part.shape[0] // CH):
            ref[z, row + m * CH : row + (m + 1) * CH, h * LANES : (h + 1) * LANES] = jnp.where(mask > 0, part[m * CH : (m + 1) * CH], jnp.zeros((), BF16))

    def blend(i, z):
        nets = [
            jnp.dot(w3_ref[...], q_ref[z, 4 * e * HID : 4 * (e + 1) * HID, :], preferred_element_type=F32)
            for e in range(STEP // 4)
        ]
        for h in range(2):
            units = [4 * i + 2 * h + g for g in range(2)]
            ks = [unit_ref[0, unit] for unit in units]
            locals_ = [unit_ref[1, unit] for unit in units]
            parts = []
            for f in range(STEP):
                y = nets[f // 4][8 * (f % 4) : 8 * (f % 4) + 8, h * LANES : (h + 1) * LANES]
                one, two = [wall_ref[k, pl.ds(local + f, 1), :] for k, local in zip(ks, locals_)]
                parts.append((y + one_row) * jnp.where(first_half, one, two))
            value = jnp.concatenate(parts, axis=0)
            for g in range(2):
                turn, tile, lo, hi = [place_ref[5 * g + f, ks[g]] for f in range(1, 5)]
                y = pltpu.roll(value, turn, 1)
                at = pl.ds(pl.multiple_of((unit_ref[2, units[g]] + STEP) * 8, 8), 8 * STEP)
                acc_ref[tile, at, :] += jnp.where((lane >= lo) & (lane < hi), y, 0.0)

    def second_conv(z, y):
        for e in range(STEP // 2):
            v = jnp.dot(w2_ref[...], a_ref[z, 2 * e * 3 * HID : (2 * e + 4) * 3 * HID, :], preferred_element_type=F32)
            v = v + u_ref[z, (2 * e + 1) * HID : (2 * e + 3) * HID, :]
            q_ref[y, 2 * e * HID : (2 * e + 2) * HID, :] = (v + v * jnp.tanh(v)).astype(BF16)

    def first_conv(i, z):
        for e in range(STEP // 2 + 1):
            u = jnp.dot(w1_ref[...], p_ref[z, 2 * e * 3 * CH : (2 * e + 4) * 3 * CH, :], preferred_element_type=F32)
            u_ref[z, 2 * e * HID : (2 * e + 2) * HID, :] = u
            act = u + u * jnp.tanh(u)
            for h in range(2):
                units = [4 * i + 2 * h + g for g in range(2)]
                locals_ = [unit_ref[1, unit] for unit in units]
                inner_lo, inner_hi = borders(unit_ref[3, units[0]])
                for r in range(2):
                    mid = act[r * HID : (r + 1) * HID, h * LANES : (h + 1) * LANES]
                    row = 2 * e + r
                    if row == 0:
                        mid = mid * by_half([local > 0 for local in locals_])
                    if row == STEP + 1:
                        mid = mid * by_half([local < SIDE - STEP for local in locals_])
                    mid = mid.astype(BF16)
                    at = row * 3 * HID
                    keep(a_ref, z, at, h, pltpu.roll(mid, 1, 1), inner_lo)
                    a_ref[z, at + HID : at + 2 * HID, h * LANES : (h + 1) * LANES] = mid
                    keep(a_ref, z, at + 2 * HID, h, pltpu.roll(mid, LANES - 1, 1), inner_hi)

    def stage(i, z):
        for h in range(2):
            units = [4 * i + 2 * h + g for g in range(2)]
            locals_ = [unit_ref[1, unit] for unit in units]
            inner_lo, inner_hi = borders(unit_ref[3, units[0]])
            ks = [unit_ref[0, unit] for unit in units]
            tiles = [place_ref[5 * g, ks[g]] for g in range(2)]
            turns = [(LANES - place_ref[5 * g + 1, ks[g]]) % LANES for g in range(2)]
            rows = [unit_ref[2, unit] for unit in units]
            low_part = lane < place_ref[10, ks[0]]
            both = []
            for tile, turn, row in zip(tiles, turns, rows):
                at = pl.ds(pl.multiple_of((row + X_TOP - 2) * CH, CH), (STEP + 4) * CH)
                both.append(pltpu.roll(xb_ref[tile, at, :], turn, 1))
            value = jnp.where(low_part, both[0], both[1])
            for j in range(STEP + 4):
                mid = value[j * CH : (j + 1) * CH]
                if j < 2:
                    mid = mid * by_half([local > 0 for local in locals_]).astype(BF16)
                if j >= STEP + 2:
                    mid = mid * by_half([local < SIDE - STEP for local in locals_]).astype(BF16)
                keep(p_ref, z, j * 3 * CH, h, pltpu.roll(mid, 1, 1), inner_lo)
                p_ref[z, j * 3 * CH + CH : j * 3 * CH + 2 * CH, h * LANES : (h + 1) * LANES] = mid
                keep(p_ref, z, j * 3 * CH + 2 * CH, h, pltpu.roll(mid, LANES - 1, 1), inner_hi)

    def step(i, carry):
        at, row = carry
        for z in range(2):
            first_conv(2 * i + z + 2, z)
            blend(2 * i + z, 1 - z)
            second_conv(1 - z, z)
            stage(2 * i + z + 3, 1 - z)
        return more(i + 1, at, row)

    def more(i, at, row):
        for h in range(8):
            at, row = advance(8 * i + 4 * LAG + h, h % 2, at, row)
        return at, row

    lax.fori_loop(0, (count + 3) // 4, step, more(0, jnp.int32(0), list_ref[1, 0]))

    def finish(i, carry):
        for t, part in ((t, part) for part in range(4) for t in range(2)):
            row = pl.multiple_of(i * 32 + part * 8, 8)
            lanes = slice(t * LANES, (t + 1) * LANES)
            total = acc_ref[t + 1, pl.ds((row + STEP) * 8 + OUT, 8, stride=8), :]
            over = 1.0 / (1.0 + total)
            for o in range(OUT):
                state = state_ref[o, pl.ds(row, 8), lanes]
                numer = acc_ref[t + 1, pl.ds((row + STEP) * 8 + o, 8, stride=8), :]
                den = (state * (1.0 + C_SKIP * total) + C_OUT * numer) * over
                den_ref[o, pl.ds(row, 8), lanes] = den
                next_ref[o, pl.ds(row, 8), lanes] = state + (SIGMA_NEXT - SIGMA) * (state - den) / SIGMA
        rows = pl.ds(pl.multiple_of(i * 32, 32), 32)
        for held, out, at in ((den_ref, den_out, 0), (next_ref, next_out, 1)):
            pltpu.make_async_copy(held.at[:, rows, :], out.at[:, rows, :], out_sems.at[at]).start()
        return carry

    lax.fori_loop(0, BY // 32, finish, 0)
    for held, out, at in ((den_ref, den_out, 0), (next_ref, next_out, 1)):
        pltpu.make_async_copy(held, out, out_sems.at[at]).wait()


def banded(kernel, times):
    outs, chans = kernel.shape[2], kernel.shape[3]
    flat = (0.5 * jnp.transpose(kernel, (2, 0, 1, 3))).astype(BF16).reshape(outs, 9 * chans)
    step = 3 * chans
    return jnp.concatenate([jnp.pad(flat, ((0, 0), (r * step, (times - 1 - r) * step))) for r in range(times)], axis=0)


def shifted(value, axis, steps):
    count = lax.axis_size(axis)
    first, last = max(0, -steps), min(count, count - steps)
    return lax.ppermute(value, axis, [(i, i + steps) for i in range(first, last)])


def per_device(condition, state, corner_rows, corner_cols, live_counts, blend_weight, conv_in, conv_mid, proj_out):
    smem = pl.BlockSpec(memory_space=pltpu.SMEM)
    vmem = pl.BlockSpec(memory_space=pltpu.VMEM)
    whole_w = pl.BlockSpec((1, 1, SLOTS, SIDE, SIDE), lambda i: (0, 0, 0, 0, 0))
    msg = jax.ShapeDtypeStruct((TILE_MSG, LANES), BF16)
    up, down = pl.pallas_call(
        pack_tile,
        grid=(1,),
        in_specs=[
            smem, smem, smem,
            pl.BlockSpec((CC, 16, BX), lambda i: (0, 0, 0)),
            pl.BlockSpec((CC, 16, BX), lambda i: (0, BY // 16 - 1, 0)),
            pl.BlockSpec((OUT, 8, BX), lambda i: (0, 0, 0)),
            pl.BlockSpec((OUT, 8, BX), lambda i: (0, BY // 8 - 1, 0)),
            whole_w,
        ],
        out_specs=[pl.BlockSpec((TILE_MSG, LANES), lambda i: (0, 0))] * 2,
        out_shape=[msg, msg],
        scratch_shapes=[pltpu.VMEM((4 * CH, LANES), F32)],
        name="pack_tile",
    )(corner_rows, corner_cols, live_counts, condition, condition, state, state, blend_weight)
    above = shifted(down, "tile", 1)
    below = shifted(up, "tile", -1)
    w1 = banded(conv_in, 2)
    w2 = banded(conv_mid, 2)
    rows8 = jnp.pad(proj_out, ((0, 8 - OUT), (0, 0)))
    w3 = jnp.concatenate([jnp.pad(rows8, ((0, 0), (r * HID, (3 - r) * HID))) for r in range(4)], axis=0)
    body, edge = pl.pallas_call(
        prepare,
        in_specs=[vmem] * 2,
        out_specs=[vmem] * 2,
        out_shape=[jax.ShapeDtypeStruct((2, BY * CH, LANES), BF16), jax.ShapeDtypeStruct((16, BY * CH), BF16)],
        name="prepare",
        compiler_params=pltpu.CompilerParams(vmem_limit_bytes=16 << 20),
        cost_estimate=pl.CostEstimate(flops=2 * 4096 * 256 * 256, bytes_accessed=5 << 20, transcendentals=0),
    )(condition, state)
    msg = jax.ShapeDtypeStruct((SUB_MSG, LANES), BF16)
    left, right = pl.pallas_call(
        pack_sub,
        in_specs=[smem] * 3 + [vmem] * 4,
        out_specs=[vmem] * 2,
        out_shape=[msg, msg],
        name="pack_sub",
        compiler_params=pltpu.CompilerParams(vmem_limit_bytes=16 << 20),
    )(corner_rows, corner_cols, live_counts, blend_weight, edge, above, below)
    from_left = shifted(right, "sub", 1)
    from_right = shifted(left, "sub", -1)
    out = jax.ShapeDtypeStruct((OUT, BY, BX), F32)
    return tuple(pl.pallas_call(
        main_kernel,
        in_specs=[smem] * 3 + [vmem] * 10,
        out_specs=[pl.BlockSpec(memory_space=pl.ANY)] * 2,
        out_shape=[out, out],
        scratch_shapes=[
            pltpu.VMEM((5, X_ROWS * CH, LANES), BF16),
            pltpu.VMEM((2, (STEP + 4) * 3 * CH, WIDE), BF16),
            pltpu.VMEM((2, (STEP + 2) * 3 * HID, WIDE), BF16),
            pltpu.VMEM((2, (STEP + 2) * HID, WIDE), F32),
            pltpu.VMEM((2, STEP * HID, WIDE), BF16),
            pltpu.VMEM((3, ACC_ROWS * 8, LANES), F32),
            pltpu.VMEM((PIECES, SIDE, LANES), F32),
            pltpu.VMEM((80, LANES), jnp.int32),
            pltpu.SMEM((80, LANES), jnp.int32),
            pltpu.SMEM((4, UNITS), jnp.int32),
            pltpu.SMEM((11, PIECES), jnp.int32),
            pltpu.SMEM((5, LANES), jnp.int32),
            pltpu.VMEM((OUT, BY, BX), F32),
            pltpu.VMEM((OUT, BY, BX), F32),
            pltpu.SemaphoreType.DMA,
            pltpu.SemaphoreType.DMA,
            pltpu.SemaphoreType.DMA((2,)),
        ],
        name="patches",
        compiler_params=pltpu.CompilerParams(vmem_limit_bytes=26 << 20),
    )(corner_rows, corner_cols, live_counts, body, state, blend_weight, above, below, from_left, from_right, w1, w2, w3))


def solution(mesh):
    placed = (
        P(None, "tile", "sub"),
        P(None, "tile", "sub"),
        P("tile", "sub", None),
        P("tile", "sub", None),
        P("tile", "sub"),
        P("tile", "sub", None, None, None),
        P(),
        P(),
        P(),
    )
    return jax.shard_map(
        per_device,
        mesh=mesh,
        in_specs=placed,
        out_specs=(P(None, "tile", "sub"), P(None, "tile", "sub")),
        check_vma=False,
    )
```
